32 devices in a mesh: dp: 8 (over z, x), expert: 4 (over y, core).
Axes of the slice: x: 2, y: 2, z: 4, core: 2. Of those that a mesh axis runs over, the one named last changes fastest.
Arguments:
- tokens: bfloat16 [16384, 768], P(('dp', 'expert')), may hold values from -6 to 6
- segments: int32 [32, 512], P(('dp', 'expert')), may hold values from 0 to 2, never falling along the last dimension, each value on 1 to 256 neighbouring positions
- routes: int32 [16384, 2], P(('dp', 'expert')), may hold values from 0 to 7, as said below
- prev_logits: float32 [16384, 8], P(('dp', 'expert')), may hold values from -3 to 3
- ln1_gain: float32 [768], replicated, may hold values from 0.25 to 1.75
- w_qkv: bfloat16 [768, 2304], replicated, may hold values from -0.21875 to 0.21875
- w_attn: bfloat16 [768, 768], replicated, may hold values from -0.875 to 0.875
- ln2_gain: float32 [768], replicated, may hold values from 0.25 to 1.75
- w_router: float32 [768, 8], replicated, may hold values from -0.109375 to 0.109375
- const_mix: float32 [768, 4], replicated, may hold values from -0.21875 to 0.21875
- const_vec: float32 [768, 2], replicated, may hold values from -6 to 6
- expert_in: bfloat16 [4, 768, 4096], P('expert'), may hold values from -0.21875 to 0.21875
- expert_out: bfloat16 [4, 2048, 768], P('expert'), may hold values from -0.1875 to 0.1875
- cotangent: bfloat16 [16384, 768], P(('dp', 'expert')), may hold values from -6 to 6
Outputs:
- output: bfloat16 [16384, 768], P(('dp', 'expert'))
- input_grad: bfloat16 [16384, 768], P(('dp', 'expert'))
- ln1_grad: float32 [768], P(('dp', 'expert'))
- qkv_grad: float32 [768, 2304], P(('dp', 'expert'))
- attn_grad: float32 [768, 768], P(('dp', 'expert'))
- ln2_grad: float32 [768], P(('dp', 'expert'))
- router_grad: float32 [768, 8], P(('dp', 'expert'))
- mix_grad: float32 [768, 4], P(('dp', 'expert'))
- vec_grad: float32 [768, 2], P(('dp', 'expert'))
- expert_in_grad: float32 [4, 768, 4096], P('expert', 'dp')
- expert_out_grad: float32 [4, 2048, 768], P('expert', 'dp')
The draws below stay inside these ranges and needn't reach their ends.
Inputs may be any that keep to these rules, and one draw needn't show every extreme that they name: `routes`: the two experts of a token differ; the first 4 numbers are feed-forward experts. In each aligned block of 512 rows no expert is named more than 256 times, and in each aligned run of 4 such blocks one feed-forward expert is named exactly 256 times in every block. `segments`: segment numbers never fall along a row; a document spans 1 to 256 places, and in each row exactly one document spans 256 places.
All inputs are finite; a program needn't handle non-finite values.
Results may differ from the reference program's by a relative error of at most 0.015.
Values may be sent and summed in bfloat16 or wider, within the bound.
A program may use at most 192 MiB of HBM per device.

```python
import math
import jax
import jax.numpy as jnp
import numpy as np
from jax import lax

D = 768
HEAD_DIM = 64
FF = 2048
TOK_DEV = 512
EXPERTS = 4
NE = 8
CAP = 256
SEQS = 32
TOKENS = 16384
N_EXPERT = 4


def shuffle_block(block_key):
    return jax.random.permutation(block_key, TOK_DEV)


def draw_routes(key, part):
    key = jax.random.fold_in(key, 7)
    block_total = TOKENS // TOK_DEV
    group_total = block_total // N_EXPERT
    key_full, key_weight, key_order, key_swap = jax.random.split(key, 4)
    full_expert = jax.random.randint(key_full, (group_total,), 0, EXPERTS)
    full_block = jnp.repeat(full_expert, N_EXPERT)
    expert_ids = jnp.arange(NE)
    is_full = expert_ids[None, :] == full_block[:, None]
    draw_weight = jax.random.randint(key_weight, (block_total, NE), 1, 17)
    draw_weight = jnp.where(is_full, 0, draw_weight * draw_weight)
    remaining = 2 * TOK_DEV - CAP
    raw_counts = remaining * draw_weight // jnp.sum(draw_weight, axis=1, keepdims=True)
    capped = jnp.minimum(raw_counts, CAP)
    deficit = remaining - jnp.sum(capped, axis=1, keepdims=True)
    room = jnp.where(is_full, 0, CAP - capped)
    room_before = jnp.cumsum(room, axis=1) - room
    extra = jnp.clip(deficit - room_before, 0, room)
    counts = jnp.where(is_full, CAP, capped + extra)
    ends = jnp.cumsum(counts, axis=1)
    places = jnp.arange(2 * TOK_DEV)
    labels = jnp.sum((places[None, :, None] >= ends[:, None, :]).astype(jnp.int32), axis=2)
    paired = jnp.stack([labels[:, :TOK_DEV], labels[:, TOK_DEV:]], axis=-1)
    orders = jax.vmap(shuffle_block)(jax.random.split(key_order, block_total))
    paired = jnp.take_along_axis(paired, orders[:, :, None], axis=1)
    swapped = jax.random.randint(key_swap, (block_total, TOK_DEV, 1), 0, 2)
    paired = jnp.where(swapped == 1, paired[..., ::-1], paired)
    return paired.reshape(TOKENS, 2).astype(jnp.int32)


def level_of(stream_key, extent, pieces, low, largest):
    def one(position, parts):
        steps = jax.random.uniform(jax.random.fold_in(jax.random.fold_in(stream_key, 6), position), (parts,), jnp.float32, low / len(pieces), largest / len(pieces))
        return jnp.repeat(jnp.exp(steps), extent[position] // parts).reshape((-1,) + (1,) * (len(extent) - position - 1))

    gain = one(*pieces[0])
    for cut in pieces[1:]:
        gain = gain * one(*cut)
    return gain


def profile(count, total, limit, skew):
    loads = [(1 << 20) // math.isqrt(grade ** skew) + 1 for grade in range(2, count + 1)]
    rest, given = total - limit - (count - 1), [1] * (count - 1)
    while rest > 0:
        free = [i for i in range(count - 1) if given[i] < limit]
        pool, left = sum([loads[i] for i in free]), rest
        for i in free:
            more = min(limit - given[i], max(1, left * loads[i] // pool), rest)
            given[i] = given[i] + more
            rest = rest - more
    return np.array([limit] + given)


def ragged_sizes(stream_key, number_of, total, bound, slope):
    if number_of == 2:
        one = jax.random.randint(stream_key, (), max(1, total - bound), min(bound, total - 1) + 1)
        return jnp.stack([one, total - one])
    sizes = jnp.asarray(profile(number_of, total, bound, slope), jnp.int32)
    couples = (number_of - 1) // 2
    giver, sink = sizes[1:1 + 2 * couples:2], sizes[2:2 + 2 * couples:2]
    room = jnp.minimum(giver - 1, bound - sink)
    shifted = jax.random.randint(jax.random.fold_in(stream_key, 1), (couples,), 0, 1 << 20) % (room + 1)
    sizes = sizes.at[1:1 + 2 * couples:2].set(giver - shifted).at[2:2 + 2 * couples:2].set(sink + shifted)
    return sizes[jax.random.permutation(jax.random.fold_in(stream_key, 2), number_of)]


def noise(rng, extent, width, reach, cuts=(), kind=jnp.bfloat16):
    drawn = width * jax.random.normal(rng, extent, jnp.float32)
    if cuts:
        drawn = drawn * level_of(rng, extent, cuts, -0.22, 0.18)
    return jnp.clip(drawn, -reach, reach).astype(kind)


def setup_inputs(seed: int = 0) -> dict:
    keys = jax.random.split(jax.random.key(seed), 15)
    return {
        "tokens": noise(keys[0], (TOKENS, D), 1.0, 6.0, ((0, 32),)),
        "segments": jax.vmap(lambda own: jnp.searchsorted(jnp.cumsum(ragged_sizes(own, 3, TOK_DEV, TOK_DEV // 2, 0)), jnp.arange(TOK_DEV), side="right"))(jax.random.split(keys[1], SEQS)).reshape((SEQS, TOK_DEV)).astype(jnp.int32),
        "routes": draw_routes(jax.random.fold_in(keys[14], 71), 0),
        "prev_logits": noise(keys[3], (TOKENS, NE), 0.5, 3.0, ((0, 32),), jnp.float32),
        "ln1_gain": jnp.clip(1.0 + 0.15 * jax.random.normal(keys[4], (D,), jnp.float32), 0.25, 1.75),
        "w_qkv": noise(keys[5], (D, 3 * D), D ** -0.5, 0.21875),
        "w_attn": noise(keys[6], (D, D), (D // 16) ** -0.5, 0.875),
        "ln2_gain": jnp.clip(1.0 + 0.15 * jax.random.normal(keys[7], (D,), jnp.float32), 0.25, 1.75),
        "w_router": noise(keys[8], (D, NE), (4 * D) ** -0.5, 0.109375, (), jnp.float32),
        "const_mix": noise(keys[9], (D, 4), D ** -0.5, 0.21875, (), jnp.float32),
        "const_vec": noise(keys[10], (D, 2), 1.0, 6.0, (), jnp.float32),
        "expert_in": noise(keys[11], (EXPERTS, D, 2 * FF), D ** -0.5, 0.21875, ((0, 4),)),
        "expert_out": noise(keys[12], (EXPERTS, FF, D), (FF // 2) ** -0.5, 0.1875, ((0, 4),)),
        "cotangent": noise(keys[13], (TOKENS, D), 1.0, 6.0, ((0, 32),)),
    }


precise = lax.Precision.HIGHEST
epsilon = 1e-06
masked_value = -1e+30

@jax.custom_vjp
def low(v):
    return lax.optimization_barrier(v.astype(jnp.bfloat16)).astype(jnp.float32)

@jax.custom_vjp
def low_back(v):
    return v

def low_keep(v):
    return (low(v), None)

def low_pass(kept, grad):
    return (grad,)

def back_keep(v):
    return (v, None)

def back_low(kept, grad):
    return (low(grad),)
low.defvjp(low_keep, low_pass)
low_back.defvjp(back_keep, back_low)

def rotary_tables(length, head_size):
    half_size = head_size // 2
    inverse = jnp.exp(jnp.arange(half_size, dtype=jnp.float32) * (-2.0 * math.log(10000.0) / head_size))
    angles = jnp.arange(length, dtype=jnp.float32)[:, None] * inverse[None, :]
    return (jnp.cos(angles)[:, None, :], jnp.sin(angles)[:, None, :])

def rotate(values, cos_table, sin_table):
    half_size = values.shape[-1] // 2
    front_half = values[..., :half_size]
    back_half = values[..., half_size:]
    return jnp.concatenate([front_half * cos_table - back_half * sin_table, back_half * cos_table + front_half * sin_table], axis=-1)

def inverse_rms(values):
    return lax.rsqrt(lax.optimization_barrier(jnp.mean(values * values, axis=-1, keepdims=True)) + epsilon)

def layer_step(params, block_data):
    ln1_gain, w_qkv, w_attn, ln2_gain, w_router, const_mix, const_vec, expert_in, expert_out = params
    tokens, segments, routes, prev_logits = block_data
    seq_count, length, model_width = tokens.shape
    head_count = model_width // HEAD_DIM
    normed_one = low(tokens * inverse_rms(tokens) * ln1_gain)
    projected = low_back(jnp.einsum('btd,de->bte', normed_one, w_qkv, precision=precise))
    projected = projected.reshape(seq_count, length, 3, head_count, HEAD_DIM)
    cos_table, sin_table = rotary_tables(length, HEAD_DIM)
    queries = low(rotate(projected[:, :, 0], cos_table, sin_table))
    key_rows = low(rotate(projected[:, :, 1], cos_table, sin_table))
    values = low(projected[:, :, 2])
    scores = low_back(jnp.einsum('bqhd,bkhd->bhqk', queries, key_rows, precision=precise) * 0.125)
    positions = jnp.arange(length)
    allowed = (segments[:, :, None] == segments[:, None, :]) & (positions[:, None] >= positions[None, :])[None]
    weights = low(jax.nn.softmax(jnp.where(allowed[:, None], scores, masked_value), axis=-1))
    attended = low_back(low(jnp.einsum('bhqk,bkhd->bqhd', weights, values, precision=precise)))
    attended = attended.reshape(seq_count, length, model_width)
    residual = tokens + low_back(jnp.einsum('btd,de->bte', attended, w_attn, precision=precise))
    normed_two = residual * inverse_rms(residual) * ln2_gain
    ffn_experts = expert_in.shape[0]
    capacity = length // 2
    total_experts = w_router.shape[1]
    hidden_width = expert_out.shape[1]
    logits = jnp.einsum('btd,de->bte', normed_two, w_router, precision=precise) + prev_logits
    choose = (routes[..., None] == jnp.arange(total_experts)).astype(jnp.float32)
    chosen = lax.optimization_barrier(jnp.sum(choose * logits[:, :, None, :], axis=-1))
    gate_weights = jax.nn.softmax(chosen, axis=-1)
    flat_routes = routes.reshape(seq_count, 2 * length)
    hit_table = (flat_routes[..., None] == jnp.arange(total_experts)).astype(jnp.int32)
    earlier = jnp.cumsum(hit_table, axis=1) - hit_table
    slot_index = lax.optimization_barrier(jnp.sum(earlier * hit_table, axis=-1)).reshape(seq_count, length, 2)
    targets = jnp.where(routes < ffn_experts, routes * capacity + slot_index, ffn_experts * capacity).astype(jnp.int32)
    sent_rows = low(normed_two)
    seq_index = jnp.arange(seq_count)[:, None]
    buffer = jnp.zeros((seq_count, ffn_experts * capacity + 1, model_width), jnp.float32)
    for route_slot in range(2):
        buffer = buffer.at[seq_index, targets[:, :, route_slot]].add(low_back(sent_rows))
    arriving = buffer[:, :ffn_experts * capacity].reshape(seq_count, ffn_experts, capacity, model_width)
    gate_up = low_back(jnp.einsum('becd,edf->becf', arriving, expert_in, precision=precise))
    hidden = low(jax.nn.silu(gate_up[..., :hidden_width]) * gate_up[..., hidden_width:])
    produced = low_back(low(jnp.einsum('becf,efd->becd', hidden, expert_out, precision=precise)))
    produced = jnp.concatenate([produced.reshape(seq_count, ffn_experts * capacity, model_width), jnp.zeros((seq_count, 1, model_width), jnp.float32)], axis=1)
    ffn_out = produced[seq_index[:, :, None], targets]
    mixing = jnp.einsum('btd,dm->btm', normed_two, const_mix, precision=precise).reshape(seq_count, length, 2, 2)
    shares = jax.nn.softmax(mixing, axis=-1)
    const_out = shares[..., 0:1] * normed_two[:, :, None, :] + shares[..., 1:2] * jnp.transpose(const_vec)[None, None]
    expert_values = ffn_out + choose[..., ffn_experts + 1:ffn_experts + 2] * normed_two[:, :, None, :]
    expert_values = expert_values + jnp.einsum('btkj,btjd->btkd', choose[..., ffn_experts + 2:], const_out, precision=precise)
    return residual + lax.optimization_barrier(jnp.sum(gate_weights[..., None] * expert_values, axis=2))

def reference(tokens, segments, routes, prev_logits, ln1_gain, w_qkv, w_attn, ln2_gain, w_router, const_mix, const_vec, expert_in, expert_out, cotangent):
    total_tokens, model_width = tokens.shape
    seq_total, length = segments.shape
    per_step = min(seq_total, max(1, 4096 // length))
    step_count = seq_total // per_step

    def split_rows(source_array):
        return source_array.reshape((step_count, per_step, length) + source_array.shape[1:])

    def forward(tokens_f, ln1_f, qkv_f, attn_f, ln2_f, router_f, mix_f, vec_f, in_f, out_f):
        params = (ln1_f, qkv_f, attn_f, ln2_f, router_f, mix_f, vec_f, in_f, out_f)

        def scan_step(scan_carry, block_data):
            return (scan_carry, layer_step(params, block_data))
        stacked = (split_rows(tokens_f), segments.reshape(step_count, per_step, length), split_rows(routes), split_rows(prev_logits))
        unused, step_outputs = lax.scan(jax.checkpoint(scan_step), jnp.zeros((), jnp.float32), stacked)
        return step_outputs.reshape(total_tokens, model_width)
    output, pullback = jax.vjp(forward, tokens.astype(jnp.float32), ln1_gain, w_qkv.astype(jnp.float32), w_attn.astype(jnp.float32), ln2_gain, w_router, const_mix, const_vec, expert_in.astype(jnp.float32), expert_out.astype(jnp.float32))
    gradients = pullback(cotangent.astype(jnp.float32))
    return (output.astype(jnp.bfloat16), gradients[0].astype(jnp.bfloat16), gradients[1], gradients[2], gradients[3], gradients[4], gradients[5], gradients[6], gradients[7], gradients[8], gradients[9])
```

```python
import functools
import math

import jax
import jax.numpy as jnp
import numpy as np
from jax import lax
from jax.experimental import pallas as pl
from jax.experimental.pallas import tpu as pltpu
from jax.sharding import PartitionSpec as P

HEAD_DIM = 64
EPS = 1e-06
MASKED = -1e30
F32 = jnp.float32
BF16 = jnp.bfloat16
VMEM_LIMIT = 62 * 1024 * 1024


def dot(a, b):
    return lax.dot_general(a, b, (((1,), (0,)), ((), ())), preferred_element_type=F32)


def dot_nt(a, b):
    return lax.dot_general(a, b, (((1,), (1,)), ((), ())), preferred_element_type=F32)


def dot_tn(a, b):
    return lax.dot_general(a, b, (((0,), (0,)), ((), ())), preferred_element_type=F32)


def tile(i, size):
    return pl.ds(pl.multiple_of(i * size, size), size)


def rotary_tables(length):
    half = HEAD_DIM // 2
    inverse = np.exp(np.arange(half, dtype=np.float32) * np.float32(-2.0 * math.log(10000.0) / HEAD_DIM))
    angles = np.arange(length, dtype=np.float32)[:, None] * inverse.astype(np.float32)[None, :]
    cos, sin = np.cos(angles), np.sin(angles)
    return (
        np.concatenate([cos] * 4, axis=1).astype(np.float32),
        np.concatenate([-sin, sin] * 2, axis=1).astype(np.float32),
    )


def rotate(x, cos, sin):
    lane = lax.broadcasted_iota(jnp.int32, x.shape, 1)
    front = (lane % HEAD_DIM) < HEAD_DIM // 2
    other = jnp.where(front, pltpu.roll(x, 96, 1), pltpu.roll(x, 32, 1))
    return x * cos + other * sin


def row_mean(x):
    return jnp.mean(x, axis=-1, keepdims=True)


def pick(x, lane, index):
    return jnp.sum(jnp.where(lane == index, x, 0.0), axis=-1, keepdims=True)


def half_mask(x, lane, which):
    keep = (lane < HEAD_DIM) if which == 0 else (lane >= HEAD_DIM)
    return jnp.where(keep, x, jnp.zeros_like(x))


def fwd_kernel(
    tok, seg, rT, pT, ln1, wqkv, wattn, ln2, wrT, cmT, cot, cos, sin,
    q, k, v, pw, att, n1, res, meta, send,
    proj, bias, wcat, rb, pb, n2b, n2l, gd,
):
    length, width = tok.shape
    capacity = length // 2
    experts = send.shape[0]

    @pl.loop(0, length // 64)
    def _(i):
        rows = tile(i, 64)
        x = tok[rows].astype(F32)
        r = lax.rsqrt(row_mean(x * x) + EPS)
        n1[rows] = (x * r * ln1[...]).astype(BF16)

    for kind, dst in enumerate((q, k, v)):

        @pl.loop(0, width // 256)
        def _(j):
            cols = pl.ds(pl.multiple_of(kind * width + j * 256, 256), 256)
            proj[...] = dot(n1[...], wqkv[:, cols])

            @pl.loop(0, length // 128)
            def _(i):
                rows = tile(i, 128)
                for part in range(2):
                    x = proj[rows, part * 128 : part * 128 + 128]
                    if kind < 2:
                        x = rotate(x, cos[rows], sin[rows])
                    if kind == 0:
                        x = x * 0.125
                    dst[rows, pl.ds(pl.multiple_of(j * 256 + part * 128, 128), 128)] = x.astype(BF16)

    seg_f = seg[...].astype(F32)
    rb[0] = jnp.transpose(jnp.broadcast_to(seg_f, (128, length)))

    @pl.loop(0, length // 128)
    def _(i):
        rows = tile(i, 128)
        row_id = lax.broadcasted_iota(jnp.int32, (128, length), 0) + i * 128
        col_id = lax.broadcasted_iota(jnp.int32, (128, length), 1)
        same = rb[0, rows, 0:1] == seg_f
        bias[rows] = jnp.where(same & (row_id >= col_id), 0.0, MASKED)

    block = length // 2

    @pl.loop(0, width // 128)
    def _(j):
        cols = tile(j, 128)
        for b in range(2):
            rows = slice(b * block, (b + 1) * block)
            nk = (b + 1) * block
            qlane = lax.broadcasted_iota(jnp.int32, (block, 128), 1)
            klane = lax.broadcasted_iota(jnp.int32, (nk, 128), 1)
            acc = jnp.zeros((block, 128), F32)
            for h in range(2):
                s = dot_nt(half_mask(q[rows, cols], qlane, h), k[0:nk, cols]) + bias[rows, 0:nk]
                m = jnp.max(s, axis=-1, keepdims=True)
                e = jnp.exp(s - m)
                w = (e * (1.0 / jnp.sum(e, axis=-1, keepdims=True))).astype(BF16)
                pw[2 * j + h, rows, 0:nk] = w
                acc = acc + dot(w, half_mask(v[0:nk, cols], klane, h))
            att[rows, cols] = acc.astype(BF16)

    @pl.loop(0, width // 256)
    def _(j):
        cols = tile(j, 256)
        res[:, cols] = tok[:, cols].astype(F32) + dot(att[...], wattn[:, cols])

    @pl.loop(0, length // 64)
    def _(i):
        rows = tile(i, 64)
        x = res[rows]
        n2 = x * lax.rsqrt(row_mean(x * x) + EPS) * ln2[...]
        high = n2.astype(BF16)
        n2b[rows] = high
        n2l[rows] = (n2 - high.astype(F32)).astype(BF16)

    wcat[...] = jnp.zeros_like(wcat)
    wcat[0:8] = wrT[...]
    wcat[8:12] = cmT[...]
    w_high = wcat[...].astype(BF16)
    w_low = (wcat[...] - w_high.astype(F32)).astype(BF16)

    for kk in range(2):
        rb[kk] = jnp.transpose(jnp.broadcast_to(rT[kk : kk + 1, :].astype(F32), (128, length)))
    pb[...] = jnp.zeros_like(pb)
    pb[0:8] = pT[...]
    rb[2] = jnp.transpose(pb[...])

    @pl.loop(0, length // 128)
    def _(i):
        rows = tile(i, 128)
        lane = lax.broadcasted_iota(jnp.int32, (128, 128), 1)
        lane_f = lane.astype(F32)
        high = n2b[rows]
        mixed = dot_nt(high, w_high) + dot_nt(high, w_low) + dot_nt(n2l[rows], w_high)
        logits = mixed + rb[2, rows]
        hits = [(rb[kk, rows] == lane_f).astype(F32) for kk in range(2)]
        chosen = [jnp.sum(h * logits, axis=-1, keepdims=True) for h in hits]
        top = jnp.maximum(chosen[0], chosen[1])
        e = [jnp.exp(c - top) for c in chosen]
        inv = 1.0 / (e[0] + e[1])
        gates = [v_ * inv for v_ in e]
        shares = []
        for j in range(2):
            a0, a1 = pick(mixed, lane, 8 + 2 * j), pick(mixed, lane, 9 + 2 * j)
            mx = jnp.maximum(a0, a1)
            b0, b1 = jnp.exp(a0 - mx), jnp.exp(a1 - mx)
            binv = 1.0 / (b0 + b1)
            shares.append((b0 * binv, b1 * binv))
        t_id = lax.broadcasted_iota(jnp.int32, (128, length), 0) + i * 128
        before = (t_id > lax.broadcasted_iota(jnp.int32, (128, length), 1)).astype(F32).astype(BF16)
        all_lane = lax.broadcasted_iota(jnp.int32, (length, 128), 1).astype(F32)
        count = ((rb[0] == all_lane).astype(F32) + (rb[1] == all_lane).astype(F32)).astype(BF16)
        place = dot(before, count) + lane_f * float(capacity) + 1.0
        target = [
            jnp.sum(jnp.where(lane < experts, h * place, 0.0), axis=-1, keepdims=True) - 1.0
            for h in hits
        ]
        gate_sum = gates[0] * hits[0] + gates[1] * hits[1]
        cg = [pick(gate_sum, lane, 6), pick(gate_sum, lane, 7)]
        keep = pick(gate_sum, lane, 5) + cg[0] * shares[0][0] + cg[1] * shares[1][0]
        values = (
            target[0], target[1], gates[0], gates[1], keep, cg[0], cg[1],
            shares[0][0], shares[0][1], shares[1][0], shares[1][1],
        )
        out = jnp.zeros((128, 128), F32)
        for n, value in enumerate(values):
            out = jnp.where(lane == n, value, out)
        meta[rows] = out
        g = cot[rows].astype(F32)
        for kk in range(2):
            gd[pl.ds(pl.multiple_of(kk * length + i * 128, 128), 128)] = (g * gates[kk]).astype(BF16)

    meta_t = jnp.transpose(meta[...])

    @pl.loop(0, experts)
    def _(e):
        s_id = (lax.broadcasted_iota(jnp.int32, (capacity, length), 0) + e * capacity).astype(F32)
        first = (meta_t[0:1] == s_id).astype(F32).astype(BF16)
        second = (meta_t[1:2] == s_id).astype(F32).astype(BF16)
        send[e, 0:capacity] = dot(first + second, n2b[...]).astype(BF16)
        send[e, capacity : 2 * capacity] = (
            dot(first, gd[0:length]) + dot(second, gd[length : 2 * length])
        ).astype(BF16)


def expert_kernel(arr, win, wout, ret, d_in, d_out, x, dy, hid, dgu, ffn, dsent):
    groups, both, width = arr.shape
    capacity = both // 2
    hidden = wout.shape[1]
    ft = hid.shape[1]
    for s in range(groups):
        x[s * capacity : (s + 1) * capacity] = arr[s, 0:capacity]
        dy[s * capacity : (s + 1) * capacity] = arr[s, capacity:both]

    @pl.loop(0, hidden // ft)
    def _(f):
        gate_cols = tile(f, ft)
        up_cols = pl.ds(pl.multiple_of(hidden + f * ft, ft), ft)

        @pl.loop(0, groups)
        def _(s):
            rows = tile(s, capacity)
            gate = dot(x[rows], win[0, :, gate_cols])
            up = dot(x[rows], win[0, :, up_cols])
            dh = dot_nt(dy[rows], wout[0, gate_cols, :])
            sig = 1.0 / (1.0 + jnp.exp(-gate))
            silu = gate * sig
            hid[rows] = (silu * up).astype(BF16)
            dgu[rows, 0:ft] = (dh * up * sig * (1.0 + gate * (1.0 - sig))).astype(BF16)
            dgu[rows, ft : 2 * ft] = (dh * silu).astype(BF16)

        d_in[:, gate_cols] = dot_tn(x[...], dgu[:, 0:ft]).astype(BF16)
        d_in[:, up_cols] = dot_tn(x[...], dgu[:, ft : 2 * ft]).astype(BF16)
        d_out[gate_cols] = dot_tn(hid[...], dy[...]).astype(BF16)

        @pl.loop(0, groups)
        def _(s):
            rows = tile(s, capacity)
            y = dot(hid[rows], wout[0, gate_cols, :])
            d = dot_nt(dgu[rows, 0:ft], win[0, :, gate_cols]) + dot_nt(
                dgu[rows, ft : 2 * ft], win[0, :, up_cols]
            )

            @pl.when(f == 0)
            def _():
                ffn[rows] = y
                dsent[rows] = d

            @pl.when(f > 0)
            def _():
                ffn[rows] += y
                dsent[rows] += d

    for s in range(groups):
        ret[s, 0:capacity] = ffn[s * capacity : (s + 1) * capacity].astype(BF16)
        ret[s, capacity:both] = dsent[s * capacity : (s + 1) * capacity].astype(BF16)


def bwd_kernel(
    tok, cot, res, meta, rT, ret, q, k, v, pw, att, n1, ln1, wqkv, wattn, ln2, wrT, cmT, cvT, cos, sin,
    out, igrad, d_qkv, d_attn, d_small,
    wcat, rb, fk0, fk1, dsn, dcat, n2b, dres, dbr, dproj, datt, dkv, lnacc, rr,
):
    length, width = tok.shape
    experts, both, _ = ret.shape
    capacity = both // 2

    wcat[...] = jnp.zeros_like(wcat)
    wcat[0:8] = wrT[...]
    wcat[8:12] = cmT[...]
    for kk in range(2):
        rb[kk] = jnp.transpose(jnp.broadcast_to(rT[kk : kk + 1, :].astype(F32), (128, length)))

    for s in range(experts):
        rr[s * capacity : (s + 1) * capacity] = ret[s, 0:capacity]
        rr[(experts + s) * capacity : (experts + s + 1) * capacity] = ret[s, capacity:both]
    slots = experts * capacity

    @pl.loop(0, length // 256)
    def _(i):
        rows = tile(i, 256)
        s_id = lax.broadcasted_iota(jnp.int32, (256, slots), 1).astype(F32)
        first = (meta[rows, 0:1] == s_id).astype(F32).astype(BF16)
        second = (meta[rows, 1:2] == s_id).astype(F32).astype(BF16)
        fk0[rows] = dot(first, rr[0:slots])
        fk1[rows] = dot(second, rr[0:slots])
        dsn[rows] = dot(first + second, rr[slots : 2 * slots])

    w_high = wcat[...].astype(BF16)
    lnacc[...] = jnp.zeros_like(lnacc)

    @pl.loop(0, length // 64)
    def _(i):
        rows = tile(i, 64)
        lane = lax.broadcasted_iota(jnp.int32, (64, 128), 1)
        lane_f = lane.astype(F32)
        m = meta[rows]
        g0, g1, keep = m[:, 2:3], m[:, 3:4], m[:, 4:5]
        cg = (m[:, 5:6], m[:, 6:7])
        shares = ((m[:, 7:8], m[:, 8:9]), (m[:, 9:10], m[:, 10:11]))
        g = cot[rows].astype(F32)
        x = res[rows]
        r2 = lax.rsqrt(row_mean(x * x) + EPS)
        xr = x * r2
        n2 = xr * ln2[...]
        n2b[rows] = n2.astype(BF16)
        f0, f1 = fk0[rows], fk1[rows]
        cv = (cvT[0:1, :], cvT[1:2, :])
        out[rows] = (
            x + g0 * f0 + g1 * f1 + keep * n2 + (cg[0] * shares[0][1]) * cv[0] + (cg[1] * shares[1][1]) * cv[1]
        ).astype(BF16)
        gn2 = jnp.sum(g * n2, axis=-1, keepdims=True)
        gcv = [jnp.sum(g * c, axis=-1, keepdims=True) for c in cv]
        hits = [(rb[kk, rows] == lane_f).astype(F32) for kk in range(2)]
        special = jnp.where(lane == 5, gn2, 0.0)
        for j in range(2):
            special = jnp.where(lane == 6 + j, shares[j][0] * gn2 + shares[j][1] * gcv[j], special)
        dg = [
            jnp.sum(g * f, axis=-1, keepdims=True) + jnp.sum(h * special, axis=-1, keepdims=True)
            for f, h in zip((f0, f1), hits)
        ]
        mean_dg = g0 * dg[0] + g1 * dg[1]
        dc0, dc1 = g0 * (dg[0] - mean_dg), g1 * (dg[1] - mean_dg)
        cat = hits[0] * dc0 + hits[1] * dc1
        for j in range(2):
            dm0, dm1 = cg[j] * gn2, cg[j] * gcv[j]
            mean_dm = shares[j][0] * dm0 + shares[j][1] * dm1
            cat = jnp.where(lane == 8 + 2 * j, shares[j][0] * (dm0 - mean_dm), cat)
            cat = jnp.where(lane == 9 + 2 * j, shares[j][1] * (dm1 - mean_dm), cat)
        dcat[rows, 0:128] = cat.astype(BF16)
        vecs = jnp.where(lane == 12, cg[0] * shares[0][1], 0.0)
        vecs = jnp.where(lane == 13, cg[1] * shares[1][1], vecs)
        dcat[rows, 128:256] = vecs.astype(BF16)
        dn2 = keep * g + dsn[rows] + dot(cat.astype(BF16), w_high)
        lnacc[0:8] += jnp.sum((dn2 * xr).reshape(8, 8, width), axis=0)
        dn = dn2 * ln2[...]
        dr = g + r2 * dn - xr * (r2 * r2) * row_mean(dn * x)
        dres[rows] = dr
        dbr[rows] = dr.astype(BF16)

    d_small[...] = dot_tn(n2b[...], dcat[:, 0:128]) + dot_tn(cot[...], dcat[:, 128:256])

    @pl.loop(0, width // 256)
    def _(j):
        cols = tile(j, 256)
        datt[:, cols] = dot_nt(dbr[...], wattn[cols, :]).astype(BF16)
        d_attn[:, cols] = dot_tn(att[...], dbr[:, cols])

    block = length // 2

    @pl.loop(0, width // 128)
    def _(j):
        cols = tile(j, 128)
        dkv[...] = jnp.zeros_like(dkv)
        for b in range(2):
            rows = slice(b * block, (b + 1) * block)
            nk = (b + 1) * block
            qlane = lax.broadcasted_iota(jnp.int32, (block, 128), 1)
            klane = lax.broadcasted_iota(jnp.int32, (nk, 128), 1)
            do = datt[rows, cols]
            prod = do.astype(F32) * att[rows, cols].astype(F32)
            dq = jnp.zeros((block, 128), F32)
            for h in range(2):
                delta = jnp.sum(half_mask(prod, qlane, h), axis=-1, keepdims=True)
                dom = half_mask(do, qlane, h)
                dp = dot_nt(dom, v[0:nk, cols])
                w = pw[2 * j + h, rows, 0:nk]
                ds = (w.astype(F32) * (dp - delta)).astype(BF16)
                dq = dq + dot(ds, half_mask(k[0:nk, cols], klane, h))
                dkv[0, 0:nk] += dot_tn(ds, half_mask(q[rows, cols], qlane, h))
                dkv[1, 0:nk] += dot_tn(w, dom)
            dproj[rows, cols] = rotate(dq * 0.125, cos[rows], -sin[rows]).astype(BF16)
        dproj[:, pl.ds(pl.multiple_of(width + j * 128, 128), 128)] = rotate(dkv[0], cos[...], -sin[...]).astype(BF16)
        dproj[:, pl.ds(pl.multiple_of(2 * width + j * 128, 128), 128)] = dkv[1].astype(BF16)

    @pl.loop(0, 3 * width // 256)
    def _(j):
        cols = tile(j, 256)
        d_qkv[:, cols] = dot_tn(n1[...], dproj[:, cols])

    @pl.loop(0, width // 256)
    def _(j):
        cols = tile(j, 256)
        fk0[:, cols] = dot_nt(dproj[...], wqkv[cols, :])

    @pl.loop(0, length // 64)
    def _(i):
        rows = tile(i, 64)
        x = tok[rows].astype(F32)
        r1 = lax.rsqrt(row_mean(x * x) + EPS)
        xr = x * r1
        d = fk0[rows]
        dn = d * ln1[...]
        lnacc[8:16] += jnp.sum((d * xr).reshape(8, 8, width), axis=0)
        igrad[rows] = (dres[rows] + r1 * dn - xr * (r1 * r1) * row_mean(dn * x)).astype(BF16)

    ln = jnp.zeros((128, width), F32)
    row = lax.broadcasted_iota(jnp.int32, (128, width), 0)
    ln = jnp.where(row == 14, jnp.sum(lnacc[8:16], axis=0, keepdims=True), ln)
    ln = jnp.where(row == 15, jnp.sum(lnacc[0:8], axis=0, keepdims=True), ln)
    d_small[...] += jnp.transpose(ln)


def shape(*s, dtype=BF16):
    return jax.ShapeDtypeStruct(s, dtype)


def call(kernel, outs, scratch, args, name):
    return pl.pallas_call(
        kernel,
        out_shape=outs,
        in_specs=[pl.BlockSpec(memory_space=pltpu.VMEM)] * len(args),
        out_specs=[pl.BlockSpec(memory_space=pltpu.VMEM)] * len(outs),
        scratch_shapes=scratch,
        compiler_params=pltpu.CompilerParams(vmem_limit_bytes=VMEM_LIMIT),
        name=name,
    )(*args)


def body(
    tokens, segments, routes, prev_logits, ln1_gain, w_qkv, w_attn, ln2_gain, w_router, const_mix, const_vec,
    expert_in, expert_out, cotangent,
):
    length, width = tokens.shape
    heads = width // HEAD_DIM
    experts = lax.axis_size("expert") * expert_in.shape[0]
    hidden = expert_out.shape[1]
    capacity = length // 2
    slots = experts * capacity
    V = pltpu.VMEM
    cos, sin = (jnp.asarray(t) for t in rotary_tables(length))
    rT, pT = routes.T, prev_logits.T
    wrT, cmT, cvT = w_router.T, const_mix.T, const_vec.T
    ln1, ln2 = ln1_gain.reshape(1, width), ln2_gain.reshape(1, width)

    q, k, v, pw, att, n1, res, meta, send = call(
        fwd_kernel,
        [
            shape(length, width), shape(length, width), shape(length, width), shape(heads, length, length),
            shape(length, width), shape(length, width), shape(length, width, dtype=F32),
            shape(length, 128, dtype=F32), shape(experts, length, width),
        ],
        [
            V((length, 256), F32), V((length, length), F32), V((128, width), F32), V((3, length, 128), F32),
            V((128, length), F32), V((length, width), BF16), V((length, width), BF16), V((2 * length, width), BF16),
        ],
        (tokens, segments, rT, pT, ln1, w_qkv, w_attn, ln2, wrT, cmT, cotangent, cos, sin),
        "attention",
    )
    arr = lax.all_to_all(send, "expert", split_axis=0, concat_axis=0, tiled=True)
    ft = 256
    ret, d_in, d_out = call(
        expert_kernel,
        [shape(experts, length, width), shape(width, 2 * hidden), shape(hidden, width)],
        [
            V((slots, width), BF16), V((slots, width), BF16), V((slots, ft), BF16), V((slots, 2 * ft), BF16),
            V((slots, width), F32), V((slots, width), F32),
        ],
        (arr, expert_in, expert_out),
        "experts",
    )
    back = lax.all_to_all(ret, "expert", split_axis=0, concat_axis=0, tiled=True)
    g_in = lax.psum_scatter(d_in, "dp", scatter_dimension=0, tiled=True).astype(F32)[None]
    g_out = lax.psum_scatter(d_out, "dp", scatter_dimension=0, tiled=True).astype(F32)[None]
    out, igrad, d_qkv, d_attn, d_small = call(
        bwd_kernel,
        [
            shape(length, width), shape(length, width), shape(width, 3 * width, dtype=F32),
            shape(width, width, dtype=F32), shape(width, 128, dtype=F32),
        ],
        [
            V((128, width), F32), V((2, length, 128), F32), V((length, width), F32), V((length, width), F32),
            V((length, width), F32), V((length, 256), BF16), V((length, width), BF16), V((length, width), F32),
            V((length, width), BF16), V((length, 3 * width), BF16), V((length, width), BF16),
            V((2, length, 128), F32), V((16, width), F32), V((2 * slots, width), BF16),
        ],
        (
            tokens, cotangent, res, meta, rT, back, q, k, v, pw, att, n1, ln1, w_qkv, w_attn, ln2, wrT, cmT, cvT,
            cos, sin,
        ),
        "backward",
    )
    both = ("dp", "expert")
    d_qkv = lax.psum_scatter(d_qkv, both, scatter_dimension=0, tiled=True)
    d_attn = lax.psum_scatter(d_attn, both, scatter_dimension=0, tiled=True)
    small = lax.psum_scatter(d_small, both, scatter_dimension=0, tiled=True)
    return (
        out, igrad, small[:, 14], d_qkv, d_attn, small[:, 15], small[:, 0:8], small[:, 8:12], small[:, 12:14],
        g_in, g_out,
    )


def solution(mesh):
    rows = P(("dp", "expert"), None)
    return jax.shard_map(
        body,
        mesh=mesh,
        in_specs=(
            rows, rows, rows, rows, P(), P(), P(), P(), P(), P(), P(),
            P("expert", None, None), P("expert", None, None), rows,
        ),
        out_specs=(
            rows, rows, P(("dp", "expert")), rows, rows, P(("dp", "expert")), rows, rows, rows,
            P("expert", "dp", None), P("expert", "dp", None),
        ),
        check_vma=False,
    )
```

```python
import functools
import math

import jax
import jax.numpy as jnp
import numpy as np
from jax import lax
from jax.experimental import pallas as pl
from jax.experimental.pallas import tpu as pltpu
from jax.sharding import PartitionSpec as P

HEAD_DIM = 64
EPS = 1e-06
MASKED = -1e30
F32 = jnp.float32
BF16 = jnp.bfloat16
VMEM_LIMIT = 62 * 1024 * 1024


def dot(a, b):
    return lax.dot_general(a, b, (((1,), (0,)), ((), ())), preferred_element_type=F32)


def dot_nt(a, b):
    return lax.dot_general(a, b, (((1,), (1,)), ((), ())), preferred_element_type=F32)


def dot_tn(a, b):
    return lax.dot_general(a, b, (((0,), (0,)), ((), ())), preferred_element_type=F32)


def tile(i, size):
    return pl.ds(pl.multiple_of(i * size, size), size)


def rotary_tables(length):
    half = HEAD_DIM // 2
    inverse = np.exp(np.arange(half, dtype=np.float32) * np.float32(-2.0 * math.log(10000.0) / HEAD_DIM))
    angles = np.arange(length, dtype=np.float32)[:, None] * inverse.astype(np.float32)[None, :]
    cos, sin = np.cos(angles), np.sin(angles)
    return (
        np.concatenate([cos] * 4, axis=1).astype(np.float32),
        np.concatenate([-sin, sin] * 2, axis=1).astype(np.float32),
    )


def rotate(x, cos, sin):
    lane = lax.broadcasted_iota(jnp.int32, x.shape, 1)
    front = (lane % HEAD_DIM) < HEAD_DIM // 2
    other = jnp.where(front, pltpu.roll(x, 96, 1), pltpu.roll(x, 32, 1))
    return x * cos + other * sin


def row_mean(x):
    return jnp.mean(x, axis=-1, keepdims=True)


def pick(x, lane, index):
    return jnp.sum(jnp.where(lane == index, x, 0.0), axis=-1, keepdims=True)


def half_mask(x, lane, which):
    keep = (lane < HEAD_DIM) if which == 0 else (lane >= HEAD_DIM)
    return jnp.where(keep, x, jnp.zeros_like(x))


MESH = pl.DeviceIdType.MESH


def flip(i, m):
    return i + m * (1 - 2 * ((i // m) % 2))


def side(mask):
    axis, m = mask
    return (lax.axis_index(axis) // m) % 2


def partner(mask):
    axis, m = mask
    return {axis: flip(lax.axis_index(axis), m)}


def greet(masks, shifts=0):
    barrier = pltpu.get_barrier_semaphore()
    for mask in masks:
        pl.semaphore_signal(barrier, inc=1, device_id=partner(mask), device_id_type=MESH)
    n = lax.axis_size("expert")
    for o in range(1, shifts + 1):
        dest = lax.rem(lax.axis_index("expert") + o, n)
        pl.semaphore_signal(barrier, inc=1, device_id={"expert": dest}, device_id_type=MESH)
    pl.semaphore_wait(barrier, len(masks) + shifts)


def exchange(src, dst, send_sem, recv_sem):
    n = lax.axis_size("expert")
    me = lax.axis_index("expert")
    copies = []
    for o in range(1, n):
        dest = lax.rem(me + o, n)
        copies.append(
            pltpu.make_async_remote_copy(
                src.at[dest], dst.at[me], send_sem.at[o - 1], recv_sem.at[o - 1],
                device_id={"expert": dest}, device_id_type=MESH,
            )
        )
    return copies


def half_copy(src, dst, mask, rows, send_sem, recv_sem):
    start = pl.multiple_of((1 - side(mask)) * rows, 8)
    return pltpu.make_async_remote_copy(
        src.at[pl.ds(start, rows)], dst, send_sem, recv_sem, device_id=partner(mask), device_id_type=MESH
    )


def half_add(src, dst, mask, rows, out=None):
    start = side(mask) * rows
    step = 48 if rows % 48 == 0 else 64 if rows % 64 == 0 else 24
    out = dst if out is None else out

    @pl.loop(0, rows // step)
    def _(i):
        here = pl.ds(pl.multiple_of(i * step, 8), step)
        mine = src[pl.ds(pl.multiple_of(start + i * step, 8), step)].astype(F32)
        out[here] = (mine + dst[here].astype(F32)).astype(out.dtype)


def place_of(shard, masks):
    place = 0
    for m in masks:
        place = 2 * place + (shard // m) % 2
    return place


def fwd_kernel(
    tok, seg, rT, pT, ln1, wqkv, wattn, ln2, wrT, cmT, cot, cos, sin,
    q, k, v, pw, att, n1, res, meta, send, g_rows,
    proj, bias, wcat, rb, pb, n2b, n2l, gl, tg, onehot, g_out, send_sem, recv_sem,
):
    length, width = tok.shape
    capacity = length // 2
    experts = send.shape[0]

    greet((), experts - 1)
    for kk in range(2):
        rb[kk] = jnp.transpose(jnp.broadcast_to(rT[kk : kk + 1, :].astype(F32), (128, length)))
    all_lane = lax.broadcasted_iota(jnp.int32, (length, 128), 1).astype(F32)
    count = ((rb[0] == all_lane).astype(F32) + (rb[1] == all_lane).astype(F32)).astype(BF16)

    @pl.loop(0, length // 128)
    def _(i):
        rows = tile(i, 128)
        lane = lax.broadcasted_iota(jnp.int32, (128, 128), 1)
        lane_f = lane.astype(F32)
        t_id = lax.broadcasted_iota(jnp.int32, (128, length), 0) + i * 128
        before = (t_id > lax.broadcasted_iota(jnp.int32, (128, length), 1)).astype(F32).astype(BF16)
        place = dot(before, count) + lane_f * float(capacity) + 1.0
        out = jnp.zeros((128, 128), F32)
        for kk in range(2):
            hit = (rb[kk, rows] == lane_f) & (lane < experts)
            out = jnp.where(lane == kk, jnp.sum(jnp.where(hit, place, 0.0), axis=-1, keepdims=True) - 1.0, out)
        tg[rows] = out

    target = jnp.transpose(tg[...])
    pb[...] = target

    @pl.loop(0, experts)
    def _(e):
        s_id = (lax.broadcasted_iota(jnp.int32, (capacity, length), 0) + e * capacity).astype(F32)
        here = (pb[0:1] == s_id).astype(F32) + (pb[1:2] == s_id).astype(F32)
        onehot[tile(e, capacity)] = here.astype(BF16)
        g_out[e] = dot(here.astype(BF16), cot[...]).astype(BF16)

    copies = exchange(g_out, g_rows, send_sem, recv_sem)
    for c in copies:
        c.start()
    me = lax.axis_index("expert")
    g_rows[me] = g_out[me]

    @pl.loop(0, length // 64)
    def _(i):
        rows = tile(i, 64)
        x = tok[rows].astype(F32)
        r = lax.rsqrt(row_mean(x * x) + EPS)
        n1[rows] = (x * r * ln1[...]).astype(BF16)

    for kind, dst in enumerate((q, k, v)):

        @pl.loop(0, width // 256)
        def _(j):
            cols = pl.ds(pl.multiple_of(kind * width + j * 256, 256), 256)
            proj[...] = dot(n1[...], wqkv[:, cols])

            @pl.loop(0, length // 128)
            def _(i):
                rows = tile(i, 128)
                for part in range(2):
                    x = proj[rows, part * 128 : part * 128 + 128]
                    if kind < 2:
                        x = rotate(x, cos[rows], sin[rows])
                    if kind == 0:
                        x = x * 0.125
                    dst[rows, pl.ds(pl.multiple_of(j * 256 + part * 128, 128), 128)] = x.astype(BF16)

    seg_f = seg[...].astype(F32)
    rb[2] = jnp.transpose(jnp.broadcast_to(seg_f, (128, length)))

    @pl.loop(0, length // 128)
    def _(i):
        rows = tile(i, 128)
        row_id = lax.broadcasted_iota(jnp.int32, (128, length), 0) + i * 128
        col_id = lax.broadcasted_iota(jnp.int32, (128, length), 1)
        same = rb[2, rows, 0:1] == seg_f
        bias[rows] = jnp.where(same & (row_id >= col_id), 0.0, MASKED)

    block = length // 2

    @pl.loop(0, width // 128)
    def _(j):
        cols = tile(j, 128)
        for b in range(2):
            rows = slice(b * block, (b + 1) * block)
            nk = (b + 1) * block
            qlane = lax.broadcasted_iota(jnp.int32, (block, 128), 1)
            klane = lax.broadcasted_iota(jnp.int32, (nk, 128), 1)
            acc = jnp.zeros((block, 128), F32)
            for h in range(2):
                s = dot_nt(half_mask(q[rows, cols], qlane, h), k[0:nk, cols]) + bias[rows, 0:nk]
                m = jnp.max(s, axis=-1, keepdims=True)
                e = jnp.exp(s - m)
                w = (e * (1.0 / jnp.sum(e, axis=-1, keepdims=True))).astype(BF16)
                pw[2 * j + h, rows, 0:nk] = w
                acc = acc + dot(w, half_mask(v[0:nk, cols], klane, h))
            att[rows, cols] = acc.astype(BF16)

    @pl.loop(0, width // 256)
    def _(j):
        cols = tile(j, 256)
        res[:, cols] = tok[:, cols].astype(F32) + dot(att[...], wattn[:, cols])

    @pl.loop(0, length // 64)
    def _(i):
        rows = tile(i, 64)
        x = res[rows]
        n2 = x * lax.rsqrt(row_mean(x * x) + EPS) * ln2[...]
        high = n2.astype(BF16)
        n2b[rows] = high
        n2l[rows] = (n2 - high.astype(F32)).astype(BF16)

    wcat[...] = jnp.zeros_like(wcat)
    wcat[0:8] = wrT[...]
    wcat[8:12] = cmT[...]
    w_high = wcat[...].astype(BF16)
    w_low = (wcat[...] - w_high.astype(F32)).astype(BF16)

    pb[8:16] = pT[...]
    rb[2] = jnp.transpose(jnp.concatenate([pb[8:16], jnp.zeros((120, length), F32)], axis=0))

    @pl.loop(0, length // 128)
    def _(i):
        rows = tile(i, 128)
        lane = lax.broadcasted_iota(jnp.int32, (128, 128), 1)
        lane_f = lane.astype(F32)
        high = n2b[rows]
        mixed = dot_nt(high, w_high) + dot_nt(high, w_low) + dot_nt(n2l[rows], w_high)
        logits = mixed + rb[2, rows]
        hits = [(rb[kk, rows] == lane_f).astype(F32) for kk in range(2)]
        chosen = [jnp.sum(h * logits, axis=-1, keepdims=True) for h in hits]
        top = jnp.maximum(chosen[0], chosen[1])
        e = [jnp.exp(c - top) for c in chosen]
        inv = 1.0 / (e[0] + e[1])
        gates = [v_ * inv for v_ in e]
        shares = []
        for j in range(2):
            a0, a1 = pick(mixed, lane, 8 + 2 * j), pick(mixed, lane, 9 + 2 * j)
            mx = jnp.maximum(a0, a1)
            b0, b1 = jnp.exp(a0 - mx), jnp.exp(a1 - mx)
            binv = 1.0 / (b0 + b1)
            shares.append((b0 * binv, b1 * binv))
        gate_sum = gates[0] * hits[0] + gates[1] * hits[1]
        cg = [pick(gate_sum, lane, 6), pick(gate_sum, lane, 7)]
        keep = pick(gate_sum, lane, 5) + cg[0] * shares[0][0] + cg[1] * shares[1][0]
        values = (
            gates[0], gates[1], keep, cg[0], cg[1], shares[0][0], shares[0][1], shares[1][0], shares[1][1],
        )
        out = tg[rows]
        for n, value in enumerate(values):
            out = jnp.where(lane == n + 2, value, out)
        meta[rows] = out
        for kk in range(2):
            g_high = gates[kk].astype(BF16).astype(F32)
            both = jnp.where(lane == 0, g_high, jnp.where(lane == 1, gates[kk] - g_high, 0.0))
            gl[pl.ds(pl.multiple_of(kk * length + i * 128, 128), 128)] = both.astype(BF16)

    @pl.loop(0, experts)
    def _(e):
        s_id = (lax.broadcasted_iota(jnp.int32, (capacity, length), 0) + e * capacity).astype(F32)
        gate = jnp.zeros((capacity, 128), F32)
        for kk in range(2):
            here = (pb[kk : kk + 1] == s_id).astype(F32).astype(BF16)
            gate = gate + dot(here, gl[kk * length : (kk + 1) * length])
        send[e, :, 0:width] = dot(onehot[tile(e, capacity)], n2b[...]).astype(BF16)
        send[e, :, width : width + 128] = gate.astype(BF16)

    for c in copies:
        c.wait()


def expert_kernel(stages, xs, g_rows, win, wout, *refs):
    if stages:
        f_back, d_back, p_in, p_out = refs[:4]
        refs = refs[4:]
    else:
        f_back, d_back, gi, go = refs[:4]
        refs = refs[4:]
    xr, dy, hid, fa, fb, dgu, acc, stage = refs[:8]
    refs = refs[8:]
    if stages:
        gi, go, in_send, in_recv, out_send, out_recv = refs[:6]
        refs = refs[6:]
    x_send, x_recv, f_send, f_recv, d_send, d_recv = refs
    groups, capacity, wide = xs.shape
    hidden, width = wout.shape[1:]
    tiles, _, ft = hid.shape
    slabs = go.shape[0]
    me = lax.axis_index("expert")

    greet([s[0] for s in stages[:2]], groups - 1)
    copies = exchange(xs, xr, x_send, x_recv)
    for c in copies:
        c.start()
    xr[me] = xs[me]
    for c in copies:
        c.wait()
    for s in range(groups):
        pair = xr[s, :, width:wide].astype(F32)
        lane = lax.broadcasted_iota(jnp.int32, pair.shape, 1)
        gate = jnp.sum(jnp.where(lane < 2, pair, 0.0), axis=-1, keepdims=True)
        dy[s] = (g_rows[s].astype(F32) * gate).astype(BF16)

    @pl.loop(0, tiles)
    def _(f):
        gate_cols = tile(f, ft)
        up_cols = pl.ds(pl.multiple_of(hidden + f * ft, ft), ft)

        @pl.loop(0, groups)
        def _(s):
            rows = tile(s, capacity)
            gate = dot(xr[s, :, 0:width], win[0, :, gate_cols])
            up = dot(xr[s, :, 0:width], win[0, :, up_cols])
            sig = 1.0 / (1.0 + jnp.exp(-gate))
            silu = gate * sig
            h = (silu * up).astype(BF16)
            hid[f, rows] = h
            fa[f, rows] = (up * sig * (1.0 + gate * (1.0 - sig))).astype(BF16)
            fb[f, rows] = silu.astype(BF16)
            y = dot(h, wout[0, gate_cols, :])

            @pl.when(f == 0)
            def _():
                acc[s] = y

            @pl.when(f > 0)
            def _():
                acc[s] += y

    stage[0] = acc[...].astype(BF16)
    f_copies = exchange(stage.at[0], f_back, f_send, f_recv)
    for c in f_copies:
        c.start()
    f_back[me] = stage[0, me]

    shards = 2 ** len(stages[0]) if stages else 0
    in_rows, out_rows = width // 2, hidden // 2
    half = tiles // 2
    for part in range(2):
        masks = stages[part] if stages else ()

        @pl.loop(part * half, (part + 1) * half)
        def _(f):
            gate_cols = tile(f, ft)
            up_cols = pl.ds(pl.multiple_of(hidden + f * ft, ft), ft)

            @pl.loop(0, groups)
            def _(s):
                rows = tile(s, capacity)
                dh = dot_nt(dy[s], wout[0, gate_cols, :])
                da = (dh * fa[f, rows].astype(F32)).astype(BF16)
                db = (dh * fb[f, rows].astype(F32)).astype(BF16)
                dgu[rows, 0:ft] = da
                dgu[rows, ft : 2 * ft] = db
                d = dot_nt(da, win[0, :, gate_cols]) + dot_nt(db, win[0, :, up_cols])

                @pl.when(f == 0)
                def _():
                    acc[s] = d

                @pl.when(f > 0)
                def _():
                    acc[s] += d

            for p in range(2):
                cols = slice(p * ft, (p + 1) * ft)
                d = dot_tn(xr[:, :, 0:width].reshape(groups * capacity, width), dgu[:, cols])
                if not stages:
                    gi[f, :, cols] = d.astype(BF16)
                    continue
                size = width // shards
                for j in range(shards):
                    at = place_of(j, [m for _, m in masks]) * size
                    gi[f, at : at + size, cols] = d[j * size : (j + 1) * size].astype(BF16)
            if stages:
                half_copy(gi.at[f], p_in.at[f], masks[0], in_rows, in_send.at[f], in_recv.at[f]).start()

    stage[1] = acc[...].astype(BF16)
    d_copies = exchange(stage.at[1], d_back, d_send, d_recv)
    for c in d_copies:
        c.start()
    d_back[me] = stage[1, me]

    out_copies = []
    size = hidden // tiles
    for c in range(slabs):
        cols = slice(c * (width // slabs), (c + 1) * (width // slabs))
        masks = stages[c % 2] if stages else ()

        @pl.loop(0, tiles)
        def _(t):
            at = place_of(t, [m for _, m in masks]) if stages else t
            go[c, tile(at, size)] = dot_tn(hid[t], dy[:, :, cols].reshape(groups * capacity, width // slabs)).astype(BF16)

        if stages:
            out_copies.append(half_copy(go.at[c], p_out.at[c], masks[0], out_rows, out_send.at[c], out_recv.at[c]))
            out_copies[-1].start()

    if stages:
        for part in range(2):
            masks = stages[part]

            @pl.loop(part * half, (part + 1) * half)
            def _(f):
                half_copy(gi.at[f], p_in.at[f], masks[0], in_rows, in_send.at[f], in_recv.at[f]).wait()
                half_add(gi.at[f], p_in.at[f], masks[0], in_rows)

        for c in range(slabs):
            out_copies[c].wait()
            half_add(go.at[c], p_out.at[c], stages[c % 2][0], out_rows)
    for c in f_copies + d_copies:
        c.wait()


def bwd_kernel(plan, *refs):
    (
        tok, cot, res, meta, rT, f_back, d_back, q, k, v, pw, att, n1, ln1, wqkv, wattn, ln2, wrT, cmT, cvT, cos, sin,
    ) = refs[:22]
    refs = refs[22:]
    if plan:
        stages, order = plan
        p_in, p_out, out, igrad, d_qkv, d_attn, d_small, g_in, g_out = refs[:9]
        refs = refs[9:]
    else:
        out, igrad, d_qkv, d_attn, d_small = refs[:5]
        refs = refs[5:]
    wcat, rb, fk0, fk1, dsn, dcat, n2b, dres, dbr, dproj, datt, dkv, lnacc = refs[:13]
    refs = refs[13:]
    length, width = tok.shape
    experts, capacity, _ = f_back.shape
    slots = experts * capacity
    block = length // 2

    halves = []
    if plan:
        in1, in2, out1, out2, in_send, in_recv, out_send, out_recv, gq, ga = refs[:10]
        gq_recv, ga_recv, g_last, r_last, fin, q_send, q_recv = (
            refs[10:14], refs[14:18], refs[18], refs[19], refs[20], refs[21], refs[22],
        )
        greet(order, 0)
        slabs_in, slabs_out = p_in.shape[0], p_out.shape[0]
        in_rows, out_rows = in1.shape[1], out1.shape[1]

        def in_copy(i, s):
            masks = stages[i * 2 // slabs_in]
            src, dst = ((p_in, in1), (in1, in2))[s]
            return half_copy(
                src.at[i], dst.at[i], masks[s + 1], dst.shape[1], in_send.at[s, i], in_recv.at[s, i]
            )

        def out_copy(i, s):
            masks = stages[i % 2]
            src, dst = ((p_out, out1), (out1, out2))[s]
            return half_copy(
                src.at[i], dst.at[i], masks[s + 1], dst.shape[1], out_send.at[s, i], out_recv.at[s, i]
            )

        ft = p_in.shape[2] // 2
        hidden = g_in.shape[1] // 2

        def in_done(i, s):
            masks = stages[i * 2 // slabs_in]
            in_copy(i, s).wait()
            if s == 0:
                half_add(p_in.at[i], in1.at[i], masks[1], in1.shape[1])
                in_copy(i, 1).start()
            else:
                for part in range(2):
                    cols = slice(part * ft, (part + 1) * ft)
                    to = slice(part * hidden + i * ft, part * hidden + (i + 1) * ft)
                    half_add(in1.at[i, :, cols], in2.at[i, :, cols], masks[2], in2.shape[1], g_in.at[:, to])

        def out_done(i, s):
            masks = stages[i % 2]
            out_copy(i, s).wait()
            if s == 0:
                half_add(p_out.at[i], out1.at[i], masks[1], out1.shape[1])
                out_copy(i, 1).start()
            else:
                wide = out2.shape[2]
                half_add(out1.at[i], out2.at[i], masks[2], out2.shape[1], g_out.at[:, i * wide : (i + 1) * wide])

        for i in range(slabs_in):
            in_copy(i, 0).start()
        for i in range(slabs_out):
            out_copy(i, 0).start()
        for s in range(2):
            for i in range(slabs_in // 2):
                halves.append((in_done, i, s))
                halves.append((in_done, slabs_in // 2 + i, s))
            for i in range(slabs_out):
                halves.append((out_done, i, s))

    def tick(n):
        for _ in range(min(n, len(halves))):
            f, i, s = halves.pop(0)
            f(i, s)

    total = lax.axis_size("dp") * lax.axis_size("expert") if plan else 0

    def slab_store(dst, s, value, cols):
        size = value.shape[0] // total
        low = order[-1]
        bits = [m * (1 if a == "expert" else lax.axis_size("expert")) for a, m in order]
        for j in range(total):
            if (j // bits[-1]) % 2:
                continue
            at = place_of(j, bits[:-1]) * 2 * size
            other = j + bits[-1]
            both = jnp.concatenate(
                [value[j * size : (j + 1) * size], value[other * size : (other + 1) * size]], axis=0
            )
            dst[s, at : at + 2 * size, cols] = both.astype(BF16)

    def slab_copy(src, bufs, s, stage, base):
        if stage < 4:
            return half_copy(
                (src if stage == 0 else bufs[stage - 1]).at[s], bufs[stage].at[s], order[stage],
                bufs[stage].shape[1], q_send.at[base + s, stage], q_recv.at[base + s, stage],
            )
        wide = src.shape[2]
        return half_copy(
            g_last.at[base + s, :, 0:wide], r_last.at[base + s, :, 0:wide], order[4],
            r_last.shape[1], q_send.at[base + s, 4], q_recv.at[base + s, 4],
        )

    def slab_done(src, bufs, s, stage, base):
        slab_copy(src, bufs, s, stage, base).wait()
        if stage < 4:
            before = (src if stage == 0 else bufs[stage - 1]).at[s]
            wide = src.shape[2]
            into = g_last.at[base + s, :, 0:wide] if stage == 3 else None
            half_add(before, bufs[stage].at[s], order[stage], bufs[stage].shape[1], into)
            slab_copy(src, bufs, s, stage + 1, base).start()
        else:
            wide = src.shape[2]
            half_add(
                g_last.at[base + s, :, 0:wide], r_last.at[base + s, :, 0:wide], order[4], r_last.shape[1],
                fin.at[base + s, :, 0:wide],
            )

    wcat[...] = jnp.zeros_like(wcat)
    wcat[0:8] = wrT[...]
    wcat[8:12] = cmT[...]
    for kk in range(2):
        rb[kk] = jnp.transpose(jnp.broadcast_to(rT[kk : kk + 1, :].astype(F32), (128, length)))

    @pl.loop(0, length // 256)
    def _(i):
        rows = tile(i, 256)
        s_id = lax.broadcasted_iota(jnp.int32, (256, slots), 1).astype(F32)
        first = (meta[rows, 0:1] == s_id).astype(F32).astype(BF16)
        second = (meta[rows, 1:2] == s_id).astype(F32).astype(BF16)
        fk0[rows] = dot(first, f_back[...].reshape(slots, width))
        fk1[rows] = dot(second, f_back[...].reshape(slots, width))
        dsn[rows] = dot(first + second, d_back[...].reshape(slots, width))

    w_high = wcat[...].astype(BF16)
    lnacc[...] = jnp.zeros_like(lnacc)

    @pl.loop(0, length // 64)
    def _(i):
        rows = tile(i, 64)
        lane = lax.broadcasted_iota(jnp.int32, (64, 128), 1)
        lane_f = lane.astype(F32)
        m = meta[rows]
        g0, g1, keep = m[:, 2:3], m[:, 3:4], m[:, 4:5]
        cg = (m[:, 5:6], m[:, 6:7])
        shares = ((m[:, 7:8], m[:, 8:9]), (m[:, 9:10], m[:, 10:11]))
        g = cot[rows].astype(F32)
        x = res[rows]
        r2 = lax.rsqrt(row_mean(x * x) + EPS)
        xr = x * r2
        n2 = xr * ln2[...]
        n2b[rows] = n2.astype(BF16)
        f0, f1 = fk0[rows], fk1[rows]
        cv = (cvT[0:1, :], cvT[1:2, :])
        out[rows] = (
            x + g0 * f0 + g1 * f1 + keep * n2 + (cg[0] * shares[0][1]) * cv[0] + (cg[1] * shares[1][1]) * cv[1]
        ).astype(BF16)
        gn2 = jnp.sum(g * n2, axis=-1, keepdims=True)
        gcv = [jnp.sum(g * c, axis=-1, keepdims=True) for c in cv]
        hits = [(rb[kk, rows] == lane_f).astype(F32) for kk in range(2)]
        special = jnp.where(lane == 5, gn2, 0.0)
        for j in range(2):
            special = jnp.where(lane == 6 + j, shares[j][0] * gn2 + shares[j][1] * gcv[j], special)
        dg = [
            jnp.sum(g * f, axis=-1, keepdims=True) + jnp.sum(h * special, axis=-1, keepdims=True)
            for f, h in zip((f0, f1), hits)
        ]
        mean_dg = g0 * dg[0] + g1 * dg[1]
        dc0, dc1 = g0 * (dg[0] - mean_dg), g1 * (dg[1] - mean_dg)
        cat = hits[0] * dc0 + hits[1] * dc1
        for j in range(2):
            dm0, dm1 = cg[j] * gn2, cg[j] * gcv[j]
            mean_dm = shares[j][0] * dm0 + shares[j][1] * dm1
            cat = jnp.where(lane == 8 + 2 * j, shares[j][0] * (dm0 - mean_dm), cat)
            cat = jnp.where(lane == 9 + 2 * j, shares[j][1] * (dm1 - mean_dm), cat)
        dcat[rows, 0:128] = cat.astype(BF16)
        vecs = jnp.where(lane == 12, cg[0] * shares[0][1], 0.0)
        vecs = jnp.where(lane == 13, cg[1] * shares[1][1], vecs)
        dcat[rows, 128:256] = vecs.astype(BF16)
        dn2 = keep * g + dsn[rows] + dot(cat.astype(BF16), w_high)
        lnacc[0:8] += jnp.sum((dn2 * xr).reshape(8, 8, width), axis=0)
        dn = dn2 * ln2[...]
        dr = g + r2 * dn - xr * (r2 * r2) * row_mean(dn * x)
        dres[rows] = dr
        dbr[rows] = dr.astype(BF16)

    tick(6)

    @pl.loop(0, width // 256)
    def _(j):
        cols = tile(j, 256)
        datt[:, cols] = dot_nt(dbr[...], wattn[cols, :]).astype(BF16)

    for j in range(width // 256):
        cols = slice(j * 256, (j + 1) * 256)
        d = dot_tn(att[...], dbr[:, cols])
        if plan:
            slab_store(ga, 0, d, cols)
        else:
            d_attn[:, cols] = d
    tick(4)

    for part in range(3):

        @pl.loop(2 * part, 2 * part + 2)
        def _(j):
            cols = tile(j, 128)
            dkv[...] = jnp.zeros_like(dkv)
            for b in range(2):
                rows = slice(b * block, (b + 1) * block)
                nk = (b + 1) * block
                qlane = lax.broadcasted_iota(jnp.int32, (block, 128), 1)
                klane = lax.broadcasted_iota(jnp.int32, (nk, 128), 1)
                do = datt[rows, cols]
                prod = do.astype(F32) * att[rows, cols].astype(F32)
                dq = jnp.zeros((block, 128), F32)
                for h in range(2):
                    delta = jnp.sum(half_mask(prod, qlane, h), axis=-1, keepdims=True)
                    dom = half_mask(do, qlane, h)
                    dp = dot_nt(dom, v[0:nk, cols])
                    w = pw[2 * j + h, rows, 0:nk]
                    ds = (w.astype(F32) * (dp - delta)).astype(BF16)
                    dq = dq + dot(ds, half_mask(k[0:nk, cols], klane, h))
                    dkv[0, 0:nk] += dot_tn(ds, half_mask(q[rows, cols], qlane, h))
                    dkv[1, 0:nk] += dot_tn(w, dom)
                dproj[rows, cols] = rotate(dq * 0.125, cos[rows], -sin[rows]).astype(BF16)
            dproj[:, pl.ds(pl.multiple_of(width + j * 128, 128), 128)] = rotate(dkv[0], cos[...], -sin[...]).astype(BF16)
            dproj[:, pl.ds(pl.multiple_of(2 * width + j * 128, 128), 128)] = dkv[1].astype(BF16)

        for kind in range(3):
            cols = slice(kind * width + part * 256, kind * width + part * 256 + 256)
            d = dot_tn(n1[...], dproj[:, cols])
            if plan:
                slab_store(gq, part, d, slice(kind * 256, kind * 256 + 256))
            else:
                d_qkv[:, cols] = d
        if plan:
            slab_copy(gq, gq_recv, part, 0, 0).start()
            for stage in range(part):
                slab_done(gq, gq_recv, part - 1 - stage, stage, 0)
        tick(3)

    @pl.loop(0, width // 256)
    def _(j):
        cols = tile(j, 256)
        fk0[:, cols] = dot_nt(dproj[...], wqkv[cols, :])

    @pl.loop(0, length // 64)
    def _(i):
        rows = tile(i, 64)
        x = tok[rows].astype(F32)
        r1 = lax.rsqrt(row_mean(x * x) + EPS)
        xr = x * r1
        d = fk0[rows]
        dn = d * ln1[...]
        lnacc[8:16] += jnp.sum((d * xr).reshape(8, 8, width), axis=0)
        igrad[rows] = (dres[rows] + r1 * dn - xr * (r1 * r1) * row_mean(dn * x)).astype(BF16)

    ln = jnp.zeros((128, width), F32)
    row = lax.broadcasted_iota(jnp.int32, (128, width), 0)
    ln = jnp.where(row == 14, jnp.sum(lnacc[8:16], axis=0, keepdims=True), ln)
    ln = jnp.where(row == 15, jnp.sum(lnacc[0:8], axis=0, keepdims=True), ln)
    small = dot_tn(n2b[...], dcat[:, 0:128]) + dot_tn(cot[...], dcat[:, 128:256]) + jnp.transpose(ln)
    if not plan:
        d_small[...] = small
        return
    slab_store(ga, 0, small, slice(width, width + 128))
    slab_copy(ga, ga_recv, 0, 0, 3).start()
    live = [(gq, gq_recv, 0, 2, 0), (gq, gq_recv, 1, 1, 0), (gq, gq_recv, 2, 0, 0), (ga, ga_recv, 0, 0, 3)]
    while live:
        for src, bufs, s, stage, base in live:
            slab_done(src, bufs, s, stage, base)
        live = [(a, b, s, stage + 1, base) for a, b, s, stage, base in live if stage < 4]
        tick(4)
    tick(100)
    for s in range(3):
        for kind in range(3):
            at = kind * width + s * 256
            d_qkv[:, at : at + 256] = fin[s, :, kind * 256 : kind * 256 + 256]
    d_attn[...] = fin[3, :, 0:width]
    d_small[...] = fin[3, :, width : width + 128]


def shape(*s, dtype=BF16):
    return jax.ShapeDtypeStruct(s, dtype)


def call(kernel, outs, scratch, args, name, collective_id):
    return pl.pallas_call(
        kernel,
        out_shape=outs,
        in_specs=[pl.BlockSpec(memory_space=pltpu.VMEM)] * len(args),
        out_specs=[pl.BlockSpec(memory_space=pltpu.VMEM)] * len(outs),
        scratch_shapes=scratch,
        compiler_params=pltpu.CompilerParams(
            vmem_limit_bytes=VMEM_LIMIT, has_side_effects=True, collective_id=collective_id
        ),
        name=name,
    )(*args)


def body(
    tokens, segments, routes, prev_logits, ln1_gain, w_qkv, w_attn, ln2_gain, w_router, const_mix, const_vec,
    expert_in, expert_out, cotangent,
):
    length, width = tokens.shape
    heads = width // HEAD_DIM
    experts = lax.axis_size("expert") * expert_in.shape[0]
    hidden = expert_out.shape[1]
    capacity = length // 2
    slots = experts * capacity
    n_dp = lax.axis_size("dp")
    V = pltpu.VMEM
    DMA = pltpu.SemaphoreType.DMA
    cos, sin = (jnp.asarray(t) for t in rotary_tables(length))
    rT, pT = routes.T, prev_logits.T
    wrT, cmT, cvT = w_router.T, const_mix.T, const_vec.T
    ln1, ln2 = ln1_gain.reshape(1, width), ln2_gain.reshape(1, width)
    peers = experts - 1

    q, k, v, pw, att, n1, res, meta, send, g_rows = call(
        fwd_kernel,
        [
            shape(length, width), shape(length, width), shape(length, width), shape(heads, length, length),
            shape(length, width), shape(length, width), shape(length, width, dtype=F32),
            shape(length, 128, dtype=F32), shape(experts, capacity, width + 128), shape(experts, capacity, width),
        ],
        [
            V((length, 256), F32), V((length, length), F32), V((128, width), F32), V((3, length, 128), F32),
            V((128, length), F32), V((length, width), BF16), V((length, width), BF16), V((2 * length, 128), BF16),
            V((length, 128), F32), V((slots, length), BF16), V((experts, capacity, width), BF16),
            DMA((peers,)), DMA((peers,)),
        ],
        (tokens, segments, rT, pT, ln1, w_qkv, w_attn, ln2, wrT, cmT, cotangent, cos, sin),
        "attention", 0,
    )

    tiles, slabs = 8, 3
    ft = hidden // tiles
    within = n_dp == tiles and experts == 4
    stages = ((("dp", 1), ("dp", 2), ("dp", 4)), (("dp", 2), ("dp", 1), ("dp", 4))) if within else ()
    order = (("expert", 1), ("expert", 2), ("dp", 1), ("dp", 2), ("dp", 4))
    slab_in, slab_out = (tiles, width, 2 * ft), (slabs, hidden, width // slabs)
    back = [shape(experts, capacity, width)] * 2

    def part_of(s, n):
        return (s[0], s[1] // n, s[2])

    in_half, out_half = part_of(slab_in, 2), part_of(slab_out, 2)
    f_back, d_back, g_in, g_out = call(
        functools.partial(expert_kernel, stages),
        back + ([shape(*in_half), shape(*out_half)] if within else [shape(*slab_in), shape(*slab_out)]),
        [
            V((experts, capacity, width + 128), BF16), V((experts, capacity, width), BF16), V((tiles, slots, ft), BF16),
            V((tiles, slots, ft), BF16), V((tiles, slots, ft), BF16), V((slots, 2 * ft), BF16),
            V((experts, capacity, width), F32), V((2, experts, capacity, width), BF16),
        ]
        + ([V(slab_in, BF16), V(slab_out, BF16)] + [DMA((tiles,))] * 2 + [DMA((slabs,))] * 2 if within else [])
        + [DMA((peers,))] * 6,
        (send, g_rows, expert_in, expert_out),
        "experts", 1,
    )

    args = (
        tokens, cotangent, res, meta, rT, f_back, d_back, q, k, v, pw, att, n1, ln1, w_qkv, w_attn, ln2, wrT, cmT, cvT,
        cos, sin,
    )
    n_all = n_dp * experts
    rows = width // n_all if within else width
    outs = [
        shape(length, width), shape(length, width), shape(rows, 3 * width, dtype=F32), shape(rows, width, dtype=F32),
        shape(rows, 128, dtype=F32),
    ]
    scratch = [
        V((128, width), F32), V((2, length, 128), F32), V((length, width), F32), V((length, width), F32),
        V((length, width), F32), V((length, 256), BF16), V((length, width), BF16), V((length, width), F32),
        V((length, width), BF16), V((length, 3 * width), BF16), V((length, width), BF16),
        V((2, length, 128), F32), V((16, width), F32),
    ]
    if within:
        args += (g_in, g_out)
        outs += [shape(width // n_dp, 2 * hidden, dtype=F32), shape(hidden // n_dp, width, dtype=F32)]
        wide = width + 128
        scratch += [
            V(part_of(slab_in, 4), BF16), V(part_of(slab_in, 8), BF16), V(part_of(slab_out, 4), BF16),
            V(part_of(slab_out, 8), BF16), DMA((2, tiles)), DMA((2, tiles)), DMA((2, slabs)), DMA((2, slabs)),
            V((3, width, width), BF16), V((1, width, wide), BF16),
        ]
        scratch += [V((3, width >> s, width), BF16) for s in range(1, 5)]
        scratch += [V((1, width >> s, wide), BF16) for s in range(1, 5)]
        scratch += [
            V((4, 2 * rows, wide), F32), V((4, rows, wide), F32), V((4, rows, wide), F32), DMA((4, 5)), DMA((4, 5)),
        ]
    plan = (stages, order) if within else ()
    done = call(functools.partial(bwd_kernel, plan), outs, scratch, args, "backward", 2 if within else None)
    out, igrad, d_qkv, d_attn, small = done[:5]
    if within:
        g_in, g_out = done[5:]
    else:
        g_in = jnp.moveaxis(g_in.reshape(tiles, width, 2, ft), 0, 2).reshape(width, 2 * hidden)
        g_out = jnp.moveaxis(g_out, 0, 1).reshape(hidden, width)
        g_in = lax.psum_scatter(g_in, "dp", scatter_dimension=0, tiled=True).astype(F32)
        g_out = lax.psum_scatter(g_out, "dp", scatter_dimension=0, tiled=True).astype(F32)
        d_qkv, d_attn, small = (
            lax.psum_scatter(d, ("dp", "expert"), scatter_dimension=0, tiled=True) for d in (d_qkv, d_attn, small)
        )
    return (
        out, igrad, small[:, 14], d_qkv, d_attn, small[:, 15], small[:, 0:8], small[:, 8:12], small[:, 12:14],
        g_in[None], g_out[None],
    )


def solution(mesh):
    rows = P(("dp", "expert"), None)
    return jax.shard_map(
        body,
        mesh=mesh,
        in_specs=(
            rows, rows, rows, rows, P(), P(), P(), P(), P(), P(), P(),
            P("expert", None, None), P("expert", None, None), rows,
        ),
        out_specs=(
            rows, rows, P(("dp", "expert")), rows, rows, P(("dp", "expert")), rows, rows, rows,
            P("expert", "dp", None), P("expert", "dp", None),
        ),
        check_vma=False,
    )
```

```python
import functools
import math

import jax
import jax.numpy as jnp
import numpy as np
from jax import lax
from jax.experimental import pallas as pl
from jax.experimental.pallas import tpu as pltpu
from jax.sharding import PartitionSpec as P

HEAD_DIM = 64
EPS = 1e-06
MASKED = -1e30
F32 = jnp.float32
BF16 = jnp.bfloat16
VMEM_LIMIT = 62 * 1024 * 1024


def dot(a, b):
    return lax.dot_general(a, b, (((1,), (0,)), ((), ())), preferred_element_type=F32)


def dot_nt(a, b):
    return lax.dot_general(a, b, (((1,), (1,)), ((), ())), preferred_element_type=F32)


def dot_tn(a, b):
    return lax.dot_general(a, b, (((0,), (0,)), ((), ())), preferred_element_type=F32)


def tile(i, size):
    return pl.ds(pl.multiple_of(i * size, size), size)


def rotary_tables(length):
    half = HEAD_DIM // 2
    inverse = np.exp(np.arange(half, dtype=np.float32) * np.float32(-2.0 * math.log(10000.0) / HEAD_DIM))
    angles = np.arange(length, dtype=np.float32)[:, None] * inverse.astype(np.float32)[None, :]
    cos, sin = np.cos(angles), np.sin(angles)
    return (
        np.concatenate([cos] * 4, axis=1).astype(np.float32),
        np.concatenate([-sin, sin] * 2, axis=1).astype(np.float32),
    )


def rotate(x, cos, sin):
    lane = lax.broadcasted_iota(jnp.int32, x.shape, 1)
    front = (lane % HEAD_DIM) < HEAD_DIM // 2
    other = jnp.where(front, pltpu.roll(x, 96, 1), pltpu.roll(x, 32, 1))
    return x * cos + other * sin


def row_mean(x):
    return jnp.mean(x, axis=-1, keepdims=True)


def pick(x, lane, index):
    return jnp.sum(jnp.where(lane == index, x, 0.0), axis=-1, keepdims=True)


def half_mask(x, lane, which):
    keep = (lane < HEAD_DIM) if which == 0 else (lane >= HEAD_DIM)
    return jnp.where(keep, x, jnp.zeros_like(x))


MESH = pl.DeviceIdType.MESH


def flip(i, m):
    return i + m * (1 - 2 * ((i // m) % 2))


def side(mask):
    axis, m = mask
    return (lax.axis_index(axis) // m) % 2


def partner(mask):
    axis, m = mask
    return {axis: flip(lax.axis_index(axis), m)}


def across(r):
    e = lax.axis_index("expert")
    for m in (1, 2):
        if r & m:
            e = flip(e, m)
    return e


def greet(masks, peers=0):
    barrier = pltpu.get_barrier_semaphore()
    for mask in masks:
        pl.semaphore_signal(barrier, inc=1, device_id=partner(mask), device_id_type=MESH)
    for r in range(1, peers + 1):
        pl.semaphore_signal(barrier, inc=1, device_id={"expert": across(r)}, device_id_type=MESH)
    pl.semaphore_wait(barrier, len(masks) + peers)


def exchange(src, dst, send_sem, recv_sem):
    return {
        r: pltpu.make_async_remote_copy(
            src.at[r], dst.at[r], send_sem.at[r - 1], recv_sem.at[r - 1],
            device_id={"expert": across(r)}, device_id_type=MESH,
        )
        for r in range(src.shape[0] - 1, 0, -1)
    }


def half_copy(src, dst, mask, rows, send_sem, recv_sem):
    start = pl.multiple_of((1 - side(mask)) * rows, 8)
    return pltpu.make_async_remote_copy(
        src.at[pl.ds(start, rows)], dst, send_sem, recv_sem, device_id=partner(mask), device_id_type=MESH
    )


def half_add(src, dst, mask, rows, out=None):
    start = side(mask) * rows
    step = 48 if rows % 48 == 0 else 64 if rows % 64 == 0 else 24
    out = dst if out is None else out

    @pl.loop(0, rows // step)
    def _(i):
        here = pl.ds(pl.multiple_of(i * step, 8), step)
        mine = src[pl.ds(pl.multiple_of(start + i * step, 8), step)].astype(F32)
        out[here] = (mine + dst[here].astype(F32)).astype(out.dtype)


def place_of(shard, masks):
    place = 0
    for m in masks:
        place = 2 * place + (shard // m) % 2
    return place


def fwd_kernel(
    tok, seg, rT, pT, ln1, wqkv, wattn, ln2, wrT, cmT, cot, cos, sin,
    q, k, v, pw, att, n1, res, meta, send, g_rows,
    proj, bias, wcat, rb, pb, n2b, n2l, gl, tg, onehot, g_out, send_sem, recv_sem,
):
    length, width = tok.shape
    capacity = length // 2
    experts = send.shape[0]

    greet((), experts - 1)
    for kk in range(2):
        rb[kk] = jnp.transpose(jnp.broadcast_to(rT[kk : kk + 1, :].astype(F32), (128, length)))
    all_lane = lax.broadcasted_iota(jnp.int32, (length, 128), 1).astype(F32)
    count = ((rb[0] == all_lane).astype(F32) + (rb[1] == all_lane).astype(F32)).astype(BF16)

    @pl.loop(0, length // 128)
    def _(i):
        rows = tile(i, 128)
        lane = lax.broadcasted_iota(jnp.int32, (128, 128), 1)
        lane_f = lane.astype(F32)
        t_id = lax.broadcasted_iota(jnp.int32, (128, length), 0) + i * 128
        before = (t_id > lax.broadcasted_iota(jnp.int32, (128, length), 1)).astype(F32).astype(BF16)
        place = dot(before, count) + lane_f * float(capacity) + 1.0
        out = jnp.zeros((128, 128), F32)
        for kk in range(2):
            hit = (rb[kk, rows] == lane_f) & (lane < experts)
            out = jnp.where(lane == kk, jnp.sum(jnp.where(hit, place, 0.0), axis=-1, keepdims=True) - 1.0, out)
        tg[rows] = out

    target = jnp.transpose(tg[...])
    pb[...] = target

    copies = exchange(g_out, g_rows, send_sem, recv_sem)
    for r in range(experts - 1, -1, -1):
        s_id = (lax.broadcasted_iota(jnp.int32, (capacity, length), 0) + across(r) * capacity).astype(F32)
        here = (pb[0:1] == s_id).astype(F32) + (pb[1:2] == s_id).astype(F32)
        onehot[r * capacity : (r + 1) * capacity] = here.astype(BF16)
        rows_r = dot(here.astype(BF16), cot[...]).astype(BF16)
        if r:
            g_out[r] = rows_r
            copies[r].start()
        else:
            g_rows[0] = rows_r

    @pl.loop(0, length // 64)
    def _(i):
        rows = tile(i, 64)
        x = tok[rows].astype(F32)
        r = lax.rsqrt(row_mean(x * x) + EPS)
        n1[rows] = (x * r * ln1[...]).astype(BF16)

    for kind, dst in enumerate((q, k, v)):

        @pl.loop(0, width // 256)
        def _(j):
            cols = pl.ds(pl.multiple_of(kind * width + j * 256, 256), 256)
            proj[...] = dot(n1[...], wqkv[:, cols])

            @pl.loop(0, length // 128)
            def _(i):
                rows = tile(i, 128)
                for part in range(2):
                    x = proj[rows, part * 128 : part * 128 + 128]
                    if kind < 2:
                        x = rotate(x, cos[rows], sin[rows])
                    if kind == 0:
                        x = x * 0.125
                    dst[rows, pl.ds(pl.multiple_of(j * 256 + part * 128, 128), 128)] = x.astype(BF16)

    seg_f = seg[...].astype(F32)
    rb[2] = jnp.transpose(jnp.broadcast_to(seg_f, (128, length)))

    @pl.loop(0, length // 128)
    def _(i):
        rows = tile(i, 128)
        row_id = lax.broadcasted_iota(jnp.int32, (128, length), 0) + i * 128
        col_id = lax.broadcasted_iota(jnp.int32, (128, length), 1)
        same = rb[2, rows, 0:1] == seg_f
        bias[rows] = jnp.where(same & (row_id >= col_id), 0.0, MASKED)

    block = length // 2

    @pl.loop(0, width // 128)
    def _(j):
        cols = tile(j, 128)
        for b in range(2):
            rows = slice(b * block, (b + 1) * block)
            nk = (b + 1) * block
            qlane = lax.broadcasted_iota(jnp.int32, (block, 128), 1)
            klane = lax.broadcasted_iota(jnp.int32, (nk, 128), 1)
            acc = jnp.zeros((block, 128), F32)
            for h in range(2):
                s = dot_nt(half_mask(q[rows, cols], qlane, h), k[0:nk, cols]) + bias[rows, 0:nk]
                m = jnp.max(s, axis=-1, keepdims=True)
                e = jnp.exp(s - m)
                w = (e * (1.0 / jnp.sum(e, axis=-1, keepdims=True))).astype(BF16)
                pw[2 * j + h, rows, 0:nk] = w
                acc = acc + dot(w, half_mask(v[0:nk, cols], klane, h))
            att[rows, cols] = acc.astype(BF16)

    @pl.loop(0, width // 256)
    def _(j):
        cols = tile(j, 256)
        res[:, cols] = tok[:, cols].astype(F32) + dot(att[...], wattn[:, cols])

    @pl.loop(0, length // 64)
    def _(i):
        rows = tile(i, 64)
        x = res[rows]
        n2 = x * lax.rsqrt(row_mean(x * x) + EPS) * ln2[...]
        high = n2.astype(BF16)
        n2b[rows] = high
        n2l[rows] = (n2 - high.astype(F32)).astype(BF16)

    wcat[...] = jnp.zeros_like(wcat)
    wcat[0:8] = wrT[...]
    wcat[8:12] = cmT[...]
    w_high = wcat[...].astype(BF16)
    w_low = (wcat[...] - w_high.astype(F32)).astype(BF16)

    pb[8:16] = pT[...]
    rb[2] = jnp.transpose(jnp.concatenate([pb[8:16], jnp.zeros((120, length), F32)], axis=0))

    @pl.loop(0, length // 128)
    def _(i):
        rows = tile(i, 128)
        lane = lax.broadcasted_iota(jnp.int32, (128, 128), 1)
        lane_f = lane.astype(F32)
        high = n2b[rows]
        mixed = dot_nt(high, w_high) + dot_nt(high, w_low) + dot_nt(n2l[rows], w_high)
        logits = mixed + rb[2, rows]
        hits = [(rb[kk, rows] == lane_f).astype(F32) for kk in range(2)]
        chosen = [jnp.sum(h * logits, axis=-1, keepdims=True) for h in hits]
        top = jnp.maximum(chosen[0], chosen[1])
        e = [jnp.exp(c - top) for c in chosen]
        inv = 1.0 / (e[0] + e[1])
        gates = [v_ * inv for v_ in e]
        shares = []
        for j in range(2):
            a0, a1 = pick(mixed, lane, 8 + 2 * j), pick(mixed, lane, 9 + 2 * j)
            mx = jnp.maximum(a0, a1)
            b0, b1 = jnp.exp(a0 - mx), jnp.exp(a1 - mx)
            binv = 1.0 / (b0 + b1)
            shares.append((b0 * binv, b1 * binv))
        gate_sum = gates[0] * hits[0] + gates[1] * hits[1]
        cg = [pick(gate_sum, lane, 6), pick(gate_sum, lane, 7)]
        keep = pick(gate_sum, lane, 5) + cg[0] * shares[0][0] + cg[1] * shares[1][0]
        values = (
            gates[0], gates[1], keep, cg[0], cg[1], shares[0][0], shares[0][1], shares[1][0], shares[1][1],
        )
        out = tg[rows]
        for n, value in enumerate(values):
            out = jnp.where(lane == n + 2, value, out)
        meta[rows] = out
        for kk in range(2):
            g_high = gates[kk].astype(BF16).astype(F32)
            both = jnp.where(lane == 0, g_high, jnp.where(lane == 1, gates[kk] - g_high, 0.0))
            gl[pl.ds(pl.multiple_of(kk * length + i * 128, 128), 128)] = both.astype(BF16)

    @pl.loop(0, experts)
    def _(e):
        owner = flip(lax.axis_index("expert"), 1)
        owner = jnp.where(e % 2 == 1, owner, lax.axis_index("expert"))
        owner = jnp.where(e // 2 == 1, flip(owner, 2), owner)
        s_id = (lax.broadcasted_iota(jnp.int32, (capacity, length), 0) + owner * capacity).astype(F32)
        gate = jnp.zeros((capacity, 128), F32)
        for kk in range(2):
            here = (pb[kk : kk + 1] == s_id).astype(F32).astype(BF16)
            gate = gate + dot(here, gl[kk * length : (kk + 1) * length])
        send[e, :, 0:width] = dot(onehot[tile(e, capacity)], n2b[...]).astype(BF16)
        send[e, :, width : width + 128] = gate.astype(BF16)

    for c in copies.values():
        c.wait()


def expert_kernel(stages, xs, g_rows, win, wout, *refs):
    f_rows, d_back, go = refs[:3]
    if stages:
        p_in = refs[3]
    else:
        gi = refs[3]
    xr, dy, hid, dgu, f_acc, d_acc, d_out = refs[4:11]
    refs = refs[11:]
    if stages:
        gi, in_send, in_recv = refs[:3]
        refs = refs[3:]
    x_send, x_recv, d_send, d_recv = refs
    groups, capacity, wide = xs.shape
    hidden, width = wout.shape[1:]
    tiles, rows_all, ft = hid.shape
    slabs = go.shape[0]
    shards = 2 ** len(stages[0]) if stages else 0
    near = rows_all // 2

    greet([s[0] for s in stages], groups - 1)
    copies = exchange(xs, xr, x_send, x_recv)
    for c in copies.values():
        c.start()
    xr[0] = xs[0]

    def gated(r):
        pair = xr[r, :, width:wide].astype(F32)
        lane = lax.broadcasted_iota(jnp.int32, pair.shape, 1)
        gate = jnp.sum(jnp.where(lane < 2, pair, 0.0), axis=-1, keepdims=True)
        dy[r * capacity : (r + 1) * capacity] = (g_rows[r].astype(F32) * gate).astype(BF16)

    def cols_of(f):
        return tile(f, ft), pl.ds(pl.multiple_of(hidden + f * ft, ft), ft)

    def work(f, part):
        gate_cols, up_cols = cols_of(f)
        rows = slice(part * near, (part + 1) * near)
        x = xr[2 * part : 2 * part + 2, :, 0:width].reshape(near, width)
        gate = dot(x, win[0, :, gate_cols])
        up = dot(x, win[0, :, up_cols])
        dh = dot_nt(dy[rows], wout[0, gate_cols, :])
        sig = 1.0 / (1.0 + jnp.exp(-gate))
        silu = gate * sig
        h = (silu * up).astype(BF16)
        da = (dh * up * (sig + silu * (1.0 - sig))).astype(BF16)
        db = (dh * silu).astype(BF16)
        hid[f, rows] = h
        dgu[f, rows, 0:ft] = da
        dgu[f, rows, ft : 2 * ft] = db
        y = dot(h, wout[0, gate_cols, :])
        d = dot_nt(da, win[0, :, gate_cols]) + dot_nt(db, win[0, :, up_cols])

        @pl.when(f == 0)
        def _():
            f_acc[rows] = y
            d_acc[rows] = d

        @pl.when(f > 0)
        def _():
            f_acc[rows] += y
            d_acc[rows] += d

    def in_copy(slab, p):
        return half_copy(
            gi.at[slab], p_in.at[slab], stages[p][0], width // 2, in_send.at[slab], in_recv.at[slab]
        )

    copies[1].wait()
    gated(0)
    gated(1)

    @pl.loop(0, tiles)
    def _(f):
        work(f, 0)

    copies[3].wait()
    copies[2].wait()
    gated(2)
    gated(3)

    @pl.loop(0, tiles)
    def _(f):
        work(f, 1)
        for p in range(2):
            d = dot_tn(xr[:, :, 0:width].reshape(rows_all, width), dgu[f, :, p * ft : (p + 1) * ft])
            if not stages:
                gi[2 * f + p] = d.astype(BF16)
                continue
            size = width // shards
            for j in range(shards):
                at = place_of(j, [m for _, m in stages[p]]) * size
                gi[2 * f + p, at : at + size] = d[j * size : (j + 1) * size].astype(BF16)
            in_copy(2 * f + p, p).start()

    d_copies = exchange(d_out, d_back, d_send, d_recv)
    for r in range(groups - 1, -1, -1):
        rows = slice(r * capacity, (r + 1) * capacity)
        y = f_acc[rows]
        f_rows[r] = y.astype(BF16)
        dots = jnp.sum(y * g_rows[r].astype(F32), axis=-1, keepdims=True)
        high = dots.astype(BF16).astype(F32)
        lane = lax.broadcasted_iota(jnp.int32, (capacity, 128), 1)
        extra = jnp.where(lane == 0, high, jnp.where(lane == 1, dots - high, 0.0)).astype(BF16)
        dst = d_out if r else d_back
        dst[r, :, 0:width] = d_acc[rows].astype(BF16)
        dst[r, :, width:wide] = extra
        if r:
            d_copies[r].start()

    for c in range(slabs):
        cols = slice(c * (width // slabs), (c + 1) * (width // slabs))

        @pl.loop(0, tiles)
        def _(t):
            d = dot_tn(hid[t], dy[:, cols]).astype(BF16)
            if not stages:
                go[c, tile(t, ft)] = d
                return
            size = hidden // shards
            for i in range(ft // size):
                at = place_of(t * (ft // size) + i, [m for _, m in stages[0]])
                go[c, tile(at, size)] = d[i * size : (i + 1) * size]

    if stages:

        @pl.loop(0, tiles)
        def _(f):
            for p in range(2):
                in_copy(2 * f + p, p).wait()
                half_add(gi.at[2 * f + p], p_in.at[2 * f + p], stages[p][0], width // 2)

    for c in d_copies.values():
        c.wait()


def bwd_kernel(plan, *refs):
    (
        tok, cot, res, meta, rT, f_rows, d_back, q, k, v, pw, att, n1, ln1, wqkv, wattn, ln2, wrT, cmT, cvT, cos, sin,
    ) = refs[:22]
    refs = refs[22:]
    if plan:
        stages, order = plan
        p_in, p_out, out, igrad, d_qkv, d_attn, d_small, g_in, g_out = refs[:9]
        refs = refs[9:]
    else:
        out, igrad, d_qkv, d_attn, d_small = refs[:5]
        refs = refs[5:]
    wcat, rb, fk0, dsn, dots, dcat, n2b, dres, dbr, dproj, datt, dkv, lnacc, f_back, f_send, f_recv = refs[:16]
    refs = refs[16:]
    length, width = tok.shape
    experts, capacity, _ = f_rows.shape
    slots = experts * capacity
    block = length // 2

    greet(order[2:] if plan else (), experts - 1)
    f_copies = exchange(f_rows, f_back, f_send, f_recv)

    events = []
    if plan:
        in1, in2, out0, out1, out2, in_send, in_recv, out_send, out_recv, gq, ga = refs[:11]
        gq_recv, ga_recv, g_last, r_last, fin, q_send, q_recv = (
            refs[11:15], refs[15:19], refs[19], refs[20], refs[21], refs[22], refs[23],
        )
        slabs_in, slabs_out = p_in.shape[0], p_out.shape[0]
        ft = p_in.shape[2]
        hidden = g_in.shape[1] // 2

        def in_copy(i, s):
            src, dst = ((p_in, in1), (in1, in2))[s]
            return half_copy(
                src.at[i], dst.at[i], stages[i % 2][s + 1], dst.shape[1], in_send.at[s, i], in_recv.at[s, i]
            )

        def out_copy(i, s):
            src, dst = ((p_out, out0), (out0, out1), (out1, out2))[s]
            return half_copy(
                src.at[i], dst.at[i], stages[0][s], dst.shape[1], out_send.at[s, i], out_recv.at[s, i]
            )

        def in_done(i, s):
            masks = stages[i % 2]
            in_copy(i, s).wait()
            if s == 0:
                half_add(p_in.at[i], in1.at[i], masks[1], in1.shape[1])
                in_copy(i, 1).start()
            else:
                to = (i % 2) * hidden + (i // 2) * ft
                half_add(in1.at[i], in2.at[i], masks[2], in2.shape[1], g_in.at[:, to : to + ft])

        def out_done(i, s):
            out_copy(i, s).wait()
            src, dst = ((p_out, out0), (out0, out1), (out1, out2))[s]
            if s < 2:
                half_add(src.at[i], dst.at[i], stages[0][s], dst.shape[1])
                out_copy(i, s + 1).start()
            else:
                wide = out2.shape[2]
                half_add(out1.at[i], out2.at[i], stages[0][2], out2.shape[1], g_out.at[:, i * wide : (i + 1) * wide])

        out_copy(0, 0).start()
        for i in range(0, slabs_in, 2):
            in_copy(i, 0).start()

        def odd_start():
            for i in range(1, slabs_in, 2):
                in_copy(i, 0).start()

        def last_start():
            out_copy(1, 0).start()

        events = [
            (in_done, 0, 0), (in_done, 2, 0), (odd_start,),
            (in_done, 4, 0), (in_done, 6, 0), (out_done, 0, 0),
            (last_start,), (in_done, 1, 0), (in_done, 3, 0), (in_done, 0, 1),
            (in_done, 5, 0), (in_done, 7, 0), (in_done, 2, 1), (out_done, 0, 1),
            (in_done, 4, 1), (in_done, 6, 1), (out_done, 1, 0), (in_done, 1, 1), (in_done, 3, 1),
            (in_done, 5, 1), (in_done, 7, 1), (out_done, 0, 2), (out_done, 1, 1), (out_done, 1, 2),
        ]
    for c in f_copies.values():
        c.start()

    def tick(n):
        for _ in range(min(n, len(events))):
            f, *a = events.pop(0)
            f(*a)

    total = lax.axis_size("dp") * lax.axis_size("expert") if plan else 0

    def slab_store(dst, s, value, cols):
        size = value.shape[0] // total
        low = order[-1]
        bits = [m * (1 if a == "expert" else lax.axis_size("expert")) for a, m in order]
        for j in range(total):
            if (j // bits[-1]) % 2:
                continue
            at = place_of(j, bits[:-1]) * 2 * size
            other = j + bits[-1]
            both = jnp.concatenate(
                [value[j * size : (j + 1) * size], value[other * size : (other + 1) * size]], axis=0
            )
            dst[s, at : at + 2 * size, cols] = both.astype(BF16)

    def slab_copy(src, bufs, s, stage, base):
        if stage < 4:
            return half_copy(
                (src if stage == 0 else bufs[stage - 1]).at[s], bufs[stage].at[s], order[stage],
                bufs[stage].shape[1], q_send.at[base + s, stage], q_recv.at[base + s, stage],
            )
        wide = src.shape[2]
        return half_copy(
            g_last.at[base + s, :, 0:wide], r_last.at[base + s, :, 0:wide], order[4],
            r_last.shape[1], q_send.at[base + s, 4], q_recv.at[base + s, 4],
        )

    def slab_done(src, bufs, s, stage, base):
        slab_copy(src, bufs, s, stage, base).wait()
        if stage < 4:
            before = (src if stage == 0 else bufs[stage - 1]).at[s]
            wide = src.shape[2]
            into = g_last.at[base + s, :, 0:wide] if stage == 3 else None
            half_add(before, bufs[stage].at[s], order[stage], bufs[stage].shape[1], into)
            slab_copy(src, bufs, s, stage + 1, base).start()
        else:
            wide = src.shape[2]
            half_add(
                g_last.at[base + s, :, 0:wide], r_last.at[base + s, :, 0:wide], order[4], r_last.shape[1],
                fin.at[base + s, :, 0:wide],
            )

    f_back[0] = f_rows[0]
    wcat[...] = jnp.zeros_like(wcat)
    wcat[0:8] = wrT[...]
    wcat[8:12] = cmT[...]
    for kk in range(2):
        rb[kk] = jnp.transpose(jnp.broadcast_to(rT[kk : kk + 1, :].astype(F32), (128, length)))

    def chosen(rows, wide):
        slot = lax.broadcasted_iota(jnp.int32, (wide, slots), 1)
        r = slot // capacity
        e = jnp.zeros_like(slot)
        for n in range(experts):
            e = jnp.where(r == n, across(n), e)
        s_id = (slot - r * capacity + e * capacity).astype(F32)
        return meta[rows, 0:1] == s_id, meta[rows, 1:2] == s_id

    @pl.loop(0, length // 256)
    def _(i):
        rows = tile(i, 256)
        first, second = (c.astype(F32).astype(BF16) for c in chosen(rows, 256))
        dsn[rows] = dot(first + second, d_back[:, :, 0:width].reshape(slots, width))
        for n, c in enumerate((first, second)):
            dots[n, rows] = dot(c, d_back[:, :, width : width + 128].reshape(slots, 128))

    w_high = wcat[...].astype(BF16)
    lnacc[...] = jnp.zeros_like(lnacc)

    @pl.loop(0, length // 64)
    def _(i):
        rows = tile(i, 64)
        lane = lax.broadcasted_iota(jnp.int32, (64, 128), 1)
        lane_f = lane.astype(F32)
        m = meta[rows]
        g0, g1, keep = m[:, 2:3], m[:, 3:4], m[:, 4:5]
        cg = (m[:, 5:6], m[:, 6:7])
        shares = ((m[:, 7:8], m[:, 8:9]), (m[:, 9:10], m[:, 10:11]))
        g = cot[rows].astype(F32)
        x = res[rows]
        r2 = lax.rsqrt(row_mean(x * x) + EPS)
        xr = x * r2
        n2 = xr * ln2[...]
        n2b[rows] = n2.astype(BF16)
        cv = (cvT[0:1, :], cvT[1:2, :])
        fk0[rows] = x + keep * n2 + (cg[0] * shares[0][1]) * cv[0] + (cg[1] * shares[1][1]) * cv[1]
        gn2 = jnp.sum(g * n2, axis=-1, keepdims=True)
        gcv = [jnp.sum(g * c, axis=-1, keepdims=True) for c in cv]
        hits = [(rb[kk, rows] == lane_f).astype(F32) for kk in range(2)]
        special = jnp.where(lane == 5, gn2, 0.0)
        for j in range(2):
            special = jnp.where(lane == 6 + j, shares[j][0] * gn2 + shares[j][1] * gcv[j], special)
        dg = [
            jnp.sum(h * special + jnp.where(lane < 2, dots[n, rows], 0.0), axis=-1, keepdims=True)
            for n, h in enumerate(hits)
        ]
        mean_dg = g0 * dg[0] + g1 * dg[1]
        dc0, dc1 = g0 * (dg[0] - mean_dg), g1 * (dg[1] - mean_dg)
        cat = hits[0] * dc0 + hits[1] * dc1
        for j in range(2):
            dm0, dm1 = cg[j] * gn2, cg[j] * gcv[j]
            mean_dm = shares[j][0] * dm0 + shares[j][1] * dm1
            cat = jnp.where(lane == 8 + 2 * j, shares[j][0] * (dm0 - mean_dm), cat)
            cat = jnp.where(lane == 9 + 2 * j, shares[j][1] * (dm1 - mean_dm), cat)
        dcat[rows, 0:128] = cat.astype(BF16)
        vecs = jnp.where(lane == 12, cg[0] * shares[0][1], 0.0)
        vecs = jnp.where(lane == 13, cg[1] * shares[1][1], vecs)
        dcat[rows, 128:256] = vecs.astype(BF16)
        dn2 = keep * g + dsn[rows] + dot(cat.astype(BF16), w_high)
        lnacc[0:8] += jnp.sum((dn2 * xr).reshape(8, 8, width), axis=0)
        dn = dn2 * ln2[...]
        dr = g + r2 * dn - xr * (r2 * r2) * row_mean(dn * x)
        dres[rows] = dr
        dbr[rows] = dr.astype(BF16)

    tick(3)

    @pl.loop(0, width // 256)
    def _(j):
        cols = tile(j, 256)
        datt[:, cols] = dot_nt(dbr[...], wattn[cols, :]).astype(BF16)

    for j in range(width // 256):
        cols = slice(j * 256, (j + 1) * 256)
        d = dot_tn(att[...], dbr[:, cols])
        if plan:
            slab_store(ga, 0, d, cols)
        else:
            d_attn[:, cols] = d
    tick(3)

    for part in range(3):

        @pl.loop(2 * part, 2 * part + 2)
        def _(j):
            cols = tile(j, 128)
            dkv[...] = jnp.zeros_like(dkv)
            for b in range(2):
                rows = slice(b * block, (b + 1) * block)
                nk = (b + 1) * block
                qlane = lax.broadcasted_iota(jnp.int32, (block, 128), 1)
                klane = lax.broadcasted_iota(jnp.int32, (nk, 128), 1)
                do = datt[rows, cols]
                prod = do.astype(F32) * att[rows, cols].astype(F32)
                dq = jnp.zeros((block, 128), F32)
                for h in range(2):
                    delta = jnp.sum(half_mask(prod, qlane, h), axis=-1, keepdims=True)
                    dom = half_mask(do, qlane, h)
                    dp = dot_nt(dom, v[0:nk, cols])
                    w = pw[2 * j + h, rows, 0:nk]
                    ds = (w.astype(F32) * (dp - delta)).astype(BF16)
                    dq = dq + dot(ds, half_mask(k[0:nk, cols], klane, h))
                    dkv[0, 0:nk] += dot_tn(ds, half_mask(q[rows, cols], qlane, h))
                    dkv[1, 0:nk] += dot_tn(w, dom)
                dproj[rows, cols] = rotate(dq * 0.125, cos[rows], -sin[rows]).astype(BF16)
            dproj[:, pl.ds(pl.multiple_of(width + j * 128, 128), 128)] = rotate(dkv[0], cos[...], -sin[...]).astype(BF16)
            dproj[:, pl.ds(pl.multiple_of(2 * width + j * 128, 128), 128)] = dkv[1].astype(BF16)

        for kind in range(3):
            cols = slice(kind * width + part * 256, kind * width + part * 256 + 256)
            d = dot_tn(n1[...], dproj[:, cols])
            if plan:
                slab_store(gq, part, d, slice(kind * 256, kind * 256 + 256))
            else:
                d_qkv[:, cols] = d
        if plan:
            slab_copy(gq, gq_recv, part, 0, 0).start()
            for stage in range(part):
                slab_done(gq, gq_recv, part - 1 - stage, stage, 0)
        tick(4)

    for c in f_copies.values():
        c.wait()

    @pl.loop(0, length // 256)
    def _(i):
        rows = tile(i, 256)
        first, second = chosen(rows, 256)
        mix = jnp.where(first, meta[rows, 2:3], jnp.where(second, meta[rows, 3:4], 0.0)).astype(BF16)
        out[rows] = (fk0[rows] + dot(mix, f_back[...].reshape(slots, width))).astype(BF16)

    tick(2)

    @pl.loop(0, width // 256)
    def _(j):
        cols = tile(j, 256)
        fk0[:, cols] = dot_nt(dproj[...], wqkv[cols, :])

    @pl.loop(0, length // 64)
    def _(i):
        rows = tile(i, 64)
        x = tok[rows].astype(F32)
        r1 = lax.rsqrt(row_mean(x * x) + EPS)
        xr = x * r1
        d = fk0[rows]
        dn = d * ln1[...]
        lnacc[8:16] += jnp.sum((d * xr).reshape(8, 8, width), axis=0)
        igrad[rows] = (dres[rows] + r1 * dn - xr * (r1 * r1) * row_mean(dn * x)).astype(BF16)

    ln = jnp.zeros((128, width), F32)
    row = lax.broadcasted_iota(jnp.int32, (128, width), 0)
    ln = jnp.where(row == 14, jnp.sum(lnacc[8:16], axis=0, keepdims=True), ln)
    ln = jnp.where(row == 15, jnp.sum(lnacc[0:8], axis=0, keepdims=True), ln)
    small = dot_tn(n2b[...], dcat[:, 0:128]) + dot_tn(cot[...], dcat[:, 128:256]) + jnp.transpose(ln)
    if not plan:
        d_small[...] = small
        return
    slab_store(ga, 0, small, slice(width, width + 128))
    slab_copy(ga, ga_recv, 0, 0, 3).start()
    live = [(gq, gq_recv, 0, 2, 0), (gq, gq_recv, 1, 1, 0), (gq, gq_recv, 2, 0, 0), (ga, ga_recv, 0, 0, 3)]
    while live:
        for src, bufs, s, stage, base in live:
            slab_done(src, bufs, s, stage, base)
        live = [(a, b, s, stage + 1, base) for a, b, s, stage, base in live if stage < 4]
        tick(4)
    tick(100)
    for s in range(3):
        for kind in range(3):
            at = kind * width + s * 256
            d_qkv[:, at : at + 256] = fin[s, :, kind * 256 : kind * 256 + 256]
    d_attn[...] = fin[3, :, 0:width]
    d_small[...] = fin[3, :, width : width + 128]


def shape(*s, dtype=BF16):
    return jax.ShapeDtypeStruct(s, dtype)


def call(kernel, outs, scratch, args, name, collective_id):
    return pl.pallas_call(
        kernel,
        out_shape=outs,
        in_specs=[pl.BlockSpec(memory_space=pltpu.VMEM)] * len(args),
        out_specs=[pl.BlockSpec(memory_space=pltpu.VMEM)] * len(outs),
        scratch_shapes=scratch,
        compiler_params=pltpu.CompilerParams(
            vmem_limit_bytes=VMEM_LIMIT, has_side_effects=True, collective_id=collective_id
        ),
        name=name,
    )(*args)


def body(
    tokens, segments, routes, prev_logits, ln1_gain, w_qkv, w_attn, ln2_gain, w_router, const_mix, const_vec,
    expert_in, expert_out, cotangent,
):
    length, width = tokens.shape
    heads = width // HEAD_DIM
    experts = lax.axis_size("expert") * expert_in.shape[0]
    hidden = expert_out.shape[1]
    capacity = length // 2
    slots = experts * capacity
    n_dp = lax.axis_size("dp")
    V = pltpu.VMEM
    DMA = pltpu.SemaphoreType.DMA
    cos, sin = (jnp.asarray(t) for t in rotary_tables(length))
    rT, pT = routes.T, prev_logits.T
    wrT, cmT, cvT = w_router.T, const_mix.T, const_vec.T
    ln1, ln2 = ln1_gain.reshape(1, width), ln2_gain.reshape(1, width)
    peers = experts - 1

    q, k, v, pw, att, n1, res, meta, send, g_rows = call(
        fwd_kernel,
        [
            shape(length, width), shape(length, width), shape(length, width), shape(heads, length, length),
            shape(length, width), shape(length, width), shape(length, width, dtype=F32),
            shape(length, 128, dtype=F32), shape(experts, capacity, width + 128), shape(experts, capacity, width),
        ],
        [
            V((length, 256), F32), V((length, length), F32), V((128, width), F32), V((3, length, 128), F32),
            V((128, length), F32), V((length, width), BF16), V((length, width), BF16), V((2 * length, 128), BF16),
            V((length, 128), F32), V((slots, length), BF16), V((experts, capacity, width), BF16),
            DMA((peers,)), DMA((peers,)),
        ],
        (tokens, segments, rT, pT, ln1, w_qkv, w_attn, ln2, wrT, cmT, cotangent, cos, sin),
        "attention", 0,
    )

    tiles, slabs = 4, 2
    ft = hidden // tiles
    within = n_dp == 8 and experts == 4
    stages = ((("dp", 1), ("dp", 2), ("dp", 4)), (("dp", 2), ("dp", 1), ("dp", 4))) if within else ()
    order = (("expert", 1), ("expert", 2), ("dp", 1), ("dp", 2), ("dp", 4))
    slab_in, slab_out = (2 * tiles, width, ft), (slabs, hidden, width // slabs)

    def part_of(s, n):
        return (s[0], s[1] // n, s[2])

    wide = width + 128
    f_rows, d_back, g_out, g_in = call(
        functools.partial(expert_kernel, stages),
        [
            shape(experts, capacity, width), shape(experts, capacity, wide), shape(*slab_out),
            shape(*part_of(slab_in, 2 if within else 1)),
        ],
        [
            V((experts, capacity, wide), BF16), V((slots, width), BF16), V((tiles, slots, ft), BF16),
            V((tiles, slots, 2 * ft), BF16), V((slots, width), F32), V((slots, width), F32),
            V((experts, capacity, wide), BF16),
        ]
        + ([V(slab_in, BF16)] + [DMA((2 * tiles,))] * 2 if within else [])
        + [DMA((peers,))] * 4,
        (send, g_rows, expert_in, expert_out),
        "experts", 1,
    )

    args = (
        tokens, cotangent, res, meta, rT, f_rows, d_back, q, k, v, pw, att, n1, ln1, w_qkv, w_attn, ln2, wrT, cmT, cvT,
        cos, sin,
    )
    n_all = n_dp * experts
    rows = width // n_all if within else width
    outs = [
        shape(length, width), shape(length, width), shape(rows, 3 * width, dtype=F32), shape(rows, width, dtype=F32),
        shape(rows, 128, dtype=F32),
    ]
    scratch = [
        V((128, width), F32), V((2, length, 128), F32), V((length, width), F32), V((length, width), F32),
        V((2, length, 128), F32), V((length, 256), BF16), V((length, width), BF16), V((length, width), F32),
        V((length, width), BF16), V((length, 3 * width), BF16), V((length, width), BF16),
        V((2, length, 128), F32), V((16, width), F32), V((experts, capacity, width), BF16), DMA((peers,)), DMA((peers,)),
    ]
    if within:
        args += (g_in, g_out)
        outs += [shape(width // n_dp, 2 * hidden, dtype=F32), shape(hidden // n_dp, width, dtype=F32)]
        scratch += [
            V(part_of(slab_in, 4), BF16), V(part_of(slab_in, 8), BF16), V(part_of(slab_out, 2), BF16),
            V(part_of(slab_out, 4), BF16), V(part_of(slab_out, 8), BF16), DMA((2, 2 * tiles)), DMA((2, 2 * tiles)),
            DMA((3, slabs)), DMA((3, slabs)),
            V((3, width, width), BF16), V((1, width, wide), BF16),
        ]
        scratch += [V((3, width >> s, width), BF16) for s in range(1, 5)]
        scratch += [V((1, width >> s, wide), BF16) for s in range(1, 5)]
        scratch += [
            V((4, 2 * rows, wide), F32), V((4, rows, wide), F32), V((4, rows, wide), F32), DMA((4, 5)), DMA((4, 5)),
        ]
    plan = (stages, order) if within else ()
    done = call(functools.partial(bwd_kernel, plan), outs, scratch, args, "backward", 2)
    out, igrad, d_qkv, d_attn, small = done[:5]
    if within:
        g_in, g_out = done[5:]
    else:
        g_in = jnp.moveaxis(g_in.reshape(tiles, 2, width, ft), 2, 0).transpose(0, 2, 1, 3).reshape(width, 2 * hidden)
        g_out = jnp.moveaxis(g_out, 0, 1).reshape(hidden, width)
        g_in = lax.psum_scatter(g_in, "dp", scatter_dimension=0, tiled=True).astype(F32)
        g_out = lax.psum_scatter(g_out, "dp", scatter_dimension=0, tiled=True).astype(F32)
        d_qkv, d_attn, small = (
            lax.psum_scatter(d, ("dp", "expert"), scatter_dimension=0, tiled=True) for d in (d_qkv, d_attn, small)
        )
    return (
        out, igrad, small[:, 14], d_qkv, d_attn, small[:, 15], small[:, 0:8], small[:, 8:12], small[:, 12:14],
        g_in[None], g_out[None],
    )


def solution(mesh):
    rows = P(("dp", "expert"), None)
    return jax.shard_map(
        body,
        mesh=mesh,
        in_specs=(
            rows, rows, rows, rows, P(), P(), P(), P(), P(), P(), P(),
            P("expert", None, None), P("expert", None, None), rows,
        ),
        out_specs=(
            rows, rows, P(("dp", "expert")), rows, rows, P(("dp", "expert")), rows, rows, rows,
            P("expert", "dp", None), P("expert", "dp", None),
        ),
        check_vma=False,
    )
```

```python
import functools
import math

import jax
import jax.numpy as jnp
import numpy as np
from jax import lax
from jax.experimental import pallas as pl
from jax.experimental.pallas import tpu as pltpu
from jax.sharding import PartitionSpec as P

HEAD_DIM = 64
EPS = 1e-06
MASKED = -1e30
F32 = jnp.float32
BF16 = jnp.bfloat16
VMEM_LIMIT = 62 * 1024 * 1024


def dot(a, b):
    return lax.dot_general(a, b, (((1,), (0,)), ((), ())), preferred_element_type=F32)


def dot_nt(a, b):
    return lax.dot_general(a, b, (((1,), (1,)), ((), ())), preferred_element_type=F32)


def dot_tn(a, b):
    return lax.dot_general(a, b, (((0,), (0,)), ((), ())), preferred_element_type=F32)


def tile(i, size):
    return pl.ds(pl.multiple_of(i * size, size), size)


def rotary_tables(length):
    half = HEAD_DIM // 2
    inverse = np.exp(np.arange(half, dtype=np.float32) * np.float32(-2.0 * math.log(10000.0) / HEAD_DIM))
    angles = np.arange(length, dtype=np.float32)[:, None] * inverse.astype(np.float32)[None, :]
    cos, sin = np.cos(angles), np.sin(angles)
    return (
        np.concatenate([cos] * 4, axis=1).astype(np.float32),
        np.concatenate([-sin, sin] * 2, axis=1).astype(np.float32),
    )


def rotate(x, cos, sin):
    lane = lax.broadcasted_iota(jnp.int32, x.shape, 1)
    front = (lane % HEAD_DIM) < HEAD_DIM // 2
    other = jnp.where(front, pltpu.roll(x, 96, 1), pltpu.roll(x, 32, 1))
    return x * cos + other * sin


def row_mean(x):
    return jnp.mean(x, axis=-1, keepdims=True)


def pick(x, lane, index):
    return jnp.sum(jnp.where(lane == index, x, 0.0), axis=-1, keepdims=True)


def half_mask(x, lane, which):
    keep = (lane < HEAD_DIM) if which == 0 else (lane >= HEAD_DIM)
    return jnp.where(keep, x, jnp.zeros_like(x))


MESH = pl.DeviceIdType.MESH


def flip(i, m):
    return i + m * (1 - 2 * ((i // m) % 2))


def side(mask):
    axis, m = mask
    return (lax.axis_index(axis) // m) % 2


def partner(mask):
    axis, m = mask
    return {axis: flip(lax.axis_index(axis), m)}


def across(r):
    e = lax.axis_index("expert")
    for m in (1, 2):
        if r & m:
            e = flip(e, m)
    return e


def greet(masks, peers=0):
    barrier = pltpu.get_barrier_semaphore()
    for mask in masks:
        pl.semaphore_signal(barrier, inc=1, device_id=partner(mask), device_id_type=MESH)
    for r in range(1, peers + 1):
        pl.semaphore_signal(barrier, inc=1, device_id={"expert": across(r)}, device_id_type=MESH)
    pl.semaphore_wait(barrier, len(masks) + peers)


def exchange(src, dst, send_sem, recv_sem):
    return {
        r: pltpu.make_async_remote_copy(
            src.at[r], dst.at[r], send_sem.at[r - 1], recv_sem.at[r - 1],
            device_id={"expert": across(r)}, device_id_type=MESH,
        )
        for r in range(src.shape[0] - 1, 0, -1)
    }


def half_copy(src, dst, mask, rows, send_sem, recv_sem):
    start = pl.multiple_of((1 - side(mask)) * rows, 8)
    return pltpu.make_async_remote_copy(
        src.at[pl.ds(start, rows)], dst, send_sem, recv_sem, device_id=partner(mask), device_id_type=MESH
    )


def half_add(src, dst, mask, rows, out=None):
    start = side(mask) * rows
    step = 48 if rows % 48 == 0 else 64 if rows % 64 == 0 else 24
    out = dst if out is None else out

    @pl.loop(0, rows // step)
    def _(i):
        here = pl.ds(pl.multiple_of(i * step, 8), step)
        mine = src[pl.ds(pl.multiple_of(start + i * step, 8), step)].astype(F32)
        out[here] = (mine + dst[here].astype(F32)).astype(out.dtype)


def place_of(shard, masks):
    place = 0
    for m in masks:
        place = 2 * place + (shard // m) % 2
    return place


def fwd_kernel(
    tok, seg, rT, pT, ln1, wqkv, wattn, ln2, wrT, cmT, cot, cos, sin,
    q_out, k_out, v_out, pw_out, att_out, n1_out, res_out, meta, send_out, g_rows,
    proj, bias, wcat, rb, pb, n2b, n2l, gl, tg, onehot, g_out, send_sem, recv_sem, pw, send, pw_sem, row_sem,
):
    length, width = tok.near.shape
    capacity = length // 2
    experts = send.shape[0]

    for ref in (cot, tok, wqkv, cos, sin, wattn):
        ref.start()
    q, k, v, att, n1, res = (ref.near for ref in (q_out, k_out, v_out, att_out, n1_out, res_out))
    greet((), experts - 1)
    for kk in range(2):
        rb[kk] = jnp.transpose(jnp.broadcast_to(rT[kk : kk + 1, :].astype(F32), (128, length)))
    all_lane = lax.broadcasted_iota(jnp.int32, (length, 128), 1).astype(F32)
    count = ((rb[0] == all_lane).astype(F32) + (rb[1] == all_lane).astype(F32)).astype(BF16)

    @pl.loop(0, length // 128)
    def _(i):
        rows = tile(i, 128)
        lane = lax.broadcasted_iota(jnp.int32, (128, 128), 1)
        lane_f = lane.astype(F32)
        t_id = lax.broadcasted_iota(jnp.int32, (128, length), 0) + i * 128
        before = (t_id > lax.broadcasted_iota(jnp.int32, (128, length), 1)).astype(F32).astype(BF16)
        place = dot(before, count) + lane_f * float(capacity) + 1.0
        out = jnp.zeros((128, 128), F32)
        for kk in range(2):
            hit = (rb[kk, rows] == lane_f) & (lane < experts)
            out = jnp.where(lane == kk, jnp.sum(jnp.where(hit, place, 0.0), axis=-1, keepdims=True) - 1.0, out)
        tg[rows] = out

    target = jnp.transpose(tg[...])
    pb[...] = target

    cot = cot.wait()
    copies = exchange(g_out, g_rows, send_sem, recv_sem)
    own_rows = pltpu.make_async_copy(g_out.at[0], g_rows.at[0], row_sem.at[experts])
    for r in range(experts - 1, -1, -1):
        s_id = (lax.broadcasted_iota(jnp.int32, (capacity, length), 0) + across(r) * capacity).astype(F32)
        here = (pb[0:1] == s_id).astype(F32) + (pb[1:2] == s_id).astype(F32)
        onehot[r * capacity : (r + 1) * capacity] = here.astype(BF16)
        g_out[r] = dot(here.astype(BF16), cot[...]).astype(BF16)
        (copies[r] if r else own_rows).start()
    tok = tok.wait()

    @pl.loop(0, length // 64)
    def _(i):
        rows = tile(i, 64)
        x = tok[rows].astype(F32)
        r = lax.rsqrt(row_mean(x * x) + EPS)
        n1[rows] = (x * r * ln1[...]).astype(BF16)

    n1_out.start()
    wqkv, cos, sin = wqkv.wait(), cos.wait(), sin.wait()
    for kind, (dst, done) in enumerate(((q, q_out), (k, k_out), (v, v_out))):

        @pl.loop(0, width // 256)
        def _(j):
            cols = pl.ds(pl.multiple_of(kind * width + j * 256, 256), 256)
            proj[...] = dot(n1[...], wqkv[:, cols])

            @pl.loop(0, length // 128)
            def _(i):
                rows = tile(i, 128)
                for part in range(2):
                    x = proj[rows, part * 128 : part * 128 + 128]
                    if kind < 2:
                        x = rotate(x, cos[rows], sin[rows])
                    if kind == 0:
                        x = x * 0.125
                    dst[rows, pl.ds(pl.multiple_of(j * 256 + part * 128, 128), 128)] = x.astype(BF16)

        done.start()

    seg_f = seg[...].astype(F32)
    rb[2] = jnp.transpose(jnp.broadcast_to(seg_f, (128, length)))

    @pl.loop(0, length // 128)
    def _(i):
        rows = tile(i, 128)
        row_id = lax.broadcasted_iota(jnp.int32, (128, length), 0) + i * 128
        col_id = lax.broadcasted_iota(jnp.int32, (128, length), 1)
        same = rb[2, rows, 0:1] == seg_f
        bias[rows] = jnp.where(same & (row_id >= col_id), 0.0, MASKED)

    block = length // 2

    def weights_copy(j, b):
        at = (pl.ds(2 * j, 2), slice(b * block, (b + 1) * block), slice(0, (b + 1) * block))
        return pltpu.make_async_copy(pw.at[at], pw_out.at[at], pw_sem.at[j, b])

    @pl.loop(0, width // 128)
    def _(j):
        cols = tile(j, 128)
        for b in range(2):
            rows = slice(b * block, (b + 1) * block)
            nk = (b + 1) * block
            qlane = lax.broadcasted_iota(jnp.int32, (block, 128), 1)
            klane = lax.broadcasted_iota(jnp.int32, (nk, 128), 1)
            acc = jnp.zeros((block, 128), F32)
            for h in range(2):
                s = dot_nt(half_mask(q[rows, cols], qlane, h), k[0:nk, cols]) + bias[rows, 0:nk]
                m = jnp.max(s, axis=-1, keepdims=True)
                e = jnp.exp(s - m)
                w = (e * (1.0 / jnp.sum(e, axis=-1, keepdims=True))).astype(BF16)
                pw[2 * j + h, rows, 0:nk] = w
                acc = acc + dot(w, half_mask(v[0:nk, cols], klane, h))
            att[rows, cols] = acc.astype(BF16)
            weights_copy(j, b).start()

    att_out.start()
    wattn = wattn.wait()

    @pl.loop(0, width // 256)
    def _(j):
        cols = tile(j, 256)
        res[:, cols] = tok[:, cols].astype(F32) + dot(att[...], wattn[:, cols])

    res_out.start()

    @pl.loop(0, length // 64)
    def _(i):
        rows = tile(i, 64)
        x = res[rows]
        n2 = x * lax.rsqrt(row_mean(x * x) + EPS) * ln2[...]
        high = n2.astype(BF16)
        n2b[rows] = high
        n2l[rows] = (n2 - high.astype(F32)).astype(BF16)

    wcat[...] = jnp.zeros_like(wcat)
    wcat[0:8] = wrT[...]
    wcat[8:12] = cmT[...]
    w_high = wcat[...].astype(BF16)
    w_low = (wcat[...] - w_high.astype(F32)).astype(BF16)

    pb[8:16] = pT[...]
    rb[2] = jnp.transpose(jnp.concatenate([pb[8:16], jnp.zeros((120, length), F32)], axis=0))

    @pl.loop(0, length // 128)
    def _(i):
        rows = tile(i, 128)
        lane = lax.broadcasted_iota(jnp.int32, (128, 128), 1)
        lane_f = lane.astype(F32)
        high = n2b[rows]
        mixed = dot_nt(high, w_high) + dot_nt(high, w_low) + dot_nt(n2l[rows], w_high)
        logits = mixed + rb[2, rows]
        hits = [(rb[kk, rows] == lane_f).astype(F32) for kk in range(2)]
        chosen = [jnp.sum(h * logits, axis=-1, keepdims=True) for h in hits]
        top = jnp.maximum(chosen[0], chosen[1])
        e = [jnp.exp(c - top) for c in chosen]
        inv = 1.0 / (e[0] + e[1])
        gates = [v_ * inv for v_ in e]
        shares = []
        for j in range(2):
            a0, a1 = pick(mixed, lane, 8 + 2 * j), pick(mixed, lane, 9 + 2 * j)
            mx = jnp.maximum(a0, a1)
            b0, b1 = jnp.exp(a0 - mx), jnp.exp(a1 - mx)
            binv = 1.0 / (b0 + b1)
            shares.append((b0 * binv, b1 * binv))
        gate_sum = gates[0] * hits[0] + gates[1] * hits[1]
        cg = [pick(gate_sum, lane, 6), pick(gate_sum, lane, 7)]
        keep = pick(gate_sum, lane, 5) + cg[0] * shares[0][0] + cg[1] * shares[1][0]
        values = (
            gates[0], gates[1], keep, cg[0], cg[1], shares[0][0], shares[0][1], shares[1][0], shares[1][1],
        )
        out = tg[rows]
        for n, value in enumerate(values):
            out = jnp.where(lane == n + 2, value, out)
        meta[rows] = out
        for kk in range(2):
            g_high = gates[kk].astype(BF16).astype(F32)
            both = jnp.where(lane == 0, g_high, jnp.where(lane == 1, gates[kk] - g_high, 0.0))
            gl[pl.ds(pl.multiple_of(kk * length + i * 128, 128), 128)] = both.astype(BF16)

    @pl.loop(0, experts)
    def _(e):
        owner = flip(lax.axis_index("expert"), 1)
        owner = jnp.where(e % 2 == 1, owner, lax.axis_index("expert"))
        owner = jnp.where(e // 2 == 1, flip(owner, 2), owner)
        s_id = (lax.broadcasted_iota(jnp.int32, (capacity, length), 0) + owner * capacity).astype(F32)
        gate = jnp.zeros((capacity, 128), F32)
        for kk in range(2):
            here = (pb[kk : kk + 1] == s_id).astype(F32).astype(BF16)
            gate = gate + dot(here, gl[kk * length : (kk + 1) * length])
        send[e, :, 0:width] = dot(onehot[tile(e, capacity)], n2b[...]).astype(BF16)
        send[e, :, width : width + 128] = gate.astype(BF16)
        pltpu.make_async_copy(send.at[e], send_out.at[e], row_sem.at[e]).start()

    for ref in (q_out, k_out, v_out, att_out, n1_out, res_out):
        ref.wait()

    @pl.loop(0, width // 128)
    def _(j):
        for b in range(2):
            weights_copy(j, b).wait()

    @pl.loop(0, experts)
    def _(e):
        pltpu.make_async_copy(send.at[e], send_out.at[e], row_sem.at[e]).wait()

    own_rows.wait()
    for c in copies.values():
        c.wait()


def expert_kernel(stages, xs, g_rows, win, wout, *refs):
    f_out, d_back, go_out = refs[:3]
    f_rows, go = f_out.near, go_out.near
    if stages:
        late_out, early_out = refs[3:5]
        p_late, p_early = late_out.near, early_out.near
        refs = refs[5:]
    else:
        gi_out = refs[3]
        gi = gi_out.near
        refs = refs[4:]
    xr, dy, hid, dgu, f_acc, d_acc, d_out = refs[:7]
    refs = refs[7:]
    if stages:
        gi, p_first, in_send, in_recv, e_send, e_recv = refs[:6]
        refs = refs[6:]
    x_send, x_recv, d_send, d_recv, own_sem = refs
    groups, capacity, wide = xs.shape
    hidden, width = wout.near.shape[1:]
    tiles, rows_all, ft = hid.shape
    slabs = go.shape[0]
    shards = 2 ** len(stages[0]) if stages else 0
    near = rows_all // 2

    greet([s[0] for s in stages], groups - 1)
    copies = exchange(xs, xr, x_send, x_recv)
    for c in copies.values():
        c.start()
    own_x = pltpu.make_async_copy(xs.at[0], xr.at[0], own_sem.at[0])
    own_x.start()
    for ref in (g_rows, win, wout):
        ref.start()

    def gated(r):
        pair = xr[r, :, width:wide].astype(F32)
        lane = lax.broadcasted_iota(jnp.int32, pair.shape, 1)
        gate = jnp.sum(jnp.where(lane < 2, pair, 0.0), axis=-1, keepdims=True)
        dy[r * capacity : (r + 1) * capacity] = (g_rows[r].astype(F32) * gate).astype(BF16)

    def cols_of(f):
        return tile(f, ft), pl.ds(pl.multiple_of(hidden + f * ft, ft), ft)

    def work(f, part):
        gate_cols, up_cols = cols_of(f)
        rows = slice(part * near, (part + 1) * near)
        x = xr[2 * part : 2 * part + 2, :, 0:width].reshape(near, width)
        gate = dot(x, win[0, :, gate_cols])
        up = dot(x, win[0, :, up_cols])
        dh = dot_nt(dy[rows], wout[0, gate_cols, :])
        sig = 1.0 / (1.0 + jnp.exp(-gate))
        silu = gate * sig
        h = (silu * up).astype(BF16)
        da = (dh * up * (sig + silu * (1.0 - sig))).astype(BF16)
        db = (dh * silu).astype(BF16)
        hid[f, rows] = h
        dgu[f, rows, 0:ft] = da
        dgu[f, rows, ft : 2 * ft] = db
        y = dot(h, wout[0, gate_cols, :])
        d = dot_nt(da, win[0, :, gate_cols]) + dot_nt(db, win[0, :, up_cols])

        @pl.when(f == 0)
        def _():
            f_acc[rows] = y
            d_acc[rows] = d

        @pl.when(f > 0)
        def _():
            f_acc[rows] += y
            d_acc[rows] += d

    def in_copy(part, f, p):
        dst = (p_first if part == 0 else p_late).at[2 * (f - part * tiles // 2) + p]
        slab = 2 * f + p
        return half_copy(gi.at[slab], dst, stages[p][0], width // 2, in_send.at[slab], in_recv.at[slab]), dst

    def early_copy(slab):
        return half_copy(
            p_first.at[slab], p_early.at[slab], stages[slab % 2][1], width // 4, e_send.at[slab], e_recv.at[slab]
        )

    own_x.wait()
    g_rows = g_rows.wait()
    copies[1].wait()
    gated(0)
    gated(1)

    win, wout = win.wait(), wout.wait()

    @pl.loop(0, tiles)
    def _(f):
        work(f, 0)

    copies[3].wait()
    copies[2].wait()
    gated(2)
    gated(3)

    for part in range(2):

        @pl.loop(part * (tiles // 2), (part + 1) * (tiles // 2))
        def _(f):
            work(f, 1)
            for p in range(2):
                d = dot_tn(xr[:, :, 0:width].reshape(rows_all, width), dgu[f, :, p * ft : (p + 1) * ft])
                if not stages:
                    gi[2 * f + p] = d.astype(BF16)
                    continue
                size = width // shards
                for j in range(shards):
                    at = place_of(j, [m for _, m in stages[p]]) * size
                    gi[2 * f + p, at : at + size] = d[j * size : (j + 1) * size].astype(BF16)
                in_copy(part, f, p)[0].start()

    d_copies = exchange(d_out, d_back, d_send, d_recv)
    own_d = pltpu.make_async_copy(d_out.at[0], d_back.at[0], own_sem.at[1])
    for r in range(groups - 1, -1, -1):
        rows = slice(r * capacity, (r + 1) * capacity)
        y = f_acc[rows]
        f_rows[r] = y.astype(BF16)
        dots = jnp.sum(y * g_rows[r].astype(F32), axis=-1, keepdims=True)
        high = dots.astype(BF16).astype(F32)
        lane = lax.broadcasted_iota(jnp.int32, (capacity, 128), 1)
        extra = jnp.where(lane == 0, high, jnp.where(lane == 1, dots - high, 0.0)).astype(BF16)
        d_out[r, :, 0:width] = d_acc[rows].astype(BF16)
        d_out[r, :, width:wide] = extra
        (d_copies[r] if r else own_d).start()
    f_out.start()

    for c in range(slabs):
        cols = slice(c * (width // slabs), (c + 1) * (width // slabs))

        @pl.loop(0, tiles)
        def _(t):
            d = dot_tn(hid[t], dy[:, cols]).astype(BF16)
            if not stages:
                go[c, tile(t, ft)] = d
                return
            size = hidden // shards
            for i in range(ft // size):
                at = place_of(t * (ft // size) + i, [m for _, m in stages[0]])
                go[c, tile(at, size)] = d[i * size : (i + 1) * size]

    go_out.start()
    if stages:
        for part in range(2):
            for f in range(part * (tiles // 2), (part + 1) * (tiles // 2)):
                for p in range(2):
                    copy, dst = in_copy(part, f, p)
                    copy.wait()
                    half_add(gi.at[2 * f + p], dst, stages[p][0], width // 2)
                    if part == 0:
                        early_copy(2 * f + p).start()
        late_out.start()
        for slab in range(tiles):
            early_copy(slab).wait()
            half_add(p_first.at[slab], p_early.at[slab], stages[slab % 2][1], width // 4)
        early_out.start()
        late_out.wait()
        early_out.wait()
    else:
        gi_out.start()
        gi_out.wait()
    f_out.wait()
    go_out.wait()
    own_d.wait()
    for c in d_copies.values():
        c.wait()


def out_start(copy, i):
    copy(i, 0).start()


def as_columns(x):
    row = jnp.sum(x, axis=0, keepdims=True)
    return jnp.transpose(jnp.broadcast_to(row, (128, row.shape[1])))


class Slab:
    def __init__(self, order, refs):
        self.order = order
        self.bufs, (self.pair, self.got, self.send, self.recv) = refs[:5], refs[5:]
        self.bits = [m * (1 if a == "expert" else lax.axis_size("expert")) for a, m in order]
        self.out = ()

    def store(self, value, at):
        total = 2 ** len(self.order)
        size, cols = value.shape[0] // total, slice(at, at + value.shape[1])
        for j in range(total):
            other = j + self.bits[-1]
            if (j // self.bits[-1]) % 2:
                continue
            row = place_of(j, self.bits[:-1]) * 2 * size
            both = jnp.concatenate([value[j * size : (j + 1) * size], value[other * size : (other + 1) * size]], axis=0)
            self.bufs[0][row : row + 2 * size, cols] = both.astype(BF16)

    def copy(self, s):
        src, dst = (self.bufs[s], self.bufs[s + 1]) if s < 4 else (self.pair, self.got)
        return half_copy(src, dst, self.order[s], dst.shape[0], self.send.at[s], self.recv.at[s])

    def start(self):
        self.copy(0).start()

    def done(self, s):
        self.copy(s).wait()
        if s < 4:
            into = self.pair if s == 3 else None
            half_add(self.bufs[s], self.bufs[s + 1], self.order[s], self.bufs[s + 1].shape[0], into)
            self.copy(s + 1).start()
            return
        rows = self.got.shape[0]
        mine = self.pair[pl.ds(pl.multiple_of(side(self.order[4]) * rows, 8), rows)]
        total = mine + self.got[...]
        for ref, at, col, n in self.out:
            ref[:, at : at + n] = total[:, col : col + n]


def bwd_kernel(plan, *refs):
    (
        tok, cot, res, meta, rT, f_rows, d_back, q, k, v, pw_far, att, n1, ln1, wqkv, wattn, ln2, wrT, cmT, cvT, cos, sin,
    ) = refs[:22]
    refs = refs[22:]
    if plan:
        stages, order = plan
        p_early, p_late, p_out, out_s, igrad_s, d_qkv, d_attn, d_small, d_ln, g_in_s, g_out_s = refs[:11]
        g_in, g_out = g_in_s.near, g_out_s.near
        refs = refs[11:]
    else:
        out_s, igrad_s, d_qkv, d_attn, d_small = refs[:5]
        refs = refs[5:]
    out, igrad = out_s.near, igrad_s.near
    wcat, rb, fk0, dsn, dots, dcat, n2b, dres, dbr, dproj, datt, dkv, lnacc, f_back, f_send, f_recv, pw, own_sem = refs[:18]
    refs = refs[18:]
    length, width = tok.near.shape
    experts, capacity, _ = f_rows.shape
    slots = experts * capacity
    block = length // 2

    weights = []
    for b in range(2):
        at = (slice(0, pw.shape[0]), slice(b * block, (b + 1) * block), slice(0, (b + 1) * block))
        weights.append(pltpu.make_async_copy(pw_far.at[at], pw.at[at], own_sem.at[b]))
    own_f = pltpu.make_async_copy(f_rows.at[0], f_back.at[0], own_sem.at[2])
    for ref in (d_back, cot, res):
        ref.start()
    greet(order[2:] if plan else (), experts - 1)
    f_copies = exchange(f_rows, f_back, f_send, f_recv)

    acts = {}
    if plan:
        in1, in2, out0, out1, out2, in_send, in_recv, out_send, out_recv = refs[:9]
        slab_refs = [refs[9 + 9 * n : 18 + 9 * n] for n in range(6)]
        late = p_late.near.shape[0]
        slabs_in = late + p_early.near.shape[0]
        ft = p_late.near.shape[2]
        hidden = g_in.shape[1] // 2

        def in_refs(i, s, far=False):
            n = i - (slabs_in - late)
            p = "far" if far else "near"
            first = getattr(p_early, p).at[i] if n < 0 else in1.at[n]
            return (getattr(p_late, p).at[n], first) if s == 0 else (first, in2.at[i])

        def in_copy(i, s):
            src, dst = in_refs(i, s, True)
            return half_copy(src, dst, stages[i % 2][s + 1], dst.shape[0], in_send.at[s, i], in_recv.at[s, i])

        def in_done(i, s):
            in_copy(i, s).wait()
            src, dst = in_refs(i, s)
            if s == 0:
                half_add(src, dst, stages[i % 2][1], dst.shape[0])
                in_copy(i, 1).start()
            else:
                to = (i % 2) * hidden + (i // 2) * ft
                half_add(src, dst, stages[i % 2][2], dst.shape[0], g_in.at[:, to : to + ft])

        def out_refs(i, s, far=False):
            return ((p_out.far if far else p_out.near, out0), (out0, out1), (out1, out2))[s]

        def out_copy(i, s):
            src, dst = out_refs(i, s, True)
            return half_copy(
                src.at[i], dst.at[i], stages[0][s], dst.shape[1], out_send.at[s, i], out_recv.at[s, i]
            )

        def out_done(i, s):
            out_copy(i, s).wait()
            src, dst = out_refs(i, s)
            wide = out2.shape[2]
            into = g_out.at[:, i * wide : (i + 1) * wide] if s == 2 else None
            half_add(src.at[i], dst.at[i], stages[0][s], dst.shape[1], into)
            if s < 2:
                out_copy(i, s + 1).start()

        swapped = (order[0], order[2], order[1], order[3], order[4])
        slabs = [Slab(o, r) for o, r in zip((order, order, order, order, swapped, order), slab_refs)]
        attn_slab, q0, q1, q2a, q2b, ln_slab = slabs

        def q_out(first, pairs):
            n = 128 * pairs
            return [(d_qkv, kind * width + first * 128, kind * n, n) for kind in range(3)]

        attn_slab.out = [(d_attn, 0, 0, width), (d_small, 0, width, 128)]
        q0.out, q1.out, q2a.out, q2b.out = q_out(0, 2), q_out(2, 2), q_out(4, 1), q_out(5, 1)
        ln_slab.out = [(d_ln, 0, 0, 128)]

        out_copy(0, 0).start()
        for i in range(slabs_in - late):
            in_copy(i, 1).start()
        for i in range(slabs_in - late, slabs_in, 2):
            in_copy(i, 0).start()
        a, b = slabs_in - late, slabs_in
        acts = {
            "token": [(in_done, i, 0) for i in range(a, b, 2)]
            + [(in_done, i, 1) for i in range(a)]
            + [(out_start, out_copy, 1)],
            "attn": [(attn_slab.start,), (out_done, 0, 0)],
            "part0": [(q0.start,), (attn_slab.done, 0)],
            "part1": [(q1.start,), (q0.done, 0), (attn_slab.done, 1), (out_done, 0, 1)]
            + [(out_start, in_copy, i) for i in range(a + 1, b, 2)]
            + [(in_done, i, 1) for i in range(a, b, 2)],
            "part2": [
                (q2a.start,), (q2b.start,), (q1.done, 0), (q0.done, 1), (attn_slab.done, 2), (out_done, 1, 0),
            ],
            "norm": [(q2a.done, 0), (q2b.done, 0), (q1.done, 1), (q0.done, 2), (attn_slab.done, 3)]
            + [(in_done, i, 0) for i in range(a + 1, b, 2)]
            + [(out_done, 0, 2)],
            "input": [
                (ln_slab.start,), (q2a.done, 1), (q2b.done, 1), (q1.done, 2), (q0.done, 3), (attn_slab.done, 4),
                (out_done, 1, 1), (ln_slab.done, 0),
            ],
            "output": [
                (q2a.done, 2), (q2b.done, 2), (ln_slab.done, 1), (q1.done, 3), (q0.done, 4), (ln_slab.done, 2),
                (q2a.done, 3), (q2b.done, 3), (q1.done, 4), (ln_slab.done, 3), (q2a.done, 4), (q2b.done, 4),
            ]
            + [(in_done, i, 1) for i in range(a + 1, b, 2)]
            + [(ln_slab.done, 4), (out_done, 1, 2)],
        }
    for c in f_copies.values():
        c.start()
    late_refs = (wattn, att, q, k, v, cos, sin, n1, wqkv, tok)
    for ref in ((p_early, p_late, p_out) if plan else ()) + late_refs[:5]:
        ref.start()
    for c in weights:
        c.start()
    own_f.start()
    for ref in late_refs[5:]:
        ref.start()
    d_back = d_back.wait()

    def act(name):
        for f, *a in acts.get(name, ()):
            f(*a)

    wcat[...] = jnp.zeros_like(wcat)
    wcat[0:8] = wrT[...]
    wcat[8:12] = cmT[...]
    for kk in range(2):
        rb[kk] = jnp.transpose(jnp.broadcast_to(rT[kk : kk + 1, :].astype(F32), (128, length)))

    def chosen(rows, wide):
        slot = lax.broadcasted_iota(jnp.int32, (wide, slots), 1)
        r = slot // capacity
        e = jnp.zeros_like(slot)
        for n in range(experts):
            e = jnp.where(r == n, across(n), e)
        s_id = (slot - r * capacity + e * capacity).astype(F32)
        return meta[rows, 0:1] == s_id, meta[rows, 1:2] == s_id

    @pl.loop(0, length // 256)
    def _(i):
        rows = tile(i, 256)
        first, second = (c.astype(F32).astype(BF16) for c in chosen(rows, 256))
        dsn[rows] = dot(first + second, d_back[:, :, 0:width].reshape(slots, width))
        for n, c in enumerate((first, second)):
            dots[n, rows] = dot(c, d_back[:, :, width : width + 128].reshape(slots, 128))

    cot, res = cot.wait(), res.wait()
    w_high = wcat[...].astype(BF16)
    lnacc[...] = jnp.zeros_like(lnacc)

    @pl.loop(0, length // 64)
    def _(i):
        rows = tile(i, 64)
        lane = lax.broadcasted_iota(jnp.int32, (64, 128), 1)
        lane_f = lane.astype(F32)
        m = meta[rows]
        g0, g1, keep = m[:, 2:3], m[:, 3:4], m[:, 4:5]
        cg = (m[:, 5:6], m[:, 6:7])
        shares = ((m[:, 7:8], m[:, 8:9]), (m[:, 9:10], m[:, 10:11]))
        g = cot[rows].astype(F32)
        x = res[rows]
        r2 = lax.rsqrt(row_mean(x * x) + EPS)
        xr = x * r2
        n2 = xr * ln2[...]
        n2b[rows] = n2.astype(BF16)
        cv = (cvT[0:1, :], cvT[1:2, :])
        fk0[rows] = x + keep * n2 + (cg[0] * shares[0][1]) * cv[0] + (cg[1] * shares[1][1]) * cv[1]
        gn2 = jnp.sum(g * n2, axis=-1, keepdims=True)
        gcv = [jnp.sum(g * c, axis=-1, keepdims=True) for c in cv]
        hits = [(rb[kk, rows] == lane_f).astype(F32) for kk in range(2)]
        special = jnp.where(lane == 5, gn2, 0.0)
        for j in range(2):
            special = jnp.where(lane == 6 + j, shares[j][0] * gn2 + shares[j][1] * gcv[j], special)
        dg = [
            jnp.sum(h * special + jnp.where(lane < 2, dots[n, rows], 0.0), axis=-1, keepdims=True)
            for n, h in enumerate(hits)
        ]
        mean_dg = g0 * dg[0] + g1 * dg[1]
        dc0, dc1 = g0 * (dg[0] - mean_dg), g1 * (dg[1] - mean_dg)
        cat = hits[0] * dc0 + hits[1] * dc1
        for j in range(2):
            dm0, dm1 = cg[j] * gn2, cg[j] * gcv[j]
            mean_dm = shares[j][0] * dm0 + shares[j][1] * dm1
            cat = jnp.where(lane == 8 + 2 * j, shares[j][0] * (dm0 - mean_dm), cat)
            cat = jnp.where(lane == 9 + 2 * j, shares[j][1] * (dm1 - mean_dm), cat)
        dcat[rows, 0:128] = cat.astype(BF16)
        vecs = jnp.where(lane == 12, cg[0] * shares[0][1], 0.0)
        vecs = jnp.where(lane == 13, cg[1] * shares[1][1], vecs)
        dcat[rows, 128:256] = vecs.astype(BF16)
        dn2 = keep * g + dsn[rows] + dot(cat.astype(BF16), w_high)
        lnacc[0:8] += jnp.sum((dn2 * xr).reshape(8, 8, width), axis=0)
        dn = dn2 * ln2[...]
        dr = g + r2 * dn - xr * (r2 * r2) * row_mean(dn * x)
        dres[rows] = dr
        dbr[rows] = dr.astype(BF16)

    if plan:
        for ref in (p_early, p_late, p_out):
            ref.wait()
    act("token")
    wattn, att = wattn.wait(), att.wait()
    small = dot_tn(n2b[...], dcat[:, 0:128]) + dot_tn(cot[...], dcat[:, 128:256])
    small = small + jnp.where(
        lax.broadcasted_iota(jnp.int32, small.shape, 1) == 15, as_columns(lnacc[0:8]), 0.0
    )
    if plan:
        attn_slab.store(small, width)
    else:
        d_small[...] = small

    @pl.loop(0, width // 256)
    def _(j):
        cols = tile(j, 256)
        datt[:, cols] = dot_nt(dbr[...], wattn[cols, :]).astype(BF16)

    for j in range(width // 256):
        cols = slice(j * 256, (j + 1) * 256)
        d = dot_tn(att[...], dbr[:, cols])
        if plan:
            attn_slab.store(d, j * 256)
        else:
            d_attn[:, cols] = d
    act("attn")
    q, k, v, cos, sin, n1 = (ref.wait() for ref in (q, k, v, cos, sin, n1))
    for c in weights:
        c.wait()

    for part in range(3):

        @pl.loop(2 * part, 2 * part + 2)
        def _(j):
            cols = tile(j, 128)
            dkv[...] = jnp.zeros_like(dkv)
            for b in range(2):
                rows = slice(b * block, (b + 1) * block)
                nk = (b + 1) * block
                qlane = lax.broadcasted_iota(jnp.int32, (block, 128), 1)
                klane = lax.broadcasted_iota(jnp.int32, (nk, 128), 1)
                do = datt[rows, cols]
                prod = do.astype(F32) * att[rows, cols].astype(F32)
                dq = jnp.zeros((block, 128), F32)
                for h in range(2):
                    delta = jnp.sum(half_mask(prod, qlane, h), axis=-1, keepdims=True)
                    dom = half_mask(do, qlane, h)
                    dp = dot_nt(dom, v[0:nk, cols])
                    w = pw[2 * j + h, rows, 0:nk]
                    ds = (w.astype(F32) * (dp - delta)).astype(BF16)
                    dq = dq + dot(ds, half_mask(k[0:nk, cols], klane, h))
                    dkv[0, 0:nk] += dot_tn(ds, half_mask(q[rows, cols], qlane, h))
                    dkv[1, 0:nk] += dot_tn(w, dom)
                dproj[rows, cols] = rotate(dq * 0.125, cos[rows], -sin[rows]).astype(BF16)
            dproj[:, pl.ds(pl.multiple_of(width + j * 128, 128), 128)] = rotate(dkv[0], cos[...], -sin[...]).astype(BF16)
            dproj[:, pl.ds(pl.multiple_of(2 * width + j * 128, 128), 128)] = dkv[1].astype(BF16)

        for kind in range(3):
            cols = slice(kind * width + part * 256, kind * width + part * 256 + 256)
            d = dot_tn(n1[...], dproj[:, cols])
            if not plan:
                d_qkv[:, cols] = d
            elif part < 2:
                (q0, q1)[part].store(d, kind * 256)
            else:
                q2a.store(d[:, 0:128], kind * 128)
                q2b.store(d[:, 128:256], kind * 128)
        act(f"part{part}")

    wqkv = wqkv.wait()

    @pl.loop(0, width // 256)
    def _(j):
        cols = tile(j, 256)
        dsn[:, cols] = dot_nt(dproj[...], wqkv[cols, :])

    act("norm")
    tok = tok.wait()

    @pl.loop(0, length // 64)
    def _(i):
        rows = tile(i, 64)
        x = tok[rows].astype(F32)
        r1 = lax.rsqrt(row_mean(x * x) + EPS)
        xr = x * r1
        d = dsn[rows]
        dn = d * ln1[...]
        lnacc[8:16] += jnp.sum((d * xr).reshape(8, 8, width), axis=0)
        igrad[rows] = (dres[rows] + r1 * dn - xr * (r1 * r1) * row_mean(dn * x)).astype(BF16)

    ln1_grad = jnp.where(
        lax.broadcasted_iota(jnp.int32, (width, 128), 1) == 0, as_columns(lnacc[8:16]), 0.0
    )
    if plan:
        ln_slab.store(ln1_grad, 0)
    else:
        d_small[...] += jnp.where(lax.broadcasted_iota(jnp.int32, (width, 128), 1) == 14, as_columns(lnacc[8:16]), 0.0)
    igrad_s.start()
    act("input")

    own_f.wait()
    for c in f_copies.values():
        c.wait()

    @pl.loop(0, length // 256)
    def _(i):
        rows = tile(i, 256)
        first, second = chosen(rows, 256)
        mix = jnp.where(first, meta[rows, 2:3], jnp.where(second, meta[rows, 3:4], 0.0)).astype(BF16)
        out[rows] = (fk0[rows] + dot(mix, f_back[...].reshape(slots, width))).astype(BF16)

    out_s.start()
    act("output")
    out_s.wait()
    igrad_s.wait()
    if plan:
        g_in_s.start()
        g_out_s.start()
        g_in_s.wait()
        g_out_s.wait()


def shape(*s, dtype=BF16):
    return jax.ShapeDtypeStruct(s, dtype)


class Staged:
    def __init__(self, far, near, sem, out):
        self.far, self.near = far, near
        src, dst = (near, far) if out else (far, near)
        self.copy = lambda: pltpu.make_async_copy(src, dst, sem)

    def start(self):
        self.copy().start()

    def wait(self):
        self.copy().wait()
        return self.near


def call(kernel, outs, scratch, args, name, collective_id, far, staged):
    shapes = [jax.ShapeDtypeStruct(a.shape, a.dtype) for a in args] + list(outs)
    specs = [
        pl.BlockSpec(memory_space=pl.ANY if n in far or n in staged else pltpu.VMEM) for n in range(len(shapes))
    ]
    own = len(shapes) + len(scratch)
    extra = [pltpu.VMEM(shapes[n].shape, shapes[n].dtype) for n in staged]

    def wrapped(*refs):
        given, rest, near, sems = list(refs[: len(shapes)]), refs[len(shapes) : own], refs[own:-1], refs[-1]
        for i, n in enumerate(staged):
            given[n] = Staged(given[n], near[i], sems.at[i], n >= len(args))
        kernel(*given, *rest)

    return pl.pallas_call(
        wrapped,
        out_shape=outs,
        in_specs=specs[: len(args)],
        out_specs=specs[len(args) :],
        scratch_shapes=list(scratch) + extra + [pltpu.SemaphoreType.DMA((len(staged),))],
        compiler_params=pltpu.CompilerParams(
            vmem_limit_bytes=VMEM_LIMIT, has_side_effects=True, collective_id=collective_id
        ),
        name=name,
    )(*args)


def body(
    tokens, segments, routes, prev_logits, ln1_gain, w_qkv, w_attn, ln2_gain, w_router, const_mix, const_vec,
    expert_in, expert_out, cotangent,
):
    length, width = tokens.shape
    heads = width // HEAD_DIM
    experts = lax.axis_size("expert") * expert_in.shape[0]
    hidden = expert_out.shape[1]
    capacity = length // 2
    slots = experts * capacity
    n_dp = lax.axis_size("dp")
    V = pltpu.VMEM
    DMA = pltpu.SemaphoreType.DMA
    cos, sin = (jnp.asarray(t) for t in rotary_tables(length))
    rT, pT = routes.T, prev_logits.T
    wrT, cmT, cvT = w_router.T, const_mix.T, const_vec.T
    ln1, ln2 = ln1_gain.reshape(1, width), ln2_gain.reshape(1, width)
    peers = experts - 1

    q, k, v, pw, att, n1, res, meta, send, g_rows = call(
        fwd_kernel,
        [
            shape(length, width), shape(length, width), shape(length, width), shape(heads, length, length),
            shape(length, width), shape(length, width), shape(length, width, dtype=F32),
            shape(length, 128, dtype=F32), shape(experts, capacity, width + 128), shape(experts, capacity, width),
        ],
        [
            V((length, 256), F32), V((length, length), F32), V((128, width), F32), V((3, length, 128), F32),
            V((128, length), F32), V((length, width), BF16), V((length, width), BF16), V((2 * length, 128), BF16),
            V((length, 128), F32), V((slots, length), BF16), V((experts, capacity, width), BF16),
            DMA((peers,)), DMA((peers,)), V((heads, length, length), BF16), V((experts, capacity, width + 128), BF16),
            DMA((width // 128, 2)), DMA((experts + 1,)),
        ],
        (tokens, segments, rT, pT, ln1, w_qkv, w_attn, ln2, wrT, cmT, cotangent, cos, sin),
        "attention", 0, (16, 21, 22), (0, 5, 6, 10, 11, 12, 13, 14, 15, 17, 18, 19),
    )

    tiles, slabs = 4, 2
    ft = hidden // tiles
    within = n_dp == 8 and experts == 4
    stages = ((("dp", 1), ("dp", 2), ("dp", 4)), (("dp", 2), ("dp", 1), ("dp", 4))) if within else ()
    order = (("expert", 1), ("expert", 2), ("dp", 1), ("dp", 2), ("dp", 4))
    slab_in, slab_out = (2 * tiles, width, ft), (slabs, hidden, width // slabs)

    def part_of(s, n):
        return (s[0], s[1] // n, s[2])

    wide = width + 128
    late = (tiles, width // 2, ft)
    early = (tiles, width // 4, ft)
    f_rows, d_back, g_out, *g_in = call(
        functools.partial(expert_kernel, stages),
        [shape(experts, capacity, width), shape(experts, capacity, wide), shape(*slab_out)]
        + ([shape(*late), shape(*early)] if within else [shape(*slab_in)]),
        [
            V((experts, capacity, wide), BF16), V((slots, width), BF16), V((tiles, slots, ft), BF16),
            V((tiles, slots, 2 * ft), BF16), V((slots, width), F32), V((slots, width), F32),
            V((experts, capacity, wide), BF16),
        ]
        + ([V(slab_in, BF16), V(late, BF16)] + [DMA((2 * tiles,))] * 2 + [DMA((tiles,))] * 2 if within else [])
        + [DMA((peers,))] * 4
        + [DMA((2,))],
        (send, g_rows, expert_in, expert_out),
        "experts", 1, (0, 5), (1, 2, 3, 4, 6) + ((7, 8) if within else (7,)),
    )

    args = (
        tokens, cotangent, res, meta, rT, f_rows, d_back, q, k, v, pw, att, n1, ln1, w_qkv, w_attn, ln2, wrT, cmT, cvT,
        cos, sin,
    )
    n_all = n_dp * experts
    rows = width // n_all if within else width
    outs = [
        shape(length, width), shape(length, width), shape(rows, 3 * width, dtype=F32), shape(rows, width, dtype=F32),
        shape(rows, 128, dtype=F32),
    ]
    scratch = [
        V((128, width), F32), V((2, length, 128), F32), V((length, width), F32), V((length, width), F32),
        V((2, length, 128), F32), V((length, 256), BF16), V((length, width), BF16), V((length, width), F32),
        V((length, width), BF16), V((length, 3 * width), BF16), V((length, width), BF16),
        V((2, length, 128), F32), V((16, width), F32), V((experts, capacity, width), BF16), DMA((peers,)), DMA((peers,)),
        V((heads, length, length), BF16), DMA((3,)),
    ]
    if within:
        args += (g_in[1], g_in[0], g_out)
        outs += [
            shape(rows, 128, dtype=F32),
            shape(width // n_dp, 2 * hidden, dtype=F32), shape(hidden // n_dp, width, dtype=F32)]
        scratch += [
            V(early, BF16), V(part_of(slab_in, 8), BF16), V(part_of(slab_out, 2), BF16),
            V(part_of(slab_out, 4), BF16), V(part_of(slab_out, 8), BF16), DMA((2, 2 * tiles)), DMA((2, 2 * tiles)),
            DMA((3, slabs)), DMA((3, slabs)),
        ]
        for cols in (wide, width, width, width // 2, width // 2, 128):
            scratch += [V((width >> s, cols), BF16) for s in range(5)]
            scratch += [V((2 * rows, cols), F32), V((rows, cols), F32), DMA((5,)), DMA((5,))]
    plan = (stages, order) if within else ()
    n = len(args)
    staged = (0, 1, 2, 6, 7, 8, 9, 11, 12, 14, 15, 20, 21) + tuple(range(22, n)) + (n, n + 1)
    staged += (n + 6, n + 7) if within else ()
    done = call(functools.partial(bwd_kernel, plan), outs, scratch, args, "backward", 2, (5, 10), staged)
    out, igrad, d_qkv, d_attn, small = done[:5]
    if within:
        ln, g_in, g_out = done[5:]
        ln = ln[:, 0]
    else:
        (g_in,) = g_in
        g_in = jnp.moveaxis(g_in.reshape(tiles, 2, width, ft), 2, 0).transpose(0, 2, 1, 3).reshape(width, 2 * hidden)
        g_out = jnp.moveaxis(g_out, 0, 1).reshape(hidden, width)
        g_in = lax.psum_scatter(g_in, "dp", scatter_dimension=0, tiled=True).astype(F32)
        g_out = lax.psum_scatter(g_out, "dp", scatter_dimension=0, tiled=True).astype(F32)
        d_qkv, d_attn, small = (
            lax.psum_scatter(d, ("dp", "expert"), scatter_dimension=0, tiled=True) for d in (d_qkv, d_attn, small)
        )
        ln = small[:, 14]
    return (
        out, igrad, ln, d_qkv, d_attn, small[:, 15], small[:, 0:8], small[:, 8:12], small[:, 12:14],
        g_in[None], g_out[None],
    )


def solution(mesh):
    rows = P(("dp", "expert"), None)
    return jax.shard_map(
        body,
        mesh=mesh,
        in_specs=(
            rows, rows, rows, rows, P(), P(), P(), P(), P(), P(), P(),
            P("expert", None, None), P("expert", None, None), rows,
        ),
        out_specs=(
            rows, rows, P(("dp", "expert")), rows, rows, P(("dp", "expert")), rows, rows, rows,
            P("expert", "dp", None), P("expert", "dp", None),
        ),
        check_vma=False,
    )
```

```python
import functools
import math

import jax
import jax.numpy as jnp
import numpy as np
from jax import lax
from jax.experimental import pallas as pl
from jax.experimental.pallas import tpu as pltpu
from jax.sharding import PartitionSpec as P

HEAD_DIM = 64
EPS = 1e-06
MASKED = -1e30
F32 = jnp.float32
BF16 = jnp.bfloat16
VMEM_LIMIT = 62 * 1024 * 1024


def dot(a, b):
    return lax.dot_general(a, b, (((1,), (0,)), ((), ())), preferred_element_type=F32)


def dot_nt(a, b):
    return lax.dot_general(a, b, (((1,), (1,)), ((), ())), preferred_element_type=F32)


def dot_tn(a, b):
    return lax.dot_general(a, b, (((0,), (0,)), ((), ())), preferred_element_type=F32)


def tile(i, size):
    return pl.ds(pl.multiple_of(i * size, size), size)


def rotary_tables(length):
    half = HEAD_DIM // 2
    inverse = np.exp(np.arange(half, dtype=np.float32) * np.float32(-2.0 * math.log(10000.0) / HEAD_DIM))
    angles = np.arange(length, dtype=np.float32)[:, None] * inverse.astype(np.float32)[None, :]
    cos, sin = np.cos(angles), np.sin(angles)
    return (
        np.concatenate([cos] * 4, axis=1).astype(np.float32),
        np.concatenate([-sin, sin] * 2, axis=1).astype(np.float32),
    )


def rotate(x, cos, sin):
    lane = lax.broadcasted_iota(jnp.int32, x.shape, 1)
    front = (lane % HEAD_DIM) < HEAD_DIM // 2
    other = jnp.where(front, pltpu.roll(x, 96, 1), pltpu.roll(x, 32, 1))
    return x * cos + other * sin


def row_mean(x):
    return jnp.mean(x, axis=-1, keepdims=True)


def pick(x, lane, index):
    return jnp.sum(jnp.where(lane == index, x, 0.0), axis=-1, keepdims=True)


def half_mask(x, lane, which):
    keep = (lane < HEAD_DIM) if which == 0 else (lane >= HEAD_DIM)
    return jnp.where(keep, x, jnp.zeros_like(x))


MESH = pl.DeviceIdType.MESH


def flip(i, m):
    return i + m * (1 - 2 * ((i // m) % 2))


def side(mask):
    axis, m = mask
    return (lax.axis_index(axis) // m) % 2


def partner(mask):
    axis, m = mask
    return {axis: flip(lax.axis_index(axis), m)}


def across(r):
    e = lax.axis_index("expert")
    for m in (1, 2):
        if r & m:
            e = flip(e, m)
    return e


def greet(masks, peers=0):
    barrier = pltpu.get_barrier_semaphore()
    for mask in masks:
        pl.semaphore_signal(barrier, inc=1, device_id=partner(mask), device_id_type=MESH)
    for r in range(1, peers + 1):
        pl.semaphore_signal(barrier, inc=1, device_id={"expert": across(r)}, device_id_type=MESH)
    pl.semaphore_wait(barrier, len(masks) + peers)


def exchange(src, dst, send_sem, recv_sem):
    return {
        r: pltpu.make_async_remote_copy(
            src.at[r], dst.at[r], send_sem.at[r - 1], recv_sem.at[r - 1],
            device_id={"expert": across(r)}, device_id_type=MESH,
        )
        for r in range(src.shape[0] - 1, 0, -1)
    }


def half_copy(src, dst, mask, rows, send_sem, recv_sem):
    start = pl.multiple_of((1 - side(mask)) * rows, 16)
    return pltpu.make_async_remote_copy(
        src.at[pl.ds(start, rows)], dst, send_sem, recv_sem, device_id=partner(mask), device_id_type=MESH
    )


def half_add(src, dst, mask, rows, out=None):
    start = side(mask) * rows
    step = 48 if rows % 48 == 0 else 64
    out = dst if out is None else out

    @pl.loop(0, rows // step)
    def _(i):
        here = pl.ds(pl.multiple_of(i * step, 16), step)
        mine = src[pl.ds(pl.multiple_of(start + i * step, 16), step)].astype(F32)
        out[here] = (mine + dst[here].astype(F32)).astype(out.dtype)


def place_of(shard, masks):
    place = 0
    for m in masks:
        place = 2 * place + (shard // m) % 2
    return place


def fwd_kernel(
    tok, seg, rT, pT, ln1, wqkv, wattn, ln2, wrT, cmT, cot, cos, sin,
    q_out, k_out, v_out, pw_out, att_out, n1_out, res_out, meta, send_out, g_rows,
    proj, bias, wcat, rb, pb, n2b, n2l, gl, tg, onehot, g_out, send_sem, recv_sem, pw, send, pw_sem, row_sem,
):
    length, width = tok.near.shape
    capacity = length // 2
    experts = send.shape[0]

    for ref in (cot, tok, wqkv, cos, sin, wattn):
        ref.start()
    q, k, v, att, n1, res = (ref.near for ref in (q_out, k_out, v_out, att_out, n1_out, res_out))
    greet((), experts - 1)
    for kk in range(2):
        rb[kk] = jnp.transpose(jnp.broadcast_to(rT[kk : kk + 1, :].astype(F32), (128, length)))
    all_lane = lax.broadcasted_iota(jnp.int32, (length, 128), 1).astype(F32)
    count = ((rb[0] == all_lane).astype(F32) + (rb[1] == all_lane).astype(F32)).astype(BF16)

    @pl.loop(0, length // 128)
    def _(i):
        rows = tile(i, 128)
        lane = lax.broadcasted_iota(jnp.int32, (128, 128), 1)
        lane_f = lane.astype(F32)
        t_id = lax.broadcasted_iota(jnp.int32, (128, length), 0) + i * 128
        before = (t_id > lax.broadcasted_iota(jnp.int32, (128, length), 1)).astype(F32).astype(BF16)
        place = dot(before, count) + lane_f * float(capacity) + 1.0
        out = jnp.zeros((128, 128), F32)
        for kk in range(2):
            hit = (rb[kk, rows] == lane_f) & (lane < experts)
            out = jnp.where(lane == kk, jnp.sum(jnp.where(hit, place, 0.0), axis=-1, keepdims=True) - 1.0, out)
        tg[rows] = out

    target = jnp.transpose(tg[...])
    pb[...] = target

    cot = cot.wait()
    copies = exchange(g_out, g_rows, send_sem, recv_sem)
    own_rows = pltpu.make_async_copy(g_out.at[0], g_rows.at[0], row_sem.at[experts])
    for r in range(experts - 1, -1, -1):
        s_id = (lax.broadcasted_iota(jnp.int32, (capacity, length), 0) + across(r) * capacity).astype(F32)
        here = (pb[0:1] == s_id).astype(F32) + (pb[1:2] == s_id).astype(F32)
        onehot[r * capacity : (r + 1) * capacity] = here.astype(BF16)
        g_out[r] = dot(here.astype(BF16), cot[...]).astype(BF16)
        (copies[r] if r else own_rows).start()
    tok = tok.wait()

    @pl.loop(0, length // 64)
    def _(i):
        rows = tile(i, 64)
        x = tok[rows].astype(F32)
        r = lax.rsqrt(row_mean(x * x) + EPS)
        n1[rows] = (x * r * ln1[0:1]).astype(BF16)

    n1_out.start()
    wqkv, cos, sin = wqkv.wait(), cos.wait(), sin.wait()
    for kind, (dst, done) in enumerate(((q, q_out), (k, k_out), (v, v_out))):

        @pl.loop(0, width // 256)
        def _(j):
            cols = pl.ds(pl.multiple_of(kind * width + j * 256, 256), 256)
            proj[...] = dot(n1[...], wqkv[:, cols])

            @pl.loop(0, length // 128)
            def _(i):
                rows = tile(i, 128)
                for part in range(2):
                    x = proj[rows, part * 128 : part * 128 + 128]
                    if kind < 2:
                        x = rotate(x, cos[rows], sin[rows])
                    if kind == 0:
                        x = x * 0.125
                    dst[rows, pl.ds(pl.multiple_of(j * 256 + part * 128, 128), 128)] = x.astype(BF16)

        done.start()

    seg_f = seg[...].astype(F32)
    rb[2] = jnp.transpose(jnp.broadcast_to(seg_f, (128, length)))

    @pl.loop(0, length // 128)
    def _(i):
        rows = tile(i, 128)
        row_id = lax.broadcasted_iota(jnp.int32, (128, length), 0) + i * 128
        col_id = lax.broadcasted_iota(jnp.int32, (128, length), 1)
        same = rb[2, rows, 0:1] == seg_f
        bias[rows] = jnp.where(same & (row_id >= col_id), 0.0, MASKED)

    block = length // 2

    def weights_copy(j, b):
        at = (pl.ds(2 * j, 2), slice(b * block, (b + 1) * block), slice(0, (b + 1) * block))
        return pltpu.make_async_copy(pw.at[at], pw_out.at[at], pw_sem.at[j, b])

    @pl.loop(0, width // 128)
    def _(j):
        cols = tile(j, 128)
        for b in range(2):
            rows = slice(b * block, (b + 1) * block)
            nk = (b + 1) * block
            qlane = lax.broadcasted_iota(jnp.int32, (block, 128), 1)
            klane = lax.broadcasted_iota(jnp.int32, (nk, 128), 1)
            acc = jnp.zeros((block, 128), F32)
            for h in range(2):
                s = dot_nt(half_mask(q[rows, cols], qlane, h), k[0:nk, cols]) + bias[rows, 0:nk]
                m = jnp.max(s, axis=-1, keepdims=True)
                e = jnp.exp(s - m)
                w = (e * (1.0 / jnp.sum(e, axis=-1, keepdims=True))).astype(BF16)
                pw[2 * j + h, rows, 0:nk] = w
                acc = acc + dot(w, half_mask(v[0:nk, cols], klane, h))
            att[rows, cols] = acc.astype(BF16)
            weights_copy(j, b).start()

    att_out.start()
    wattn = wattn.wait()

    @pl.loop(0, width // 256)
    def _(j):
        cols = tile(j, 256)
        res[:, cols] = tok[:, cols].astype(F32) + dot(att[...], wattn[:, cols])

    res_out.start()

    @pl.loop(0, length // 64)
    def _(i):
        rows = tile(i, 64)
        x = res[rows]
        n2 = x * lax.rsqrt(row_mean(x * x) + EPS) * ln2[1:2]
        high = n2.astype(BF16)
        n2b[rows] = high
        n2l[rows] = (n2 - high.astype(F32)).astype(BF16)

    wcat[...] = jnp.zeros_like(wcat)
    wcat[0:8] = wrT[...]
    wcat[8:12] = cmT[...]
    w_high = wcat[...].astype(BF16)
    w_low = (wcat[...] - w_high.astype(F32)).astype(BF16)

    pb[8:16] = pT[...]
    rb[2] = jnp.transpose(jnp.concatenate([pb[8:16], jnp.zeros((120, length), F32)], axis=0))

    @pl.loop(0, length // 128)
    def _(i):
        rows = tile(i, 128)
        lane = lax.broadcasted_iota(jnp.int32, (128, 128), 1)
        lane_f = lane.astype(F32)
        high = n2b[rows]
        mixed = dot_nt(high, w_high) + dot_nt(high, w_low) + dot_nt(n2l[rows], w_high)
        logits = mixed + rb[2, rows]
        hits = [(rb[kk, rows] == lane_f).astype(F32) for kk in range(2)]
        chosen = [jnp.sum(h * logits, axis=-1, keepdims=True) for h in hits]
        top = jnp.maximum(chosen[0], chosen[1])
        e = [jnp.exp(c - top) for c in chosen]
        inv = 1.0 / (e[0] + e[1])
        gates = [v_ * inv for v_ in e]
        shares = []
        for j in range(2):
            a0, a1 = pick(mixed, lane, 8 + 2 * j), pick(mixed, lane, 9 + 2 * j)
            mx = jnp.maximum(a0, a1)
            b0, b1 = jnp.exp(a0 - mx), jnp.exp(a1 - mx)
            binv = 1.0 / (b0 + b1)
            shares.append((b0 * binv, b1 * binv))
        gate_sum = gates[0] * hits[0] + gates[1] * hits[1]
        cg = [pick(gate_sum, lane, 6), pick(gate_sum, lane, 7)]
        keep = pick(gate_sum, lane, 5) + cg[0] * shares[0][0] + cg[1] * shares[1][0]
        values = (
            gates[0], gates[1], keep, cg[0], cg[1], shares[0][0], shares[0][1], shares[1][0], shares[1][1],
        )
        out = tg[rows]
        for n, value in enumerate(values):
            out = jnp.where(lane == n + 2, value, out)
        meta[rows] = out
        for kk in range(2):
            g_high = gates[kk].astype(BF16).astype(F32)
            both = jnp.where(lane == 0, g_high, jnp.where(lane == 1, gates[kk] - g_high, 0.0))
            gl[pl.ds(pl.multiple_of(kk * length + i * 128, 128), 128)] = both.astype(BF16)

    @pl.loop(0, experts)
    def _(e):
        owner = flip(lax.axis_index("expert"), 1)
        owner = jnp.where(e % 2 == 1, owner, lax.axis_index("expert"))
        owner = jnp.where(e // 2 == 1, flip(owner, 2), owner)
        s_id = (lax.broadcasted_iota(jnp.int32, (capacity, length), 0) + owner * capacity).astype(F32)
        gate = jnp.zeros((capacity, 128), F32)
        for kk in range(2):
            here = (pb[kk : kk + 1] == s_id).astype(F32).astype(BF16)
            gate = gate + dot(here, gl[kk * length : (kk + 1) * length])
        send[e, :, 0:width] = dot(onehot[tile(e, capacity)], n2b[...]).astype(BF16)
        send[e, :, width : width + 128] = gate.astype(BF16)
        pltpu.make_async_copy(send.at[e], send_out.at[e], row_sem.at[e]).start()

    for ref in (q_out, k_out, v_out, att_out, n1_out, res_out):
        ref.wait()

    @pl.loop(0, width // 128)
    def _(j):
        for b in range(2):
            weights_copy(j, b).wait()

    @pl.loop(0, experts)
    def _(e):
        pltpu.make_async_copy(send.at[e], send_out.at[e], row_sem.at[e]).wait()

    own_rows.wait()
    for c in copies.values():
        c.wait()


def expert_kernel(stages, xs, g_rows, win, wout, *refs):
    f_out, d_back, go_out = refs[:3]
    f_rows, go = f_out.near, go_out.near
    if stages:
        late_out, early_out = refs[3:5]
        p_late, p_early = late_out.near, early_out.near
        refs = refs[5:]
    else:
        gi_out = refs[3]
        gi = gi_out.near
        refs = refs[4:]
    xr, dy, hid, dgu, f_acc, d_acc, d_out = refs[:7]
    refs = refs[7:]
    if stages:
        gi, p_first, in_send, in_recv, e_send, e_recv = refs[:6]
        refs = refs[6:]
    x_send, x_recv, d_send, d_recv, own_sem = refs
    groups, capacity, wide = xs.shape
    hidden, width = wout.near.shape[1:]
    tiles, rows_all, ft = hid.shape
    slabs = go.shape[0]
    shards = 2 ** len(stages[0]) if stages else 0
    near = rows_all // 2

    greet([s[0] for s in stages], groups - 1)
    copies = exchange(xs, xr, x_send, x_recv)
    for c in copies.values():
        c.start()
    own_x = pltpu.make_async_copy(xs.at[0], xr.at[0], own_sem.at[0])
    own_x.start()
    for ref in (g_rows, win, wout):
        ref.start()

    def gated(r):
        pair = xr[r, :, width:wide].astype(F32)
        lane = lax.broadcasted_iota(jnp.int32, pair.shape, 1)
        gate = jnp.sum(jnp.where(lane < 2, pair, 0.0), axis=-1, keepdims=True)
        dy[r * capacity : (r + 1) * capacity] = (g_rows[r].astype(F32) * gate).astype(BF16)

    def cols_of(f):
        return tile(f, ft), pl.ds(pl.multiple_of(hidden + f * ft, ft), ft)

    def work(f, part):
        gate_cols, up_cols = cols_of(f)
        rows = slice(part * near, (part + 1) * near)
        x = xr[2 * part : 2 * part + 2, :, 0:width].reshape(near, width)
        gate = dot(x, win[0, :, gate_cols])
        up = dot(x, win[0, :, up_cols])
        dh = dot_nt(dy[rows], wout[0, gate_cols, :])
        sig = 1.0 / (1.0 + jnp.exp(-gate))
        silu = gate * sig
        h = (silu * up).astype(BF16)
        da = (dh * up * (sig + silu * (1.0 - sig))).astype(BF16)
        db = (dh * silu).astype(BF16)
        hid[f, rows] = h
        dgu[f, rows, 0:ft] = da
        dgu[f, rows, ft : 2 * ft] = db
        y = dot(h, wout[0, gate_cols, :])
        d = dot_nt(da, win[0, :, gate_cols]) + dot_nt(db, win[0, :, up_cols])

        @pl.when(f == 0)
        def _():
            f_acc[rows] = y
            d_acc[rows] = d

        @pl.when(f > 0)
        def _():
            f_acc[rows] += y
            d_acc[rows] += d

    def in_copy(part, f, p):
        dst = (p_first if part == 0 else p_late).at[2 * (f - part * tiles // 2) + p]
        slab = 2 * f + p
        return half_copy(gi.at[slab], dst, stages[p][0], width // 2, in_send.at[slab], in_recv.at[slab]), dst

    def early_copy(slab):
        return half_copy(
            p_first.at[slab], p_early.at[slab], stages[slab % 2][1], width // 4, e_send.at[slab], e_recv.at[slab]
        )

    own_x.wait()
    g_rows = g_rows.wait()
    copies[1].wait()
    gated(0)
    gated(1)

    win, wout = win.wait(), wout.wait()

    @pl.loop(0, tiles)
    def _(f):
        work(f, 0)

    copies[3].wait()
    copies[2].wait()
    gated(2)
    gated(3)

    for part in range(2):

        @pl.loop(part * (tiles // 2), (part + 1) * (tiles // 2))
        def _(f):
            work(f, 1)
            for p in range(2):
                d = dot_tn(xr[:, :, 0:width].reshape(rows_all, width), dgu[f, :, p * ft : (p + 1) * ft])
                if not stages:
                    gi[2 * f + p] = d.astype(BF16)
                    continue
                size = width // shards
                for j in range(shards):
                    at = place_of(j, [m for _, m in stages[p]]) * size
                    gi[2 * f + p, at : at + size] = d[j * size : (j + 1) * size].astype(BF16)
                in_copy(part, f, p)[0].start()

    d_copies = exchange(d_out, d_back, d_send, d_recv)
    own_d = pltpu.make_async_copy(d_out.at[0], d_back.at[0], own_sem.at[1])
    for r in range(groups - 1, -1, -1):
        rows = slice(r * capacity, (r + 1) * capacity)
        y = f_acc[rows]
        f_rows[r] = y.astype(BF16)
        dots = jnp.sum(y * g_rows[r].astype(F32), axis=-1, keepdims=True)
        high = dots.astype(BF16).astype(F32)
        lane = lax.broadcasted_iota(jnp.int32, (capacity, 128), 1)
        extra = jnp.where(lane == 0, high, jnp.where(lane == 1, dots - high, 0.0)).astype(BF16)
        d_out[r, :, 0:width] = d_acc[rows].astype(BF16)
        d_out[r, :, width:wide] = extra
        (d_copies[r] if r else own_d).start()
    f_out.start()

    for c in range(slabs):
        cols = slice(c * (width // slabs), (c + 1) * (width // slabs))

        @pl.loop(0, tiles)
        def _(t):
            d = dot_tn(hid[t], dy[:, cols]).astype(BF16)
            if not stages:
                go[c, tile(t, ft)] = d
                return
            size = hidden // shards
            for i in range(ft // size):
                at = place_of(t * (ft // size) + i, [m for _, m in stages[0]])
                go[c, tile(at, size)] = d[i * size : (i + 1) * size]

    go_out.start()
    if stages:
        for part in range(2):
            for f in range(part * (tiles // 2), (part + 1) * (tiles // 2)):
                for p in range(2):
                    copy, dst = in_copy(part, f, p)
                    copy.wait()
                    half_add(gi.at[2 * f + p], dst, stages[p][0], width // 2)
                    if part == 0:
                        early_copy(2 * f + p).start()
        late_out.start()
        for slab in range(tiles):
            early_copy(slab).wait()
            half_add(p_first.at[slab], p_early.at[slab], stages[slab % 2][1], width // 4)
        early_out.start()
        late_out.wait()
        early_out.wait()
    else:
        gi_out.start()
        gi_out.wait()
    f_out.wait()
    go_out.wait()
    own_d.wait()
    for c in d_copies.values():
        c.wait()


def out_start(copy, i, s):
    copy(i, s).start()


def as_columns(x):
    row = jnp.sum(x, axis=0, keepdims=True)
    return jnp.transpose(jnp.broadcast_to(row, (128, row.shape[1])))


class Slab:
    def __init__(self, order, refs):
        self.order = order
        self.bufs, (self.send, self.recv) = refs[:6], refs[6:]
        self.bits = [m * (1 if a == "expert" else lax.axis_size("expert")) for a, m in order]
        self.out = ()

    def store(self, value, piece):
        total = 2 ** len(self.order)
        size = value.shape[0] // total
        for j in range(total):
            row = place_of(j, self.bits) * 2 * size
            mine = value[j * size : (j + 1) * size]
            both = jnp.concatenate([mine[:, 0:128], mine[:, 128:256]], axis=0)
            self.bufs[0][row : row + 2 * size, piece * 128 : piece * 128 + 128] = both.astype(BF16)

    def copy(self, s):
        dst = self.bufs[s + 1]
        return half_copy(self.bufs[s], dst, self.order[s], dst.shape[0], self.send.at[s], self.recv.at[s])

    def start(self):
        self.copy(0).start()

    def done(self, s):
        self.copy(s).wait()
        rows = self.bufs[s + 1].shape[0]
        if s < 4:
            half_add(self.bufs[s], self.bufs[s + 1], self.order[s], rows)
            self.copy(s + 1).start()
            return
        mine = self.bufs[4][pl.ds(pl.multiple_of(side(self.order[4]) * rows, 16), rows)]
        total = mine.astype(F32) + self.bufs[5][...].astype(F32)
        for piece, parts in enumerate(self.out):
            for n, (ref, at) in enumerate(parts):
                half = slice(n * rows // 2, (n + 1) * rows // 2)
                ref[:, at : at + 128] = total[half, piece * 128 : piece * 128 + 128]


def bwd_kernel(plan, *refs):
    (
        tok, cot, res, meta, rT, f_rows, d_back, q, k, v, pw_far, att, n1, ln1, wqkv, wattn, ln2, wrT, cmT, cvT, cos, sin,
    ) = refs[:22]
    refs = refs[22:]
    if plan:
        stages, order = plan
        p_early, p_late, p_out, out_s, igrad_s, d_qkv, d_attn, d_small, d_ln, g_in_s, g_out_s = refs[:11]
        g_in, g_out = g_in_s.near, g_out_s.near
        refs = refs[11:]
    else:
        out_s, igrad_s, d_qkv, d_attn, d_small = refs[:5]
        refs = refs[5:]
    out, igrad = out_s.near, igrad_s.near
    wcat, rb, fk0, dsn, dots, dcat, n2b, dres, dbr, dproj, datt, dkv, lnacc, f_back, f_send, f_recv, pw, own_sem = refs[:18]
    refs = refs[18:]
    length, width = tok.near.shape
    experts, capacity, _ = f_rows.shape
    slots = experts * capacity
    block = length // 2

    weights = []
    for b in range(2):
        at = (slice(0, pw.shape[0]), slice(b * block, (b + 1) * block), slice(0, (b + 1) * block))
        weights.append(pltpu.make_async_copy(pw_far.at[at], pw.at[at], own_sem.at[b]))
    own_f = pltpu.make_async_copy(f_rows.at[0], f_back.at[0], own_sem.at[2])
    for ref in (d_back, cot, res):
        ref.start()
    greet(order[2:] if plan else (), experts - 1)
    f_copies = exchange(f_rows, f_back, f_send, f_recv)

    acts = {}
    if plan:
        in1, in2, out0, out1, out2, in_send, in_recv, out_send, out_recv = refs[:9]
        slab_refs = [refs[9 + 8 * n : 17 + 8 * n] for n in range(6)]
        late = p_late.near.shape[0]
        slabs_in = late + p_early.near.shape[0]
        ft = p_late.near.shape[2]
        hidden = g_in.shape[1] // 2

        def in_refs(i, s, far=False):
            n = i - (slabs_in - late)
            p = "far" if far else "near"
            first = getattr(p_early, p).at[i] if n < 0 else in1.at[n]
            return (getattr(p_late, p).at[n], first) if s == 0 else (first, in2.at[i])

        def in_copy(i, s):
            src, dst = in_refs(i, s, True)
            return half_copy(src, dst, stages[i % 2][s + 1], dst.shape[0], in_send.at[s, i], in_recv.at[s, i])

        def in_done(i, s):
            in_copy(i, s).wait()
            src, dst = in_refs(i, s)
            if s == 0:
                half_add(src, dst, stages[i % 2][1], dst.shape[0])
                in_copy(i, 1).start()
            else:
                to = (i % 2) * hidden + (i // 2) * ft
                half_add(src, dst, stages[i % 2][2], dst.shape[0], g_in.at[:, to : to + ft])

        def out_refs(i, s, far=False):
            return ((p_out.far if far else p_out.near, out0), (out0, out1), (out1, out2))[s]

        def out_copy(i, s):
            src, dst = out_refs(i, s, True)
            return half_copy(
                src.at[i], dst.at[i], stages[0][s], dst.shape[1], out_send.at[s, i], out_recv.at[s, i]
            )

        def out_done(i, s):
            out_copy(i, s).wait()
            src, dst = out_refs(i, s)
            wide = out2.shape[2]
            into = g_out.at[:, i * wide : (i + 1) * wide] if s == 2 else None
            half_add(src.at[i], dst.at[i], stages[0][s], dst.shape[1], into)
            if s < 2:
                out_copy(i, s + 1).start()

        attn_slab, q0, q1, q2a, q2b, ln_slab = (Slab(order, r) for r in slab_refs)

        def columns(ref, at):
            return ((ref, at), (ref, at + 128))

        attn_slab.out = [columns(d_attn, 256 * n) for n in range(3)]
        q0.out = [columns(d_qkv, kind * width) for kind in range(3)]
        q1.out = [columns(d_qkv, kind * width + 256) for kind in range(3)]
        q2a.out = [columns(d_qkv, kind * width + 512) for kind in range(2)]
        q2b.out = [columns(d_qkv, 2 * width + 512)]
        ln_slab.out = [((d_ln, 0), (d_small, 0))]

        for i in (1, 2):
            in_copy(i, 1).start()
        out_copy(0, 0).start()
        in_copy(6, 0).start()
        in_copy(3, 1).start()
        out_copy(1, 0).start()
        acts = {
            "token": [(out_start, in_copy, 5, 0), (in_done, 1, 1)],
            "attn": [
                (out_start, in_copy, 0, 1), (out_start, in_copy, 4, 0), (attn_slab.start,), (in_done, 6, 0),
                (in_done, 2, 1),
            ],
            "part0": [(q0.start,), (in_done, 3, 1), (attn_slab.done, 0)],
            "part1": [
                (out_start, in_copy, 7, 0), (q1.start,), (in_done, 0, 1), (out_done, 0, 0), (in_done, 4, 0),
                (q0.done, 0),
            ],
            "part2": [(q2a.start,), (q2b.start,), (in_done, 6, 1), (q1.done, 0), (attn_slab.done, 1)],
            "norm": [(q2a.done, 0), (q2b.done, 0), (q0.done, 1), (out_done, 0, 1)],
            "input": [(ln_slab.start,), (in_done, 4, 1)],
            "output": [
                (out_done, 1, 0), (ln_slab.done, 0), (q1.done, 1), (in_done, 5, 0), (q2a.done, 1), (out_done, 0, 2),
                (in_done, 7, 0), (q2b.done, 1), (ln_slab.done, 1), (out_done, 1, 1), (attn_slab.done, 2),
                (in_done, 5, 1), (q0.done, 2), (in_done, 7, 1), (q1.done, 2), (q2a.done, 2), (q2b.done, 2),
                (attn_slab.done, 3), (ln_slab.done, 2), (q0.done, 3), (out_done, 1, 2), (q1.done, 3), (q2a.done, 3),
                (q2b.done, 3), (attn_slab.done, 4), (ln_slab.done, 3), (q0.done, 4), (q1.done, 4), (q2a.done, 4),
                (q2b.done, 4), (ln_slab.done, 4),
            ],
        }
    for c in f_copies.values():
        c.start()
    late_refs = (wattn, att, q, k, v, cos, sin, n1, wqkv, tok)
    for ref in ((p_early, p_late, p_out) if plan else ()) + late_refs[:5]:
        ref.start()
    for c in weights:
        c.start()
    own_f.start()
    for ref in late_refs[5:]:
        ref.start()
    d_back = d_back.wait()

    def act(name):
        for f, *a in acts.get(name, ()):
            f(*a)

    wcat[...] = jnp.zeros_like(wcat)
    wcat[0:8] = wrT[...]
    wcat[8:12] = cmT[...]
    for kk in range(2):
        rb[kk] = jnp.transpose(jnp.broadcast_to(rT[kk : kk + 1, :].astype(F32), (128, length)))

    def chosen(rows, wide):
        slot = lax.broadcasted_iota(jnp.int32, (wide, slots), 1)
        r = slot // capacity
        e = jnp.zeros_like(slot)
        for n in range(experts):
            e = jnp.where(r == n, across(n), e)
        s_id = (slot - r * capacity + e * capacity).astype(F32)
        return meta[rows, 0:1] == s_id, meta[rows, 1:2] == s_id

    @pl.loop(0, length // 256)
    def _(i):
        rows = tile(i, 256)
        first, second = (c.astype(F32).astype(BF16) for c in chosen(rows, 256))
        dsn[rows] = dot(first + second, d_back[:, :, 0:width].reshape(slots, width))
        for n, c in enumerate((first, second)):
            dots[n, rows] = dot(c, d_back[:, :, width : width + 128].reshape(slots, 128))

    cot, res = cot.wait(), res.wait()
    w_high = wcat[...].astype(BF16)
    lnacc[...] = jnp.zeros_like(lnacc)

    @pl.loop(0, length // 64)
    def _(i):
        rows = tile(i, 64)
        lane = lax.broadcasted_iota(jnp.int32, (64, 128), 1)
        lane_f = lane.astype(F32)
        m = meta[rows]
        g0, g1, keep = m[:, 2:3], m[:, 3:4], m[:, 4:5]
        cg = (m[:, 5:6], m[:, 6:7])
        shares = ((m[:, 7:8], m[:, 8:9]), (m[:, 9:10], m[:, 10:11]))
        g = cot[rows].astype(F32)
        x = res[rows]
        r2 = lax.rsqrt(row_mean(x * x) + EPS)
        xr = x * r2
        n2 = xr * ln2[1:2]
        n2b[rows] = n2.astype(BF16)
        cv = (cvT[0:1, :], cvT[1:2, :])
        fk0[rows] = x + keep * n2 + (cg[0] * shares[0][1]) * cv[0] + (cg[1] * shares[1][1]) * cv[1]
        gn2 = jnp.sum(g * n2, axis=-1, keepdims=True)
        gcv = [jnp.sum(g * c, axis=-1, keepdims=True) for c in cv]
        hits = [(rb[kk, rows] == lane_f).astype(F32) for kk in range(2)]
        special = jnp.where(lane == 5, gn2, 0.0)
        for j in range(2):
            special = jnp.where(lane == 6 + j, shares[j][0] * gn2 + shares[j][1] * gcv[j], special)
        dg = [
            jnp.sum(h * special + jnp.where(lane < 2, dots[n, rows], 0.0), axis=-1, keepdims=True)
            for n, h in enumerate(hits)
        ]
        mean_dg = g0 * dg[0] + g1 * dg[1]
        dc0, dc1 = g0 * (dg[0] - mean_dg), g1 * (dg[1] - mean_dg)
        cat = hits[0] * dc0 + hits[1] * dc1
        for j in range(2):
            dm0, dm1 = cg[j] * gn2, cg[j] * gcv[j]
            mean_dm = shares[j][0] * dm0 + shares[j][1] * dm1
            cat = jnp.where(lane == 8 + 2 * j, shares[j][0] * (dm0 - mean_dm), cat)
            cat = jnp.where(lane == 9 + 2 * j, shares[j][1] * (dm1 - mean_dm), cat)
        dcat[rows, 0:128] = cat.astype(BF16)
        vecs = jnp.where(lane == 12, cg[0] * shares[0][1], 0.0)
        vecs = jnp.where(lane == 13, cg[1] * shares[1][1], vecs)
        dcat[rows, 128:256] = vecs.astype(BF16)
        dn2 = keep * g + dsn[rows] + dot(cat.astype(BF16), w_high)
        lnacc[0:8] += jnp.sum((dn2 * xr).reshape(8, 8, width), axis=0)
        dn = dn2 * ln2[1:2]
        dr = g + r2 * dn - xr * (r2 * r2) * row_mean(dn * x)
        dres[rows] = dr
        dbr[rows] = dr.astype(BF16)

    if plan:
        for ref in (p_early, p_late, p_out):
            ref.wait()
    act("token")
    wattn, att = wattn.wait(), att.wait()
    @pl.loop(0, width // 256)
    def _(j):
        cols = tile(j, 256)
        datt[:, cols] = dot_nt(dbr[...], wattn[cols, :]).astype(BF16)

    for j in range(width // 256):
        cols = slice(j * 256, (j + 1) * 256)
        d = dot_tn(att[...], dbr[:, cols])
        if plan:
            attn_slab.store(d, j)
        else:
            d_attn[:, cols] = d
    act("attn")
    q, k, v, cos, sin, n1 = (ref.wait() for ref in (q, k, v, cos, sin, n1))
    for c in weights:
        c.wait()

    for part in range(3):

        @pl.loop(2 * part, 2 * part + 2)
        def _(j):
            cols = tile(j, 128)
            dkv[...] = jnp.zeros_like(dkv)
            for b in range(2):
                rows = slice(b * block, (b + 1) * block)
                nk = (b + 1) * block
                qlane = lax.broadcasted_iota(jnp.int32, (block, 128), 1)
                klane = lax.broadcasted_iota(jnp.int32, (nk, 128), 1)
                do = datt[rows, cols]
                prod = do.astype(F32) * att[rows, cols].astype(F32)
                dq = jnp.zeros((block, 128), F32)
                for h in range(2):
                    delta = jnp.sum(half_mask(prod, qlane, h), axis=-1, keepdims=True)
                    dom = half_mask(do, qlane, h)
                    dp = dot_nt(dom, v[0:nk, cols])
                    w = pw[2 * j + h, rows, 0:nk]
                    ds = (w.astype(F32) * (dp - delta)).astype(BF16)
                    dq = dq + dot(ds, half_mask(k[0:nk, cols], klane, h))
                    dkv[0, 0:nk] += dot_tn(ds, half_mask(q[rows, cols], qlane, h))
                    dkv[1, 0:nk] += dot_tn(w, dom)
                dproj[rows, cols] = rotate(dq * 0.125, cos[rows], -sin[rows]).astype(BF16)
            dproj[:, pl.ds(pl.multiple_of(width + j * 128, 128), 128)] = rotate(dkv[0], cos[...], -sin[...]).astype(BF16)
            dproj[:, pl.ds(pl.multiple_of(2 * width + j * 128, 128), 128)] = dkv[1].astype(BF16)

        for kind in range(3):
            cols = slice(kind * width + part * 256, kind * width + part * 256 + 256)
            d = dot_tn(n1[...], dproj[:, cols])
            if not plan:
                d_qkv[:, cols] = d
            elif part < 2:
                (q0, q1)[part].store(d, kind)
            elif kind < 2:
                q2a.store(d, kind)
            else:
                q2b.store(d, 0)
        act(f"part{part}")

    wqkv = wqkv.wait()

    @pl.loop(0, width // 256)
    def _(j):
        cols = tile(j, 256)
        dsn[:, cols] = dot_nt(dproj[...], wqkv[cols, :])

    act("norm")
    tok = tok.wait()

    @pl.loop(0, length // 64)
    def _(i):
        rows = tile(i, 64)
        x = tok[rows].astype(F32)
        r1 = lax.rsqrt(row_mean(x * x) + EPS)
        xr = x * r1
        d = dsn[rows]
        dn = d * ln1[0:1]
        lnacc[8:16] += jnp.sum((d * xr).reshape(8, 8, width), axis=0)
        igrad[rows] = (dres[rows] + r1 * dn - xr * (r1 * r1) * row_mean(dn * x)).astype(BF16)

    lanes = lax.broadcasted_iota(jnp.int32, (width, 128), 1)
    small = dot_tn(n2b[...], dcat[:, 0:128]) + dot_tn(cot[...], dcat[:, 128:256])
    small = small + jnp.where(lanes == 14, as_columns(lnacc[8:16]), 0.0)
    small = small + jnp.where(lanes == 15, as_columns(lnacc[0:8]), 0.0)
    if plan:
        ln_slab.store(jnp.concatenate([small, small], axis=1), 0)
    else:
        d_small[...] = small
    igrad_s.start()
    act("input")

    own_f.wait()
    for c in f_copies.values():
        c.wait()

    @pl.loop(0, length // 256)
    def _(i):
        rows = tile(i, 256)
        first, second = chosen(rows, 256)
        mix = jnp.where(first, meta[rows, 2:3], jnp.where(second, meta[rows, 3:4], 0.0)).astype(BF16)
        out[rows] = (fk0[rows] + dot(mix, f_back[...].reshape(slots, width))).astype(BF16)

    out_s.start()
    act("output")
    out_s.wait()
    igrad_s.wait()
    if plan:
        g_in_s.start()
        g_out_s.start()
        g_in_s.wait()
        g_out_s.wait()


def shape(*s, dtype=BF16):
    return jax.ShapeDtypeStruct(s, dtype)


class Staged:
    def __init__(self, far, near, sem, out):
        self.far, self.near = far, near
        src, dst = (near, far) if out else (far, near)
        self.copy = lambda: pltpu.make_async_copy(src, dst, sem)

    def start(self):
        self.copy().start()

    def wait(self):
        self.copy().wait()
        return self.near


def call(kernel, outs, scratch, args, name, collective_id, far, staged):
    shapes = [jax.ShapeDtypeStruct(a.shape, a.dtype) for a in args] + list(outs)
    specs = [
        pl.BlockSpec(memory_space=pl.ANY if n in far or n in staged else pltpu.VMEM) for n in range(len(shapes))
    ]
    own = len(shapes) + len(scratch)
    extra = [pltpu.VMEM(shapes[n].shape, shapes[n].dtype) for n in staged]

    def wrapped(*refs):
        given, rest, near, sems = list(refs[: len(shapes)]), refs[len(shapes) : own], refs[own:-1], refs[-1]
        for i, n in enumerate(staged):
            given[n] = Staged(given[n], near[i], sems.at[i], n >= len(args))
        kernel(*given, *rest)

    return pl.pallas_call(
        wrapped,
        out_shape=outs,
        in_specs=specs[: len(args)],
        out_specs=specs[len(args) :],
        scratch_shapes=list(scratch) + extra + [pltpu.SemaphoreType.DMA((len(staged),))],
        compiler_params=pltpu.CompilerParams(
            vmem_limit_bytes=VMEM_LIMIT, has_side_effects=True, collective_id=collective_id
        ),
        name=name,
    )(*args)


def final_kernel(n, *refs):
    src, small, dst = refs[:n], refs[n], refs[n + 1 : 2 * n + 1]
    router, mix, vec, ln1, ln2 = refs[2 * n + 1 : 2 * n + 6]
    near, sems = refs[2 * n + 6 : 3 * n + 6], refs[-1]
    loads = [pltpu.make_async_copy(a, b, sems.at[0, i]) for i, (a, b) in enumerate(zip(src, near))]
    copies = [pltpu.make_async_copy(a, b, sems.at[1, i]) for i, (a, b) in enumerate(zip(near, dst))]
    for c in loads:
        c.start()
    rows = small.shape[0]
    t = jnp.transpose(jnp.concatenate([small[...], jnp.zeros((128 - rows, 128), F32)], axis=0))[:, 0:rows]
    router[...] = t[0:8]
    mix[...] = t[8:12]
    vec[...] = t[12:14]
    ln1[...] = t[14:15]
    ln2[...] = t[15:16]
    for a, b in zip(loads, copies):
        a.wait()
        b.start()
    for c in copies:
        c.wait()


def final(big, small):
    rows = small.shape[0]
    far, near = pl.BlockSpec(memory_space=pl.ANY), pl.BlockSpec(memory_space=pltpu.VMEM)
    return pl.pallas_call(
        functools.partial(final_kernel, len(big)),
        out_shape=[jax.ShapeDtypeStruct(a.shape, a.dtype) for a in big]
        + [shape(n, rows, dtype=F32) for n in (8, 4, 2, 1, 1)],
        in_specs=[far] * len(big) + [near],
        out_specs=[far] * len(big) + [near] * 5,
        scratch_shapes=[pltpu.VMEM(a.shape, a.dtype) for a in big] + [pltpu.SemaphoreType.DMA((2, len(big)))],
        compiler_params=pltpu.CompilerParams(vmem_limit_bytes=VMEM_LIMIT),
        name="results",
    )(*big, small)


def body(
    tokens, segments, routes, prev_logits, ln1_gain, w_qkv, w_attn, ln2_gain, w_router, const_mix, const_vec,
    expert_in, expert_out, cotangent,
):
    length, width = tokens.shape
    heads = width // HEAD_DIM
    experts = lax.axis_size("expert") * expert_in.shape[0]
    hidden = expert_out.shape[1]
    capacity = length // 2
    slots = experts * capacity
    n_dp = lax.axis_size("dp")
    V = pltpu.VMEM
    DMA = pltpu.SemaphoreType.DMA
    cos, sin = (jnp.asarray(t) for t in rotary_tables(length))
    rT, pT = routes.T, prev_logits.T
    wrT, cmT, cvT = w_router.T, const_mix.T, const_vec.T
    gains = jnp.stack([ln1_gain, ln2_gain])
    ln1 = ln2 = gains
    peers = experts - 1

    q, k, v, pw, att, n1, res, meta, send, g_rows = call(
        fwd_kernel,
        [
            shape(length, width), shape(length, width), shape(length, width), shape(heads, length, length),
            shape(length, width), shape(length, width), shape(length, width, dtype=F32),
            shape(length, 128, dtype=F32), shape(experts, capacity, width + 128), shape(experts, capacity, width),
        ],
        [
            V((length, 256), F32), V((length, length), F32), V((128, width), F32), V((3, length, 128), F32),
            V((128, length), F32), V((length, width), BF16), V((length, width), BF16), V((2 * length, 128), BF16),
            V((length, 128), F32), V((slots, length), BF16), V((experts, capacity, width), BF16),
            DMA((peers,)), DMA((peers,)), V((heads, length, length), BF16), V((experts, capacity, width + 128), BF16),
            DMA((width // 128, 2)), DMA((experts + 1,)),
        ],
        (tokens, segments, rT, pT, ln1, w_qkv, w_attn, ln2, wrT, cmT, cotangent, cos, sin),
        "attention", 0, (16, 21, 22), (0, 5, 6, 10, 11, 12, 13, 14, 15, 17, 18, 19),
    )

    tiles, slabs = 4, 2
    ft = hidden // tiles
    within = n_dp == 8 and experts == 4
    stages = ((("dp", 1), ("dp", 2), ("dp", 4)), (("dp", 2), ("dp", 1), ("dp", 4))) if within else ()
    order = (("expert", 1), ("expert", 2), ("dp", 1), ("dp", 2), ("dp", 4))
    slab_in, slab_out = (2 * tiles, width, ft), (slabs, hidden, width // slabs)

    def part_of(s, n):
        return (s[0], s[1] // n, s[2])

    wide = width + 128
    late = (tiles, width // 2, ft)
    early = (tiles, width // 4, ft)
    f_rows, d_back, g_out, *g_in = call(
        functools.partial(expert_kernel, stages),
        [shape(experts, capacity, width), shape(experts, capacity, wide), shape(*slab_out)]
        + ([shape(*late), shape(*early)] if within else [shape(*slab_in)]),
        [
            V((experts, capacity, wide), BF16), V((slots, width), BF16), V((tiles, slots, ft), BF16),
            V((tiles, slots, 2 * ft), BF16), V((slots, width), F32), V((slots, width), F32),
            V((experts, capacity, wide), BF16),
        ]
        + ([V(slab_in, BF16), V(late, BF16)] + [DMA((2 * tiles,))] * 2 + [DMA((tiles,))] * 2 if within else [])
        + [DMA((peers,))] * 4
        + [DMA((2,))],
        (send, g_rows, expert_in, expert_out),
        "experts", 1, (0, 5), (1, 2, 3, 4, 6) + ((7, 8) if within else (7,)),
    )

    args = (
        tokens, cotangent, res, meta, rT, f_rows, d_back, q, k, v, pw, att, n1, ln1, w_qkv, w_attn, ln2, wrT, cmT, cvT,
        cos, sin,
    )
    n_all = n_dp * experts
    rows = width // n_all if within else width
    outs = [
        shape(length, width), shape(length, width), shape(rows, 3 * width, dtype=F32), shape(rows, width, dtype=F32),
        shape(rows, 128, dtype=F32),
    ]
    scratch = [
        V((128, width), F32), V((2, length, 128), F32), V((length, width), F32), V((length, width), F32),
        V((2, length, 128), F32), V((length, 256), BF16), V((length, width), BF16), V((length, width), F32),
        V((length, width), BF16), V((length, 3 * width), BF16), V((length, width), BF16),
        V((2, length, 128), F32), V((16, width), F32), V((experts, capacity, width), BF16), DMA((peers,)), DMA((peers,)),
        V((heads, length, length), BF16), DMA((3,)),
    ]
    if within:
        args += (g_in[1], g_in[0], g_out)
        outs += [
            shape(rows, 128, dtype=F32),
            shape(width // n_dp, 2 * hidden, dtype=F32), shape(hidden // n_dp, width, dtype=F32)]
        scratch += [
            V(early, BF16), V(part_of(slab_in, 8), BF16), V(part_of(slab_out, 2), BF16),
            V(part_of(slab_out, 4), BF16), V(part_of(slab_out, 8), BF16), DMA((2, 2 * tiles)), DMA((2, 2 * tiles)),
            DMA((3, slabs)), DMA((3, slabs)),
        ]
        for cols in (width, width, width, 512, 256, 256):
            scratch += [V((2 * width >> s, cols // 2), BF16) for s in range(6)] + [DMA((5,)), DMA((5,))]
    plan = (stages, order) if within else ()
    n = len(args)
    staged = (0, 1, 2, 6, 7, 8, 9, 11, 12, 14, 15, 20, 21) + tuple(range(22, n)) + (n, n + 1)
    staged += (n + 6, n + 7) if within else ()
    done = call(functools.partial(bwd_kernel, plan), outs, scratch, args, "backward", 2, (5, 10), staged)
    out, igrad, d_qkv, d_attn, small = done[:5]
    if within:
        out, igrad, d_qkv, d_attn, g_in, g_out, router, mix, vec, ln_one, ln_two = final(
            (out, igrad, d_qkv, d_attn, done[6], done[7]), small
        )
        return (
            out, igrad, ln_one.reshape(rows), d_qkv, d_attn, ln_two.reshape(rows), router.T, mix.T, vec.T,
            g_in[None], g_out[None],
        )
    (g_in,) = g_in
    g_in = jnp.moveaxis(g_in.reshape(tiles, 2, width, ft), 2, 0).transpose(0, 2, 1, 3).reshape(width, 2 * hidden)
    g_out = jnp.moveaxis(g_out, 0, 1).reshape(hidden, width)
    g_in = lax.psum_scatter(g_in, "dp", scatter_dimension=0, tiled=True).astype(F32)
    g_out = lax.psum_scatter(g_out, "dp", scatter_dimension=0, tiled=True).astype(F32)
    d_qkv, d_attn, small = (
        lax.psum_scatter(d, ("dp", "expert"), scatter_dimension=0, tiled=True) for d in (d_qkv, d_attn, small)
    )
    return (
        out, igrad, small[:, 14], d_qkv, d_attn, small[:, 15], small[:, 0:8], small[:, 8:12], small[:, 12:14],
        g_in[None], g_out[None],
    )


def solution(mesh):
    rows = P(("dp", "expert"), None)
    return jax.shard_map(
        body,
        mesh=mesh,
        in_specs=(
            rows, rows, rows, rows, P(), P(), P(), P(), P(), P(), P(),
            P("expert", None, None), P("expert", None, None), rows,
        ),
        out_specs=(
            rows, rows, P(("dp", "expert")), rows, rows, P(("dp", "expert")), rows, rows, rows,
            P("expert", "dp", None), P("expert", "dp", None),
        ),
        check_vma=False,
    )
```

```python
import functools
import math

import jax
import jax.numpy as jnp
import numpy as np
from jax import lax
from jax.experimental import pallas as pl
from jax.experimental.pallas import tpu as pltpu
from jax.sharding import PartitionSpec as P

HEAD_DIM = 64
EPS = 1e-06
MASKED = -1e30
F32 = jnp.float32
BF16 = jnp.bfloat16
VMEM_LIMIT = 62 * 1024 * 1024


def dot(a, b):
    return lax.dot_general(a, b, (((1,), (0,)), ((), ())), preferred_element_type=F32)


def dot_nt(a, b):
    return lax.dot_general(a, b, (((1,), (1,)), ((), ())), preferred_element_type=F32)


def dot_tn(a, b):
    return lax.dot_general(a, b, (((0,), (0,)), ((), ())), preferred_element_type=F32)


def tile(i, size):
    return pl.ds(pl.multiple_of(i * size, size), size)


def rotary_tables(length):
    half = HEAD_DIM // 2
    inverse = np.exp(np.arange(half, dtype=np.float32) * np.float32(-2.0 * math.log(10000.0) / HEAD_DIM))
    angles = np.arange(length, dtype=np.float32)[:, None] * inverse.astype(np.float32)[None, :]
    cos, sin = np.cos(angles), np.sin(angles)
    return (
        np.concatenate([cos] * 4, axis=1).astype(np.float32),
        np.concatenate([-sin, sin] * 2, axis=1).astype(np.float32),
    )


def rotate(x, cos, sin):
    lane = lax.broadcasted_iota(jnp.int32, x.shape, 1)
    front = (lane % HEAD_DIM) < HEAD_DIM // 2
    other = jnp.where(front, pltpu.roll(x, 96, 1), pltpu.roll(x, 32, 1))
    return x * cos + other * sin


def row_mean(x):
    return jnp.mean(x, axis=-1, keepdims=True)


def pick(x, lane, index):
    return jnp.sum(jnp.where(lane == index, x, 0.0), axis=-1, keepdims=True)


def half_mask(x, lane, which):
    keep = (lane < HEAD_DIM) if which == 0 else (lane >= HEAD_DIM)
    return jnp.where(keep, x, jnp.zeros_like(x))


MESH = pl.DeviceIdType.MESH


def flip(i, m):
    return i + m * (1 - 2 * ((i // m) % 2))


def side(mask):
    axis, m = mask
    return (lax.axis_index(axis) // m) % 2


def partner(mask):
    axis, m = mask
    return {axis: flip(lax.axis_index(axis), m)}


def across(r):
    e = lax.axis_index("expert")
    for m in (1, 2):
        if r & m:
            e = flip(e, m)
    return e


def greet(masks, peers=0):
    barrier = pltpu.get_barrier_semaphore()
    for mask in masks:
        pl.semaphore_signal(barrier, inc=1, device_id=partner(mask), device_id_type=MESH)
    for r in range(1, peers + 1):
        pl.semaphore_signal(barrier, inc=1, device_id={"expert": across(r)}, device_id_type=MESH)
    pl.semaphore_wait(barrier, len(masks) + peers)


def exchange(src, dst, send_sem, recv_sem):
    return {
        r: pltpu.make_async_remote_copy(
            src.at[r], dst.at[r], send_sem.at[r - 1], recv_sem.at[r - 1],
            device_id={"expert": across(r)}, device_id_type=MESH,
        )
        for r in range(src.shape[0] - 1, 0, -1)
    }


def half_copy(src, dst, mask, rows, send_sem, recv_sem):
    start = pl.multiple_of((1 - side(mask)) * rows, 16)
    return pltpu.make_async_remote_copy(
        src.at[pl.ds(start, rows)], dst, send_sem, recv_sem, device_id=partner(mask), device_id_type=MESH
    )


def half_add(src, dst, mask, rows, out=None):
    start = side(mask) * rows
    step = 48 if rows % 48 == 0 else 64
    out = dst if out is None else out

    @pl.loop(0, rows // step)
    def _(i):
        here = pl.ds(pl.multiple_of(i * step, 16), step)
        mine = src[pl.ds(pl.multiple_of(start + i * step, 16), step)].astype(F32)
        out[here] = (mine + dst[here].astype(F32)).astype(out.dtype)


def place_of(shard, masks):
    place = 0
    for m in masks:
        place = 2 * place + (shard // m) % 2
    return place


def fwd_kernel(
    tok, seg, rT, pT, ln1, wqkv, wattn, ln2, wrT, cmT, cot, cos, sin,
    q_out, k_out, v_out, pw_out, att_out, n1_out, res_out, meta, send_out, g_rows, gate_row,
    bias, wcat, rb, pb, n2b, n2l, tg, onehot, g_out, send_sem, recv_sem, pw, send, pw_sem, row_sem,
):
    length, width = tok.near.shape
    capacity = length // 2
    experts = send.shape[0]

    for ref in (cot, tok, wqkv, cos, sin, wattn):
        ref.start()
    q, k, v, att, n1, res = (ref.near for ref in (q_out, k_out, v_out, att_out, n1_out, res_out))
    greet((), experts - 1)
    for kk in range(2):
        rb[kk] = jnp.transpose(jnp.broadcast_to(rT[kk : kk + 1, :].astype(F32), (128, length)))
    all_lane = lax.broadcasted_iota(jnp.int32, (length, 128), 1).astype(F32)
    count = ((rb[0] == all_lane).astype(F32) + (rb[1] == all_lane).astype(F32)).astype(BF16)

    @pl.loop(0, length // 128)
    def _(i):
        rows = tile(i, 128)
        lane = lax.broadcasted_iota(jnp.int32, (128, 128), 1)
        lane_f = lane.astype(F32)
        t_id = lax.broadcasted_iota(jnp.int32, (128, length), 0) + i * 128
        before = (t_id > lax.broadcasted_iota(jnp.int32, (128, length), 1)).astype(F32).astype(BF16)
        place = dot(before, count) + lane_f * float(capacity) + 1.0
        out = jnp.zeros((128, 128), F32)
        for kk in range(2):
            hit = (rb[kk, rows] == lane_f) & (lane < experts)
            out = jnp.where(lane == kk, jnp.sum(jnp.where(hit, place, 0.0), axis=-1, keepdims=True) - 1.0, out)
        tg[rows] = out

    target = jnp.transpose(tg[...])
    pb[...] = target

    cot = cot.wait()
    copies = exchange(g_out, g_rows, send_sem, recv_sem)
    own_rows = pltpu.make_async_copy(g_out.at[0], g_rows.at[0], row_sem.at[experts])
    for r in range(experts - 1, -1, -1):
        s_id = (lax.broadcasted_iota(jnp.int32, (capacity, length), 0) + across(r) * capacity).astype(F32)
        here = (pb[0:1] == s_id).astype(F32) + (pb[1:2] == s_id).astype(F32)
        onehot[r * capacity : (r + 1) * capacity] = here.astype(BF16)
        g_out[r] = dot(here.astype(BF16), cot[...]).astype(BF16)
        (copies[r] if r else own_rows).start()
    tok = tok.wait()

    @pl.loop(0, length // 256)
    def _(i):
        rows = tile(i, 256)
        x = tok[rows].astype(F32)
        r = lax.rsqrt(row_mean(x * x) + EPS)
        n1[rows] = (x * r * ln1[0:1]).astype(BF16)

    n1_out.start()
    wqkv, cos, sin = wqkv.wait(), cos.wait(), sin.wait()

    @pl.loop(0, width // 256)
    def _(j):
        for kind, dst in enumerate((q, k, v)):
            cols = pl.ds(pl.multiple_of(kind * width + j * 256, 256), 256)
            both = dot(n1[...], wqkv[:, cols])
            for part in range(2):
                x = both[:, part * 128 : part * 128 + 128]
                if kind < 2:
                    x = rotate(x, cos[...], sin[...])
                if kind == 0:
                    x = x * 0.125
                dst[:, pl.ds(pl.multiple_of(j * 256 + part * 128, 128), 128)] = x.astype(BF16)

    for done in (q_out, k_out, v_out):
        done.start()

    seg_f = seg[...].astype(F32)
    rb[2] = jnp.transpose(jnp.broadcast_to(seg_f, (128, length)))

    @pl.loop(0, length // 128)
    def _(i):
        rows = tile(i, 128)
        row_id = lax.broadcasted_iota(jnp.int32, (128, length), 0) + i * 128
        col_id = lax.broadcasted_iota(jnp.int32, (128, length), 1)
        same = rb[2, rows, 0:1] == seg_f
        bias[rows] = jnp.where(same & (row_id >= col_id), 0.0, MASKED)

    block = length // 2

    def weights_copy(j, b):
        at = (pl.ds(2 * j, 2), slice(b * block, (b + 1) * block), slice(0, (b + 1) * block))
        return pltpu.make_async_copy(pw.at[at], pw_out.at[at], pw_sem.at[j, b])

    def heads(j):
        cols = tile(j, 128)
        for b in range(2):
            rows = slice(b * block, (b + 1) * block)
            nk = (b + 1) * block
            qlane = lax.broadcasted_iota(jnp.int32, (block, 128), 1)
            klane = lax.broadcasted_iota(jnp.int32, (nk, 128), 1)
            acc = jnp.zeros((block, 128), F32)
            for h in range(2):
                s = dot_nt(half_mask(q[rows, cols], qlane, h), k[0:nk, cols]) + bias[rows, 0:nk]
                m = jnp.max(s, axis=-1, keepdims=True)
                e = jnp.exp(s - m)
                w = (e * (1.0 / jnp.sum(e, axis=-1, keepdims=True))).astype(BF16)
                pw[2 * j + h, rows, 0:nk] = w
                acc = acc + dot(w, half_mask(v[0:nk, cols], klane, h))
            att[rows, cols] = acc.astype(BF16)
            weights_copy(j, b).start()

    @pl.loop(0, width // 256)
    def _(jj):
        heads(2 * jj)
        heads(2 * jj + 1)

    att_out.start()
    wattn = wattn.wait()

    res[...] = tok[...].astype(F32) + dot(att[...], wattn[...])

    res_out.start()

    @pl.loop(0, length // 256)
    def _(i):
        rows = tile(i, 256)
        x = res[rows]
        n2 = x * lax.rsqrt(row_mean(x * x) + EPS) * ln2[1:2]
        high = n2.astype(BF16)
        n2b[rows] = high
        n2l[rows] = (n2 - high.astype(F32)).astype(BF16)

    wcat[...] = jnp.zeros_like(wcat)
    wcat[0:8] = wrT[...]
    wcat[8:12] = cmT[...]
    w_high = wcat[...].astype(BF16)
    w_low = (wcat[...] - w_high.astype(F32)).astype(BF16)

    pb[8:16] = pT[...]
    rb[2] = jnp.transpose(jnp.concatenate([pb[8:16], jnp.zeros((120, length), F32)], axis=0))

    @pl.loop(0, length // 128)
    def _(i):
        rows = tile(i, 128)
        lane = lax.broadcasted_iota(jnp.int32, (128, 128), 1)
        lane_f = lane.astype(F32)
        high = n2b[rows]
        mixed = dot_nt(high, w_high) + dot_nt(high, w_low) + dot_nt(n2l[rows], w_high)
        logits = mixed + rb[2, rows]
        hits = [(rb[kk, rows] == lane_f).astype(F32) for kk in range(2)]
        chosen = [jnp.sum(h * logits, axis=-1, keepdims=True) for h in hits]
        top = jnp.maximum(chosen[0], chosen[1])
        e = [jnp.exp(c - top) for c in chosen]
        inv = 1.0 / (e[0] + e[1])
        gates = [v_ * inv for v_ in e]
        shares = []
        for j in range(2):
            a0, a1 = pick(mixed, lane, 8 + 2 * j), pick(mixed, lane, 9 + 2 * j)
            mx = jnp.maximum(a0, a1)
            b0, b1 = jnp.exp(a0 - mx), jnp.exp(a1 - mx)
            binv = 1.0 / (b0 + b1)
            shares.append((b0 * binv, b1 * binv))
        gate_sum = gates[0] * hits[0] + gates[1] * hits[1]
        cg = [pick(gate_sum, lane, 6), pick(gate_sum, lane, 7)]
        keep = pick(gate_sum, lane, 5) + cg[0] * shares[0][0] + cg[1] * shares[1][0]
        values = (
            gates[0], gates[1], keep, cg[0], cg[1], shares[0][0], shares[0][1], shares[1][0], shares[1][1],
        )
        out = tg[rows]
        for n, value in enumerate(values):
            out = jnp.where(lane == n + 2, value, out)
        meta[rows] = out

    @pl.loop(0, experts)
    def _(e):
        owner = flip(lax.axis_index("expert"), 1)
        owner = jnp.where(e % 2 == 1, owner, lax.axis_index("expert"))
        owner = jnp.where(e // 2 == 1, flip(owner, 2), owner)
        slot = (lax.broadcasted_iota(jnp.int32, (length, capacity), 1) + owner * capacity).astype(F32)
        gate = jnp.where(meta[:, 0:1] == slot, meta[:, 2:3], jnp.where(meta[:, 1:2] == slot, meta[:, 3:4], 0.0))
        gate_row[e] = jnp.broadcast_to(jnp.sum(gate, axis=0, keepdims=True), (8, capacity))
        send[e] = dot(onehot[tile(e, capacity)], n2b[...]).astype(BF16)
        pltpu.make_async_copy(send.at[e], send_out.at[e], row_sem.at[e]).start()

    for ref in (q_out, k_out, v_out, att_out, n1_out, res_out):
        ref.wait()

    @pl.loop(0, width // 128)
    def _(j):
        for b in range(2):
            weights_copy(j, b).wait()

    @pl.loop(0, experts)
    def _(e):
        pltpu.make_async_copy(send.at[e], send_out.at[e], row_sem.at[e]).wait()

    own_rows.wait()
    for c in copies.values():
        c.wait()


def expert_kernel(stages, xs, g_rows, win, wout, gate_row, *refs):
    f_out, d_back, go_out, dot_back = refs[:4]
    refs = refs[:3] + refs[4:]
    f_rows, go = f_out.near, go_out.near
    if stages:
        late_out, early_out = refs[3:5]
        p_late, p_early = late_out.near, early_out.near
        refs = refs[5:]
    else:
        gi_out = refs[3]
        gi = gi_out.near
        refs = refs[4:]
    xr, dy, hid, dgu, f_acc, d_acc, d_out = refs[:7]
    refs = refs[7:]
    if stages:
        gi, p_first, in_send, in_recv, e_send, e_recv = refs[:6]
        refs = refs[6:]
    x_send, x_recv, d_send, d_recv, own_sem, gates, dot_row, r_send, r_recv, s_send, s_recv = refs
    groups, capacity, _ = xs.shape
    hidden, width = wout.near.shape[1:]
    tiles, rows_all, ft = hid.shape
    slabs = go.shape[0]
    shards = 2 ** len(stages[0]) if stages else 0
    near = rows_all // 2

    greet([s[0] for s in stages], groups - 1)
    copies = exchange(xs, xr, x_send, x_recv)
    row_copies = exchange(gate_row, gates, r_send, r_recv)
    for r, c in copies.items():
        row_copies[r].start()
        c.start()
    gates[0] = gate_row[0]
    own_x = pltpu.make_async_copy(xs.at[0], xr.at[0], own_sem.at[0])
    own_x.start()
    for ref in (g_rows, win, wout):
        ref.start()

    def gated(r):
        if r:
            row_copies[r].wait()
            copies[r].wait()
        gate = jnp.transpose(jnp.broadcast_to(gates[r, 0:1], (128, capacity)))[:, 0:1]
        dy[r * capacity : (r + 1) * capacity] = (g_rows[r].astype(F32) * gate).astype(BF16)

    def cols_of(f):
        return tile(f, ft), pl.ds(pl.multiple_of(hidden + f * ft, ft), ft)

    def work(f, part):
        gate_cols, up_cols = cols_of(f)
        rows = slice(part * near, (part + 1) * near)
        x = xr[2 * part : 2 * part + 2].reshape(near, width)
        gate = dot(x, win[0, :, gate_cols])
        up = dot(x, win[0, :, up_cols])
        dh = dot_nt(dy[rows], wout[0, gate_cols, :])
        sig = 1.0 / (1.0 + jnp.exp(-gate))
        silu = gate * sig
        h = (silu * up).astype(BF16)
        da = (dh * up * (sig + silu * (1.0 - sig))).astype(BF16)
        db = (dh * silu).astype(BF16)
        hid[f, rows] = h
        dgu[f, rows, 0:ft] = da
        dgu[f, rows, ft : 2 * ft] = db
        y = dot(h, wout[0, gate_cols, :])
        d = dot_nt(da, win[0, :, gate_cols]) + dot_nt(db, win[0, :, up_cols])

        @pl.when(f == 0)
        def _():
            f_acc[rows] = y
            d_acc[rows] = d

        @pl.when(f > 0)
        def _():
            f_acc[rows] += y
            d_acc[rows] += d

    def in_copy(part, f, p):
        dst = (p_first if part == 0 else p_late).at[2 * (f - part * tiles // 2) + p]
        slab = 2 * f + p
        return half_copy(gi.at[slab], dst, stages[p][0], width // 2, in_send.at[slab], in_recv.at[slab]), dst

    def early_copy(slab):
        return half_copy(
            p_first.at[slab], p_early.at[slab], stages[slab % 2][1], width // 4, e_send.at[slab], e_recv.at[slab]
        )

    own_x.wait()
    g_rows = g_rows.wait()
    gated(0)
    gated(1)

    win, wout = win.wait(), wout.wait()

    @pl.loop(0, tiles)
    def _(f):
        work(f, 0)

    gated(3)
    gated(2)

    for part in range(2):

        @pl.loop(part * (tiles // 2), (part + 1) * (tiles // 2))
        def _(f):
            work(f, 1)
            for p in range(2):
                d = dot_tn(xr[...].reshape(rows_all, width), dgu[f, :, p * ft : (p + 1) * ft])
                if not stages:
                    gi[2 * f + p] = d.astype(BF16)
                    continue
                size = width // shards
                for j in range(shards):
                    at = place_of(j, [m for _, m in stages[p]]) * size
                    gi[2 * f + p, at : at + size] = d[j * size : (j + 1) * size].astype(BF16)
                in_copy(part, f, p)[0].start()

    d_copies = exchange(d_out, d_back, d_send, d_recv)
    dot_copies = exchange(dot_row, dot_back, s_send, s_recv)
    own_d = pltpu.make_async_copy(d_out.at[0], d_back.at[0], own_sem.at[1])
    for r in range(groups - 1, -1, -1):
        rows = slice(r * capacity, (r + 1) * capacity)
        y = f_acc[rows]
        f_rows[r] = y.astype(BF16)
        dots = jnp.sum(y * g_rows[r].astype(F32), axis=-1, keepdims=True)
        as_rows = jnp.transpose(jnp.broadcast_to(dots, (capacity, 128)))[0:8]
        d_out[r] = d_acc[rows].astype(BF16)
        if r:
            dot_row[r] = as_rows
            dot_copies[r].start()
            d_copies[r].start()
        else:
            dot_back[0] = as_rows
            own_d.start()
    f_out.start()

    for c in range(slabs):
        cols = slice(c * (width // slabs), (c + 1) * (width // slabs))

        @pl.loop(0, tiles)
        def _(t):
            d = dot_tn(hid[t], dy[:, cols]).astype(BF16)
            if not stages:
                go[c, tile(t, ft)] = d
                return
            size = hidden // shards
            for i in range(ft // size):
                at = place_of(t * (ft // size) + i, [m for _, m in stages[0]])
                go[c, tile(at, size)] = d[i * size : (i + 1) * size]

    go_out.start()
    if stages:
        for part in range(2):
            for f in range(part * (tiles // 2), (part + 1) * (tiles // 2)):
                for p in range(2):
                    copy, dst = in_copy(part, f, p)
                    copy.wait()
                    half_add(gi.at[2 * f + p], dst, stages[p][0], width // 2)
                    if part == 0:
                        early_copy(2 * f + p).start()
        late_out.start()
        for slab in range(tiles):
            early_copy(slab).wait()
            half_add(p_first.at[slab], p_early.at[slab], stages[slab % 2][1], width // 4)
        early_out.start()
        late_out.wait()
        early_out.wait()
    else:
        gi_out.start()
        gi_out.wait()
    f_out.wait()
    go_out.wait()
    own_d.wait()
    for r, c in d_copies.items():
        dot_copies[r].wait()
        c.wait()


def out_start(copy, i, s):
    copy(i, s).start()


def as_columns(x):
    row = jnp.sum(x, axis=0, keepdims=True)
    return jnp.transpose(jnp.broadcast_to(row, (128, row.shape[1])))


class Slab:
    def __init__(self, order, refs):
        self.order = order
        self.bufs, (self.send, self.recv) = refs[:6], refs[6:]
        self.bits = [m * (1 if a == "expert" else lax.axis_size("expert")) for a, m in order]
        self.out = ()

    def store(self, value, piece):
        total = 2 ** len(self.order)
        size = value.shape[0] // total
        for j in range(total):
            row = place_of(j, self.bits) * 2 * size
            mine = value[j * size : (j + 1) * size]
            both = jnp.concatenate([mine[:, 0:128], mine[:, 128:256]], axis=0)
            self.bufs[0][row : row + 2 * size, piece * 128 : piece * 128 + 128] = both.astype(BF16)

    def copy(self, s):
        dst = self.bufs[s + 1]
        return half_copy(self.bufs[s], dst, self.order[s], dst.shape[0], self.send.at[s], self.recv.at[s])

    def start(self):
        self.copy(0).start()

    def done(self, s):
        self.copy(s).wait()
        rows = self.bufs[s + 1].shape[0]
        if s < 4:
            half_add(self.bufs[s], self.bufs[s + 1], self.order[s], rows)
            self.copy(s + 1).start()
            return
        mine = self.bufs[4][pl.ds(pl.multiple_of(side(self.order[4]) * rows, 16), rows)]
        total = mine.astype(F32) + self.bufs[5][...].astype(F32)
        for piece, parts in enumerate(self.out):
            for n, (ref, at) in enumerate(parts):
                half = slice(n * rows // 2, (n + 1) * rows // 2)
                ref[:, at : at + 128] = total[half, piece * 128 : piece * 128 + 128]


def bwd_kernel(plan, *refs):
    (
        tok, cot, res, meta, dot_back, rT, f_rows, d_back, q, k, v, pw_far, att, n1, ln1, wqkv, wattn, ln2, wrT, cmT, cvT, cos, sin,
    ) = refs[:23]
    refs = refs[23:]
    if plan:
        stages, order = plan
        p_early, p_late, p_out, out_s, igrad_s, d_qkv, d_attn, d_small, d_ln, g_in_s, g_out_s = refs[:11]
        g_in, g_out = g_in_s.near, g_out_s.near
        refs = refs[11:]
    else:
        out_s, igrad_s, d_qkv, d_attn, d_small = refs[:5]
        refs = refs[5:]
    out, igrad = out_s.near, igrad_s.near
    wcat, rb, fk0, dsn, dots, dcat, n2b, dres, dbr, dproj, datt, dkv, lnacc, f_back, f_send, f_recv, pw, own_sem = refs[:18]
    refs = refs[18:]
    length, width = tok.near.shape
    experts, capacity, _ = f_rows.shape
    slots = experts * capacity
    block = length // 2

    weights = []
    for b in range(2):
        at = (slice(0, pw.shape[0]), slice(b * block, (b + 1) * block), slice(0, (b + 1) * block))
        weights.append(pltpu.make_async_copy(pw_far.at[at], pw.at[at], own_sem.at[b]))
    own_f = pltpu.make_async_copy(f_rows.at[0], f_back.at[0], own_sem.at[2])
    for ref in (d_back, cot, res):
        ref.start()
    greet(order[2:] if plan else (), experts - 1)
    f_copies = exchange(f_rows, f_back, f_send, f_recv)

    acts = {}
    if plan:
        in1, in2, out0, out1, out2, in_send, in_recv, out_send, out_recv = refs[:9]
        slab_refs = [refs[9 + 8 * n : 17 + 8 * n] for n in range(6)]
        late = p_late.near.shape[0]
        slabs_in = late + p_early.near.shape[0]
        ft = p_late.near.shape[2]
        hidden = g_in.shape[1] // 2

        def in_refs(i, s, far=False):
            n = i - (slabs_in - late)
            p = "far" if far else "near"
            first = getattr(p_early, p).at[i] if n < 0 else in1.at[n]
            return (getattr(p_late, p).at[n], first) if s == 0 else (first, in2.at[i])

        def in_copy(i, s):
            src, dst = in_refs(i, s, True)
            return half_copy(src, dst, stages[i % 2][s + 1], dst.shape[0], in_send.at[s, i], in_recv.at[s, i])

        def in_done(i, s):
            in_copy(i, s).wait()
            src, dst = in_refs(i, s)
            if s == 0:
                half_add(src, dst, stages[i % 2][1], dst.shape[0])
                in_copy(i, 1).start()
            else:
                to = (i % 2) * hidden + (i // 2) * ft
                half_add(src, dst, stages[i % 2][2], dst.shape[0], g_in.at[:, to : to + ft])

        def out_refs(i, s, far=False):
            return ((p_out.far if far else p_out.near, out0), (out0, out1), (out1, out2))[s]

        def out_copy(i, s):
            src, dst = out_refs(i, s, True)
            return half_copy(
                src.at[i], dst.at[i], stages[0][s], dst.shape[1], out_send.at[s, i], out_recv.at[s, i]
            )

        def out_done(i, s):
            out_copy(i, s).wait()
            src, dst = out_refs(i, s)
            wide = out2.shape[2]
            into = g_out.at[:, i * wide : (i + 1) * wide] if s == 2 else None
            half_add(src.at[i], dst.at[i], stages[0][s], dst.shape[1], into)
            if s < 2:
                out_copy(i, s + 1).start()

        attn_slab, q0, q1, q2a, q2b, ln_slab = (Slab(order, r) for r in slab_refs)

        def columns(ref, at):
            return ((ref, at), (ref, at + 128))

        attn_slab.out = [columns(d_attn, 256 * n) for n in range(3)]
        q0.out = [columns(d_qkv, kind * width) for kind in range(3)]
        q1.out = [columns(d_qkv, kind * width + 256) for kind in range(3)]
        q2a.out = [columns(d_qkv, kind * width + 512) for kind in range(2)]
        q2b.out = [columns(d_qkv, 2 * width + 512)]
        ln_slab.out = [((d_ln, 0), (d_small, 0))]

        for i in (1, 2):
            in_copy(i, 1).start()
        out_copy(0, 0).start()
        in_copy(6, 0).start()
        in_copy(3, 1).start()
        out_copy(1, 0).start()
        acts = {
            "token": [(out_start, in_copy, 5, 0), (in_done, 1, 1)],
            "attn": [
                (out_start, in_copy, 0, 1), (out_start, in_copy, 4, 0), (attn_slab.start,), (in_done, 6, 0),
                (in_done, 2, 1),
            ],
            "part0": [(q0.start,), (in_done, 3, 1), (attn_slab.done, 0)],
            "part1": [
                (out_start, in_copy, 7, 0), (q1.start,), (in_done, 0, 1), (out_done, 0, 0), (in_done, 4, 0),
                (q0.done, 0),
            ],
            "part2": [(q2a.start,), (q2b.start,), (in_done, 6, 1), (q1.done, 0), (attn_slab.done, 1)],
            "norm": [(q2a.done, 0), (q2b.done, 0), (q0.done, 1), (out_done, 0, 1)],
            "input": [(ln_slab.start,), (in_done, 4, 1)],
            "output": [
                (out_done, 1, 0), (ln_slab.done, 0), (q1.done, 1), (in_done, 5, 0), (q2a.done, 1), (out_done, 0, 2),
                (in_done, 7, 0), (q2b.done, 1), (ln_slab.done, 1), (out_done, 1, 1), (attn_slab.done, 2),
                (in_done, 5, 1), (q0.done, 2), (in_done, 7, 1), (q1.done, 2), (q2a.done, 2), (q2b.done, 2),
                (attn_slab.done, 3), (ln_slab.done, 2), (q0.done, 3), (out_done, 1, 2), (q1.done, 3), (q2a.done, 3),
                (q2b.done, 3), (attn_slab.done, 4), (ln_slab.done, 3), (q0.done, 4), (q1.done, 4), (q2a.done, 4),
                (q2b.done, 4), (ln_slab.done, 4),
            ],
        }
    for c in f_copies.values():
        c.start()
    late_refs = (wattn, att, q, k, v, cos, sin, n1, wqkv, tok)
    for ref in ((p_early, p_late, p_out) if plan else ()) + late_refs[:5]:
        ref.start()
    for c in weights:
        c.start()
    own_f.start()
    for ref in late_refs[5:]:
        ref.start()
    d_back = d_back.wait()

    def act(name):
        for f, *a in acts.get(name, ()):
            f(*a)

    wcat[...] = jnp.zeros_like(wcat)
    wcat[0:8] = wrT[...]
    wcat[8:12] = cmT[...]
    for kk in range(2):
        rb[kk] = jnp.transpose(jnp.broadcast_to(rT[kk : kk + 1, :].astype(F32), (128, length)))

    def chosen(rows, wide):
        slot = lax.broadcasted_iota(jnp.int32, (wide, slots), 1)
        r = slot // capacity
        e = jnp.zeros_like(slot)
        for n in range(experts):
            e = jnp.where(r == n, across(n), e)
        s_id = (slot - r * capacity + e * capacity).astype(F32)
        return meta[rows, 0:1] == s_id, meta[rows, 1:2] == s_id

    @pl.loop(0, length // 256)
    def _(i):
        rows = tile(i, 256)
        masks = chosen(rows, 256)
        either = (masks[0] | masks[1]).astype(F32).astype(BF16)
        dsn[rows] = dot(either, d_back[...].reshape(slots, width))
        line = jnp.concatenate([dot_back[r, 0:1] for r in range(experts)], axis=1)
        lane = lax.broadcasted_iota(jnp.int32, (256, 128), 1)
        for n, c in enumerate(masks):
            dots[n, rows] = jnp.where(lane == 0, jnp.sum(jnp.where(c, line, 0.0), axis=-1, keepdims=True), 0.0)

    cot, res = cot.wait(), res.wait()
    w_high = wcat[...].astype(BF16)
    lnacc[...] = jnp.zeros_like(lnacc)

    @pl.loop(0, length // 64)
    def _(i):
        rows = tile(i, 64)
        lane = lax.broadcasted_iota(jnp.int32, (64, 128), 1)
        lane_f = lane.astype(F32)
        m = meta[rows]
        g0, g1, keep = m[:, 2:3], m[:, 3:4], m[:, 4:5]
        cg = (m[:, 5:6], m[:, 6:7])
        shares = ((m[:, 7:8], m[:, 8:9]), (m[:, 9:10], m[:, 10:11]))
        g = cot[rows].astype(F32)
        x = res[rows]
        r2 = lax.rsqrt(row_mean(x * x) + EPS)
        xr = x * r2
        n2 = xr * ln2[1:2]
        n2b[rows] = n2.astype(BF16)
        cv = (cvT[0:1, :], cvT[1:2, :])
        fk0[rows] = x + keep * n2 + (cg[0] * shares[0][1]) * cv[0] + (cg[1] * shares[1][1]) * cv[1]
        gn2 = jnp.sum(g * n2, axis=-1, keepdims=True)
        gcv = [jnp.sum(g * c, axis=-1, keepdims=True) for c in cv]
        hits = [(rb[kk, rows] == lane_f).astype(F32) for kk in range(2)]
        special = jnp.where(lane == 5, gn2, 0.0)
        for j in range(2):
            special = jnp.where(lane == 6 + j, shares[j][0] * gn2 + shares[j][1] * gcv[j], special)
        dg = [
            jnp.sum(h * special + dots[n, rows], axis=-1, keepdims=True)
            for n, h in enumerate(hits)
        ]
        mean_dg = g0 * dg[0] + g1 * dg[1]
        dc0, dc1 = g0 * (dg[0] - mean_dg), g1 * (dg[1] - mean_dg)
        cat = hits[0] * dc0 + hits[1] * dc1
        for j in range(2):
            dm0, dm1 = cg[j] * gn2, cg[j] * gcv[j]
            mean_dm = shares[j][0] * dm0 + shares[j][1] * dm1
            cat = jnp.where(lane == 8 + 2 * j, shares[j][0] * (dm0 - mean_dm), cat)
            cat = jnp.where(lane == 9 + 2 * j, shares[j][1] * (dm1 - mean_dm), cat)
        dcat[rows, 0:128] = cat.astype(BF16)
        vecs = jnp.where(lane == 12, cg[0] * shares[0][1], 0.0)
        vecs = jnp.where(lane == 13, cg[1] * shares[1][1], vecs)
        dcat[rows, 128:256] = vecs.astype(BF16)
        dn2 = keep * g + dsn[rows] + dot(cat.astype(BF16), w_high)
        lnacc[0:8] += jnp.sum((dn2 * xr).reshape(8, 8, width), axis=0)
        dn = dn2 * ln2[1:2]
        dr = g + r2 * dn - xr * (r2 * r2) * row_mean(dn * x)
        dres[rows] = dr
        dbr[rows] = dr.astype(BF16)

    if plan:
        for ref in (p_early, p_late, p_out):
            ref.wait()
    act("token")
    wattn, att = wattn.wait(), att.wait()
    @pl.loop(0, width // 256)
    def _(j):
        cols = tile(j, 256)
        datt[:, cols] = dot_nt(dbr[...], wattn[cols, :]).astype(BF16)

    for j in range(width // 256):
        cols = slice(j * 256, (j + 1) * 256)
        d = dot_tn(att[...], dbr[:, cols])
        if plan:
            attn_slab.store(d, j)
        else:
            d_attn[:, cols] = d
    act("attn")
    q, k, v, cos, sin, n1 = (ref.wait() for ref in (q, k, v, cos, sin, n1))
    for c in weights:
        c.wait()

    for part in range(3):

        @pl.loop(2 * part, 2 * part + 2)
        def _(j):
            cols = tile(j, 128)
            dkv[...] = jnp.zeros_like(dkv)
            for b in range(2):
                rows = slice(b * block, (b + 1) * block)
                nk = (b + 1) * block
                qlane = lax.broadcasted_iota(jnp.int32, (block, 128), 1)
                klane = lax.broadcasted_iota(jnp.int32, (nk, 128), 1)
                do = datt[rows, cols]
                prod = do.astype(F32) * att[rows, cols].astype(F32)
                dq = jnp.zeros((block, 128), F32)
                for h in range(2):
                    delta = jnp.sum(half_mask(prod, qlane, h), axis=-1, keepdims=True)
                    dom = half_mask(do, qlane, h)
                    dp = dot_nt(dom, v[0:nk, cols])
                    w = pw[2 * j + h, rows, 0:nk]
                    ds = (w.astype(F32) * (dp - delta)).astype(BF16)
                    dq = dq + dot(ds, half_mask(k[0:nk, cols], klane, h))
                    dkv[0, 0:nk] += dot_tn(ds, half_mask(q[rows, cols], qlane, h))
                    dkv[1, 0:nk] += dot_tn(w, dom)
                dproj[rows, cols] = rotate(dq * 0.125, cos[rows], -sin[rows]).astype(BF16)
            dproj[:, pl.ds(pl.multiple_of(width + j * 128, 128), 128)] = rotate(dkv[0], cos[...], -sin[...]).astype(BF16)
            dproj[:, pl.ds(pl.multiple_of(2 * width + j * 128, 128), 128)] = dkv[1].astype(BF16)

        for kind in range(3):
            cols = slice(kind * width + part * 256, kind * width + part * 256 + 256)
            d = dot_tn(n1[...], dproj[:, cols])
            if not plan:
                d_qkv[:, cols] = d
            elif part < 2:
                (q0, q1)[part].store(d, kind)
            elif kind < 2:
                q2a.store(d, kind)
            else:
                q2b.store(d, 0)
        act(f"part{part}")

    wqkv = wqkv.wait()

    @pl.loop(0, width // 256)
    def _(j):
        cols = tile(j, 256)
        dsn[:, cols] = dot_nt(dproj[...], wqkv[cols, :])

    act("norm")
    tok = tok.wait()

    @pl.loop(0, length // 64)
    def _(i):
        rows = tile(i, 64)
        x = tok[rows].astype(F32)
        r1 = lax.rsqrt(row_mean(x * x) + EPS)
        xr = x * r1
        d = dsn[rows]
        dn = d * ln1[0:1]
        lnacc[8:16] += jnp.sum((d * xr).reshape(8, 8, width), axis=0)
        igrad[rows] = (dres[rows] + r1 * dn - xr * (r1 * r1) * row_mean(dn * x)).astype(BF16)

    lanes = lax.broadcasted_iota(jnp.int32, (width, 128), 1)
    small = dot_tn(n2b[...], dcat[:, 0:128]) + dot_tn(cot[...], dcat[:, 128:256])
    small = small + jnp.where(lanes == 14, as_columns(lnacc[8:16]), 0.0)
    small = small + jnp.where(lanes == 15, as_columns(lnacc[0:8]), 0.0)
    if plan:
        ln_slab.store(jnp.concatenate([small, small], axis=1), 0)
    else:
        d_small[...] = small
    igrad_s.start()
    act("input")

    own_f.wait()
    for c in f_copies.values():
        c.wait()

    @pl.loop(0, length // 256)
    def _(i):
        rows = tile(i, 256)
        first, second = chosen(rows, 256)
        mix = jnp.where(first, meta[rows, 2:3], jnp.where(second, meta[rows, 3:4], 0.0)).astype(BF16)
        out[rows] = (fk0[rows] + dot(mix, f_back[...].reshape(slots, width))).astype(BF16)

    out_s.start()
    act("output")
    out_s.wait()
    igrad_s.wait()
    if plan:
        g_in_s.start()
        g_out_s.start()
        g_in_s.wait()
        g_out_s.wait()


def shape(*s, dtype=BF16):
    return jax.ShapeDtypeStruct(s, dtype)


class Staged:
    def __init__(self, far, near, sem, out):
        self.far, self.near = far, near
        src, dst = (near, far) if out else (far, near)
        self.copy = lambda: pltpu.make_async_copy(src, dst, sem)

    def start(self):
        self.copy().start()

    def wait(self):
        self.copy().wait()
        return self.near


def call(kernel, outs, scratch, args, name, collective_id, far, staged):
    shapes = [jax.ShapeDtypeStruct(a.shape, a.dtype) for a in args] + list(outs)
    specs = [
        pl.BlockSpec(memory_space=pl.ANY if n in far or n in staged else pltpu.VMEM) for n in range(len(shapes))
    ]
    own = len(shapes) + len(scratch)
    extra = [pltpu.VMEM(shapes[n].shape, shapes[n].dtype) for n in staged]

    def wrapped(*refs):
        given, rest, near, sems = list(refs[: len(shapes)]), refs[len(shapes) : own], refs[own:-1], refs[-1]
        for i, n in enumerate(staged):
            given[n] = Staged(given[n], near[i], sems.at[i], n >= len(args))
        kernel(*given, *rest)

    return pl.pallas_call(
        wrapped,
        out_shape=outs,
        in_specs=specs[: len(args)],
        out_specs=specs[len(args) :],
        scratch_shapes=list(scratch) + extra + [pltpu.SemaphoreType.DMA((len(staged),))],
        compiler_params=pltpu.CompilerParams(
            vmem_limit_bytes=VMEM_LIMIT, has_side_effects=True, collective_id=collective_id
        ),
        name=name,
    )(*args)


def final_kernel(n, *refs):
    src, small, dst = refs[:n], refs[n], refs[n + 1 : 2 * n + 1]
    router, mix, vec, ln1, ln2 = refs[2 * n + 1 : 2 * n + 6]
    near, sems = refs[2 * n + 6 : 3 * n + 6], refs[-1]
    loads = [pltpu.make_async_copy(a, b, sems.at[0, i]) for i, (a, b) in enumerate(zip(src, near))]
    copies = [pltpu.make_async_copy(a, b, sems.at[1, i]) for i, (a, b) in enumerate(zip(near, dst))]
    for c in loads:
        c.start()
    rows = small.shape[0]
    t = jnp.transpose(jnp.concatenate([small[...], jnp.zeros((128 - rows, 128), F32)], axis=0))[:, 0:rows]
    router[...] = t[0:8]
    mix[...] = t[8:12]
    vec[...] = t[12:14]
    ln1[...] = t[14:15]
    ln2[...] = t[15:16]
    for a, b in zip(loads, copies):
        a.wait()
        b.start()
    for c in copies:
        c.wait()


def final(big, small):
    rows = small.shape[0]
    far, near = pl.BlockSpec(memory_space=pl.ANY), pl.BlockSpec(memory_space=pltpu.VMEM)
    return pl.pallas_call(
        functools.partial(final_kernel, len(big)),
        out_shape=[jax.ShapeDtypeStruct(a.shape, a.dtype) for a in big]
        + [shape(n, rows, dtype=F32) for n in (8, 4, 2, 1, 1)],
        in_specs=[far] * len(big) + [near],
        out_specs=[far] * len(big) + [near] * 5,
        scratch_shapes=[pltpu.VMEM(a.shape, a.dtype) for a in big] + [pltpu.SemaphoreType.DMA((2, len(big)))],
        compiler_params=pltpu.CompilerParams(vmem_limit_bytes=VMEM_LIMIT),
        name="results",
    )(*big, small)


def body(
    tokens, segments, routes, prev_logits, ln1_gain, w_qkv, w_attn, ln2_gain, w_router, const_mix, const_vec,
    expert_in, expert_out, cotangent,
):
    length, width = tokens.shape
    heads = width // HEAD_DIM
    experts = lax.axis_size("expert") * expert_in.shape[0]
    hidden = expert_out.shape[1]
    capacity = length // 2
    slots = experts * capacity
    n_dp = lax.axis_size("dp")
    V = pltpu.VMEM
    DMA = pltpu.SemaphoreType.DMA
    cos, sin = (jnp.asarray(t) for t in rotary_tables(length))
    rT, pT = routes.T, prev_logits.T
    wrT, cmT, cvT = w_router.T, const_mix.T, const_vec.T
    gains = jnp.stack([ln1_gain, ln2_gain])
    ln1 = ln2 = gains
    peers = experts - 1

    q, k, v, pw, att, n1, res, meta, send, g_rows, gate_row = call(
        fwd_kernel,
        [
            shape(length, width), shape(length, width), shape(length, width), shape(heads, length, length),
            shape(length, width), shape(length, width), shape(length, width, dtype=F32),
            shape(length, 128, dtype=F32), shape(experts, capacity, width), shape(experts, capacity, width),
            shape(experts, 8, capacity, dtype=F32),
        ],
        [
            V((length, length), F32), V((128, width), F32), V((3, length, 128), F32),
            V((128, length), F32), V((length, width), BF16), V((length, width), BF16),
            V((length, 128), F32), V((slots, length), BF16), V((experts, capacity, width), BF16),
            DMA((peers,)), DMA((peers,)), V((heads, length, length), BF16), V((experts, capacity, width), BF16),
            DMA((width // 128, 2)), DMA((experts + 1,)),
        ],
        (tokens, segments, rT, pT, ln1, w_qkv, w_attn, ln2, wrT, cmT, cotangent, cos, sin),
        "attention", 0, (16, 21, 22), (0, 5, 6, 10, 11, 12, 13, 14, 15, 17, 18, 19),
    )

    tiles, slabs = 4, 2
    ft = hidden // tiles
    within = n_dp == 8 and experts == 4
    stages = ((("dp", 1), ("dp", 2), ("dp", 4)), (("dp", 2), ("dp", 1), ("dp", 4))) if within else ()
    order = (("expert", 1), ("expert", 2), ("dp", 1), ("dp", 2), ("dp", 4))
    slab_in, slab_out = (2 * tiles, width, ft), (slabs, hidden, width // slabs)

    def part_of(s, n):
        return (s[0], s[1] // n, s[2])

    late = (tiles, width // 2, ft)
    early = (tiles, width // 4, ft)
    f_rows, d_back, g_out, dot_back, *g_in = call(
        functools.partial(expert_kernel, stages),
        [
            shape(experts, capacity, width), shape(experts, capacity, width), shape(*slab_out),
            shape(experts, 8, capacity, dtype=F32),
        ]
        + ([shape(*late), shape(*early)] if within else [shape(*slab_in)]),
        [
            V((experts, capacity, width), BF16), V((slots, width), BF16), V((tiles, slots, ft), BF16),
            V((tiles, slots, 2 * ft), BF16), V((slots, width), F32), V((slots, width), F32),
            V((experts, capacity, width), BF16),
        ]
        + ([V(slab_in, BF16), V(late, BF16)] + [DMA((2 * tiles,))] * 2 + [DMA((tiles,))] * 2 if within else [])
        + [DMA((peers,))] * 4
        + [DMA((2,)), V((experts, 8, capacity), F32), V((experts, 8, capacity), F32)]
        + [DMA((peers,))] * 4,
        (send, g_rows, expert_in, expert_out, gate_row),
        "experts", 1, (0, 6), (1, 2, 3, 5, 7) + ((9, 10) if within else (9,)),
    )

    args = (
        tokens, cotangent, res, meta, dot_back, rT, f_rows, d_back, q, k, v, pw, att, n1, ln1, w_qkv, w_attn, ln2, wrT, cmT, cvT,
        cos, sin,
    )
    n_all = n_dp * experts
    rows = width // n_all if within else width
    outs = [
        shape(length, width), shape(length, width), shape(rows, 3 * width, dtype=F32), shape(rows, width, dtype=F32),
        shape(rows, 128, dtype=F32),
    ]
    scratch = [
        V((128, width), F32), V((2, length, 128), F32), V((length, width), F32), V((length, width), F32),
        V((2, length, 128), F32), V((length, 256), BF16), V((length, width), BF16), V((length, width), F32),
        V((length, width), BF16), V((length, 3 * width), BF16), V((length, width), BF16),
        V((2, length, 128), F32), V((16, width), F32), V((experts, capacity, width), BF16), DMA((peers,)), DMA((peers,)),
        V((heads, length, length), BF16), DMA((3,)),
    ]
    if within:
        args += (g_in[1], g_in[0], g_out)
        outs += [
            shape(rows, 128, dtype=F32),
            shape(width // n_dp, 2 * hidden, dtype=F32), shape(hidden // n_dp, width, dtype=F32)]
        scratch += [
            V(early, BF16), V(part_of(slab_in, 8), BF16), V(part_of(slab_out, 2), BF16),
            V(part_of(slab_out, 4), BF16), V(part_of(slab_out, 8), BF16), DMA((2, 2 * tiles)), DMA((2, 2 * tiles)),
            DMA((3, slabs)), DMA((3, slabs)),
        ]
        for cols in (width, width, width, 512, 256, 256):
            scratch += [V((2 * width >> s, cols // 2), BF16) for s in range(6)] + [DMA((5,)), DMA((5,))]
    plan = (stages, order) if within else ()
    n = len(args)
    staged = (0, 1, 2, 7, 8, 9, 10, 12, 13, 15, 16, 21, 22) + tuple(range(23, n)) + (n, n + 1)
    staged += (n + 6, n + 7) if within else ()
    done = call(functools.partial(bwd_kernel, plan), outs, scratch, args, "backward", 2, (6, 11), staged)
    out, igrad, d_qkv, d_attn, small = done[:5]
    if within:
        out, igrad, d_qkv, d_attn, g_in, g_out, router, mix, vec, ln_one, ln_two = final(
            (out, igrad, d_qkv, d_attn, done[6], done[7]), small
        )
        return (
            out, igrad, ln_one.reshape(rows), d_qkv, d_attn, ln_two.reshape(rows), router.T, mix.T, vec.T,
            g_in[None], g_out[None],
        )
    (g_in,) = g_in
    g_in = jnp.moveaxis(g_in.reshape(tiles, 2, width, ft), 2, 0).transpose(0, 2, 1, 3).reshape(width, 2 * hidden)
    g_out = jnp.moveaxis(g_out, 0, 1).reshape(hidden, width)
    g_in = lax.psum_scatter(g_in, "dp", scatter_dimension=0, tiled=True).astype(F32)
    g_out = lax.psum_scatter(g_out, "dp", scatter_dimension=0, tiled=True).astype(F32)
    d_qkv, d_attn, small = (
        lax.psum_scatter(d, ("dp", "expert"), scatter_dimension=0, tiled=True) for d in (d_qkv, d_attn, small)
    )
    return (
        out, igrad, small[:, 14], d_qkv, d_attn, small[:, 15], small[:, 0:8], small[:, 8:12], small[:, 12:14],
        g_in[None], g_out[None],
    )


def solution(mesh):
    rows = P(("dp", "expert"), None)
    return jax.shard_map(
        body,
        mesh=mesh,
        in_specs=(
            rows, rows, rows, rows, P(), P(), P(), P(), P(), P(), P(),
            P("expert", None, None), P("expert", None, None), rows,
        ),
        out_specs=(
            rows, rows, P(("dp", "expert")), rows, rows, P(("dp", "expert")), rows, rows, rows,
            P("expert", "dp", None), P("expert", "dp", None),
        ),
        check_vma=False,
    )
```

```python
import functools
import math

import jax
import jax.numpy as jnp
import numpy as np
from jax import lax
from jax.experimental import pallas as pl
from jax.experimental.pallas import tpu as pltpu
from jax.sharding import PartitionSpec as P

HEAD_DIM = 64
EPS = 1e-06
MASKED = -1e30
F32 = jnp.float32
BF16 = jnp.bfloat16
VMEM_LIMIT = 62 * 1024 * 1024


def dot(a, b):
    return lax.dot_general(a, b, (((1,), (0,)), ((), ())), preferred_element_type=F32)


def dot_nt(a, b):
    return lax.dot_general(a, b, (((1,), (1,)), ((), ())), preferred_element_type=F32)


def dot_tn(a, b):
    return lax.dot_general(a, b, (((0,), (0,)), ((), ())), preferred_element_type=F32)


def tile(i, size):
    return pl.ds(pl.multiple_of(i * size, size), size)


def rotary_tables(length):
    half = HEAD_DIM // 2
    inverse = np.exp(np.arange(half, dtype=np.float32) * np.float32(-2.0 * math.log(10000.0) / HEAD_DIM))
    angles = np.arange(length, dtype=np.float32)[:, None] * inverse.astype(np.float32)[None, :]
    cos, sin = np.cos(angles), np.sin(angles)
    return (
        np.concatenate([cos] * 4, axis=1).astype(np.float32),
        np.concatenate([-sin, sin] * 2, axis=1).astype(np.float32),
    )


def rotate(x, cos, sin):
    lane = lax.broadcasted_iota(jnp.int32, x.shape, 1)
    front = (lane % HEAD_DIM) < HEAD_DIM // 2
    other = jnp.where(front, pltpu.roll(x, 96, 1), pltpu.roll(x, 32, 1))
    return x * cos + other * sin


def row_mean(x):
    return jnp.mean(x, axis=-1, keepdims=True)


def as_row(gain):
    return gain[...].reshape(1, gain.shape[0])


def pick(x, lane, index):
    return jnp.sum(jnp.where(lane == index, x, 0.0), axis=-1, keepdims=True)


def half_mask(x, lane, which):
    keep = (lane < HEAD_DIM) if which == 0 else (lane >= HEAD_DIM)
    return jnp.where(keep, x, jnp.zeros_like(x))


MESH = pl.DeviceIdType.MESH


def flip(i, m):
    return i + m * (1 - 2 * ((i // m) % 2))


def side(mask):
    axis, m = mask
    return (lax.axis_index(axis) // m) % 2


def partner(mask):
    axis, m = mask
    return {axis: flip(lax.axis_index(axis), m)}


def across(r):
    e = lax.axis_index("expert")
    for m in (1, 2):
        if r & m:
            e = flip(e, m)
    return e


def greet(masks, peers=0, wait=True):
    barrier = pltpu.get_barrier_semaphore()
    for mask in masks:
        pl.semaphore_signal(barrier, inc=1, device_id=partner(mask), device_id_type=MESH)
    for r in range(1, peers + 1):
        pl.semaphore_signal(barrier, inc=1, device_id={"expert": across(r)}, device_id_type=MESH)
    if wait:
        pl.semaphore_wait(barrier, len(masks) + peers)


def exchange(src, dst, send_sem, recv_sem):
    return {
        r: pltpu.make_async_remote_copy(
            src.at[r], dst.at[r], send_sem.at[r - 1], recv_sem.at[r - 1],
            device_id={"expert": across(r)}, device_id_type=MESH,
        )
        for r in range(src.shape[0] - 1, 0, -1)
    }


def half_copy(src, dst, mask, rows, send_sem, recv_sem):
    start = pl.multiple_of((1 - side(mask)) * rows, 16)
    return pltpu.make_async_remote_copy(
        src.at[pl.ds(start, rows)], dst, send_sem, recv_sem, device_id=partner(mask), device_id_type=MESH
    )


def half_add(src, dst, mask, rows, out=None):
    start = side(mask) * rows
    step = 48 if rows % 48 == 0 else 64
    out = dst if out is None else out

    @pl.loop(0, rows // step)
    def _(i):
        here = pl.ds(pl.multiple_of(i * step, 16), step)
        mine = src[pl.ds(pl.multiple_of(start + i * step, 16), step)].astype(F32)
        out[here] = (mine + dst[here].astype(F32)).astype(out.dtype)


def place_of(shard, masks):
    place = 0
    for m in masks:
        place = 2 * place + (shard // m) % 2
    return place


def fwd_kernel(
    tok, seg, rT, ln1, wqkv, wattn, ln2, cot, cos, sin,
    q_out, k_out, v_out, pw_out, att_out, n1_out, res_out, tg, send_out, g_rows, high_out, low_out,
    bias, rb, pb, onehot, g_out, send_sem, recv_sem, pw, send, pw_sem, row_sem,
):
    length, width = tok.near.shape
    capacity = length // 2
    experts = send.shape[0]

    for ref in (cot, tok, wqkv, cos, sin, wattn):
        ref.start()
    q, k, v, att, n1, res = (ref.near for ref in (q_out, k_out, v_out, att_out, n1_out, res_out))
    n2b, n2l = high_out.near, low_out.near
    greet((), experts - 1, wait=False)
    for kk in range(2):
        rb[kk] = jnp.transpose(jnp.broadcast_to(rT[kk : kk + 1, :].astype(F32), (128, length)))
    all_lane = lax.broadcasted_iota(jnp.int32, (length, 128), 1).astype(F32)
    count = ((rb[0] == all_lane).astype(F32) + (rb[1] == all_lane).astype(F32)).astype(BF16)

    @pl.loop(0, length // 128)
    def _(i):
        rows = tile(i, 128)
        lane = lax.broadcasted_iota(jnp.int32, (128, 128), 1)
        lane_f = lane.astype(F32)
        t_id = lax.broadcasted_iota(jnp.int32, (128, length), 0) + i * 128
        before = (t_id > lax.broadcasted_iota(jnp.int32, (128, length), 1)).astype(F32).astype(BF16)
        place = dot(before, count) + lane_f * float(capacity) + 1.0
        out = jnp.zeros((128, 128), F32)
        for kk in range(2):
            hit = (rb[kk, rows] == lane_f) & (lane < experts)
            out = jnp.where(lane == kk, jnp.sum(jnp.where(hit, place, 0.0), axis=-1, keepdims=True) - 1.0, out)
        tg[rows] = out

    target = jnp.transpose(tg[...])
    pb[...] = target

    cot = cot.wait()
    pl.semaphore_wait(pltpu.get_barrier_semaphore(), experts - 1)
    copies = exchange(g_out, g_rows, send_sem, recv_sem)
    own_rows = pltpu.make_async_copy(g_out.at[0], g_rows.at[0], row_sem.at[experts])
    for r in range(experts - 1, -1, -1):
        s_id = (lax.broadcasted_iota(jnp.int32, (capacity, length), 0) + across(r) * capacity).astype(F32)
        here = (pb[0:1] == s_id).astype(F32) + (pb[1:2] == s_id).astype(F32)
        onehot[r * capacity : (r + 1) * capacity] = here.astype(BF16)
        g_out[r] = dot(here.astype(BF16), cot[...]).astype(BF16)
        (copies[r] if r else own_rows).start()
    tok = tok.wait()

    @pl.loop(0, length // 256)
    def _(i):
        rows = tile(i, 256)
        x = tok[rows].astype(F32)
        r = lax.rsqrt(row_mean(x * x) + EPS)
        n1[rows] = (x * r * as_row(ln1)).astype(BF16)

    n1_out.start()
    wqkv, cos, sin = wqkv.wait(), cos.wait(), sin.wait()

    @pl.loop(0, width // 256)
    def _(j):
        for kind, dst in enumerate((q, k, v)):
            cols = pl.ds(pl.multiple_of(kind * width + j * 256, 256), 256)
            both = dot(n1[...], wqkv[:, cols])
            for part in range(2):
                x = both[:, part * 128 : part * 128 + 128]
                if kind < 2:
                    x = rotate(x, cos[...], sin[...])
                if kind == 0:
                    x = x * 0.125
                dst[:, pl.ds(pl.multiple_of(j * 256 + part * 128, 128), 128)] = x.astype(BF16)

    for done in (q_out, k_out, v_out):
        done.start()

    seg_f = seg[...].astype(F32)
    rb[2] = jnp.transpose(jnp.broadcast_to(seg_f, (128, length)))

    @pl.loop(0, length // 128)
    def _(i):
        rows = tile(i, 128)
        row_id = lax.broadcasted_iota(jnp.int32, (128, length), 0) + i * 128
        col_id = lax.broadcasted_iota(jnp.int32, (128, length), 1)
        same = rb[2, rows, 0:1] == seg_f
        bias[rows] = jnp.where(same & (row_id >= col_id), 0.0, MASKED)

    block = length // 2

    def weights_copy(j, b):
        at = (pl.ds(2 * j, 2), slice(b * block, (b + 1) * block), slice(0, (b + 1) * block))
        return pltpu.make_async_copy(pw.at[at], pw_out.at[at], pw_sem.at[j, b])

    def heads(j):
        cols = tile(j, 128)
        for b in range(2):
            rows = slice(b * block, (b + 1) * block)
            nk = (b + 1) * block
            qlane = lax.broadcasted_iota(jnp.int32, (block, 128), 1)
            klane = lax.broadcasted_iota(jnp.int32, (nk, 128), 1)
            acc = jnp.zeros((block, 128), F32)
            for h in range(2):
                s = dot_nt(half_mask(q[rows, cols], qlane, h), k[0:nk, cols]) + bias[rows, 0:nk]
                m = jnp.max(s, axis=-1, keepdims=True)
                e = jnp.exp(s - m)
                w = (e * (1.0 / jnp.sum(e, axis=-1, keepdims=True))).astype(BF16)
                pw[2 * j + h, rows, 0:nk] = w
                acc = acc + dot(w, half_mask(v[0:nk, cols], klane, h))
            att[rows, cols] = acc.astype(BF16)
            weights_copy(j, b).start()

    @pl.loop(0, width // 256)
    def _(jj):
        heads(2 * jj)
        heads(2 * jj + 1)

    att_out.start()
    wattn = wattn.wait()

    res[...] = tok[...].astype(F32) + dot(att[...], wattn[...])

    res_out.start()

    @pl.loop(0, length // 256)
    def _(i):
        rows = tile(i, 256)
        x = res[rows]
        n2 = x * lax.rsqrt(row_mean(x * x) + EPS) * as_row(ln2)
        high = n2.astype(BF16)
        n2b[rows] = high
        n2l[rows] = (n2 - high.astype(F32)).astype(BF16)

    high_out.start()
    low_out.start()

    @pl.loop(0, experts)
    def _(e):
        send[e] = dot(onehot[tile(e, capacity)], n2b[...]).astype(BF16)
        pltpu.make_async_copy(send.at[e], send_out.at[e], row_sem.at[e]).start()

    for ref in (q_out, k_out, v_out, att_out, n1_out, res_out, high_out, low_out):
        ref.wait()

    @pl.loop(0, width // 128)
    def _(j):
        for b in range(2):
            weights_copy(j, b).wait()

    @pl.loop(0, experts)
    def _(e):
        pltpu.make_async_copy(send.at[e], send_out.at[e], row_sem.at[e]).wait()

    own_rows.wait()
    for c in copies.values():
        c.wait()


def expert_kernel(stages, xs, g_rows, win, wout, n2b, n2l, tg, rT, pT, wrT, cmT, *refs):
    f_out, d_back, go_out, dot_back, meta = refs[:5]
    refs = refs[:3] + refs[5:]
    f_rows, go = f_out.near, go_out.near
    if stages:
        late_out, early_out = refs[3:5]
        p_late, p_early = late_out.near, early_out.near
        refs = refs[5:]
    else:
        gi_out = refs[3]
        gi = gi_out.near
        refs = refs[4:]
    xr, dy, hid, dgu, f_acc, d_acc, d_out = refs[:7]
    refs = refs[7:]
    if stages:
        gi, p_first, in_send, in_recv, e_send, e_recv = refs[:6]
        refs = refs[6:]
    x_send, x_recv, d_send, d_recv, own_sem, gates, gate_row, dot_row, wcat, rb, r_send, r_recv, s_send, s_recv = refs
    groups, capacity, _ = xs.shape
    hidden, width = wout.near.shape[1:]
    tiles, rows_all, ft = hid.shape
    slabs = go.shape[0]
    shards = 2 ** len(stages[0]) if stages else 0
    near = rows_all // 2

    greet([s[0] for s in stages], groups - 1)
    copies = exchange(xs, xr, x_send, x_recv)
    n2b.start()
    n2l.start()
    for c in copies.values():
        c.start()
    own_x = pltpu.make_async_copy(xs.at[0], xr.at[0], own_sem.at[0])
    own_x.start()
    for ref in (g_rows, win, wout):
        ref.start()
    n2b, n2l = n2b.wait(), n2l.wait()
    length = n2b.shape[0]
    wcat[...] = jnp.zeros_like(wcat)
    wcat[0:8] = wrT[...]
    wcat[8:12] = cmT[...]
    w_high = wcat[...].astype(BF16)
    w_low = (wcat[...] - w_high.astype(F32)).astype(BF16)

    for kk in range(2):
        rb[kk] = jnp.transpose(jnp.broadcast_to(rT[kk : kk + 1, :].astype(F32), (128, length)))
    rb[2] = jnp.transpose(jnp.concatenate([pT[...], jnp.zeros((120, length), F32)], axis=0))

    @pl.loop(0, length // 128)
    def _(i):
        rows = tile(i, 128)
        lane = lax.broadcasted_iota(jnp.int32, (128, 128), 1)
        lane_f = lane.astype(F32)
        high = n2b[rows]
        mixed = dot_nt(high, w_high) + dot_nt(high, w_low) + dot_nt(n2l[rows], w_high)
        logits = mixed + rb[2, rows]
        hits = [(rb[kk, rows] == lane_f).astype(F32) for kk in range(2)]
        chosen = [jnp.sum(h * logits, axis=-1, keepdims=True) for h in hits]
        top = jnp.maximum(chosen[0], chosen[1])
        e = [jnp.exp(c - top) for c in chosen]
        inv = 1.0 / (e[0] + e[1])
        gates = [v_ * inv for v_ in e]
        shares = []
        for j in range(2):
            a0, a1 = pick(mixed, lane, 8 + 2 * j), pick(mixed, lane, 9 + 2 * j)
            mx = jnp.maximum(a0, a1)
            b0, b1 = jnp.exp(a0 - mx), jnp.exp(a1 - mx)
            binv = 1.0 / (b0 + b1)
            shares.append((b0 * binv, b1 * binv))
        gate_sum = gates[0] * hits[0] + gates[1] * hits[1]
        cg = [pick(gate_sum, lane, 6), pick(gate_sum, lane, 7)]
        keep = pick(gate_sum, lane, 5) + cg[0] * shares[0][0] + cg[1] * shares[1][0]
        values = (
            gates[0], gates[1], keep, cg[0], cg[1], shares[0][0], shares[0][1], shares[1][0], shares[1][1],
        )
        out = tg[rows]
        for n, value in enumerate(values):
            out = jnp.where(lane == n + 2, value, out)
        meta[rows] = out

    row_copies = exchange(gate_row, gates, r_send, r_recv)
    for r in range(groups - 1, -1, -1):
        slot = (lax.broadcasted_iota(jnp.int32, (length, capacity), 1) + across(r) * capacity).astype(F32)
        gate = jnp.where(meta[:, 0:1] == slot, meta[:, 2:3], jnp.where(meta[:, 1:2] == slot, meta[:, 3:4], 0.0))
        line = jnp.broadcast_to(jnp.sum(gate, axis=0, keepdims=True), (8, capacity))
        if r:
            gate_row[r] = line
            row_copies[r].start()
        else:
            gates[0] = line

    def gated(r):
        if r:
            row_copies[r].wait()
            copies[r].wait()
        gate = jnp.transpose(jnp.broadcast_to(gates[r, 0:1], (128, capacity)))[:, 0:1]
        dy[r * capacity : (r + 1) * capacity] = (g_rows[r].astype(F32) * gate).astype(BF16)

    def cols_of(f):
        return tile(f, ft), pl.ds(pl.multiple_of(hidden + f * ft, ft), ft)

    def work(f, part):
        gate_cols, up_cols = cols_of(f)
        rows = slice(part * near, (part + 1) * near)
        x = xr[2 * part : 2 * part + 2].reshape(near, width)
        gate = dot(x, win[0, :, gate_cols])
        up = dot(x, win[0, :, up_cols])
        dh = dot_nt(dy[rows], wout[0, gate_cols, :])
        sig = 1.0 / (1.0 + jnp.exp(-gate))
        silu = gate * sig
        h = (silu * up).astype(BF16)
        da = (dh * up * (sig + silu * (1.0 - sig))).astype(BF16)
        db = (dh * silu).astype(BF16)
        hid[f, rows] = h
        dgu[f, rows, 0:ft] = da
        dgu[f, rows, ft : 2 * ft] = db

    def gather(f, part):
        gate_cols, up_cols = cols_of(f)
        rows = slice(part * near, (part + 1) * near)
        y = dot(hid[f, rows], wout[0, gate_cols, :])
        d = dot_nt(dgu[f, rows, 0:ft], win[0, :, gate_cols]) + dot_nt(dgu[f, rows, ft : 2 * ft], win[0, :, up_cols])

        @pl.when(f == 0)
        def _():
            f_acc[rows] = y
            d_acc[rows] = d

        @pl.when(f > 0)
        def _():
            f_acc[rows] += y
            d_acc[rows] += d

    def in_copy(part, f, p):
        dst = (p_first if part == 0 else p_late).at[2 * (f - part * tiles // 2) + p]
        slab = 2 * f + p
        return half_copy(gi.at[slab], dst, stages[p][0], width // 2, in_send.at[slab], in_recv.at[slab]), dst

    def early_copy(slab):
        return half_copy(
            p_first.at[slab], p_early.at[slab], stages[slab % 2][1], width // 4, e_send.at[slab], e_recv.at[slab]
        )

    own_x.wait()
    g_rows = g_rows.wait()
    gated(0)
    gated(1)

    win, wout = win.wait(), wout.wait()

    @pl.loop(0, tiles)
    def _(f):
        work(f, 0)
        gather(f, 0)

    gated(3)
    gated(2)

    for part in range(2):

        @pl.loop(part * (tiles // 2), (part + 1) * (tiles // 2))
        def _(f):
            work(f, 1)
            for p in range(2):
                d = dot_tn(xr[...].reshape(rows_all, width), dgu[f, :, p * ft : (p + 1) * ft])
                if not stages:
                    gi[2 * f + p] = d.astype(BF16)
                    continue
                size = width // shards
                for j in range(shards):
                    at = place_of(j, [m for _, m in stages[p]]) * size
                    gi[2 * f + p, at : at + size] = d[j * size : (j + 1) * size].astype(BF16)
                in_copy(part, f, p)[0].start()
            gather(f, 1)

    d_copies = exchange(d_out, d_back, d_send, d_recv)
    dot_copies = exchange(dot_row, dot_back, s_send, s_recv)
    own_d = pltpu.make_async_copy(d_out.at[0], d_back.at[0], own_sem.at[1])
    for r in range(groups - 1, -1, -1):
        rows = slice(r * capacity, (r + 1) * capacity)
        y = f_acc[rows]
        f_rows[r] = y.astype(BF16)
        dots = jnp.sum(y * g_rows[r].astype(F32), axis=-1, keepdims=True)
        as_rows = jnp.transpose(jnp.broadcast_to(dots, (capacity, 128)))[0:8]
        d_out[r] = d_acc[rows].astype(BF16)
        if r:
            dot_row[r] = as_rows
            dot_copies[r].start()
            d_copies[r].start()
        else:
            dot_back[0] = as_rows
            own_d.start()
    f_out.start()

    for c in range(slabs):
        cols = slice(c * (width // slabs), (c + 1) * (width // slabs))

        @pl.loop(0, tiles)
        def _(t):
            d = dot_tn(hid[t], dy[:, cols]).astype(BF16)
            if not stages:
                go[c, tile(t, ft)] = d
                return
            size = hidden // shards
            for i in range(ft // size):
                at = place_of(t * (ft // size) + i, [m for _, m in stages[0]])
                go[c, tile(at, size)] = d[i * size : (i + 1) * size]

    go_out.start()
    if stages:
        for part in range(2):
            for f in range(part * (tiles // 2), (part + 1) * (tiles // 2)):
                for p in range(2):
                    copy, dst = in_copy(part, f, p)
                    copy.wait()
                    half_add(gi.at[2 * f + p], dst, stages[p][0], width // 2)
                    if part == 0:
                        early_copy(2 * f + p).start()
        late_out.start()
        for slab in range(tiles):
            early_copy(slab).wait()
            half_add(p_first.at[slab], p_early.at[slab], stages[slab % 2][1], width // 4)
        early_out.start()
        late_out.wait()
        early_out.wait()
    else:
        gi_out.start()
        gi_out.wait()
    f_out.wait()
    go_out.wait()
    own_d.wait()
    for r, c in d_copies.items():
        dot_copies[r].wait()
        c.wait()


def out_start(copy, i, s):
    copy(i, s).start()


def as_columns(x):
    row = jnp.sum(x, axis=0, keepdims=True)
    return jnp.transpose(jnp.broadcast_to(row, (128, row.shape[1])))


class Slab:
    def __init__(self, order, refs):
        self.order = order
        self.bufs, (self.send, self.recv) = refs[:6], refs[6:]
        self.bits = [m * (1 if a == "expert" else lax.axis_size("expert")) for a, m in order]
        self.out = ()

    def store(self, value, piece):
        total = 2 ** len(self.order)
        size = value.shape[0] // total
        for j in range(total):
            row = place_of(j, self.bits) * 2 * size
            mine = value[j * size : (j + 1) * size]
            both = jnp.concatenate([mine[:, 0:128], mine[:, 128:256]], axis=0)
            self.bufs[0][row : row + 2 * size, piece * 128 : piece * 128 + 128] = both.astype(BF16)

    def copy(self, s):
        dst = self.bufs[s + 1]
        return half_copy(self.bufs[s], dst, self.order[s], dst.shape[0], self.send.at[s], self.recv.at[s])

    def start(self):
        self.copy(0).start()

    def done(self, s):
        self.copy(s).wait()
        rows = self.bufs[s + 1].shape[0]
        if s < 4:
            half_add(self.bufs[s], self.bufs[s + 1], self.order[s], rows)
            self.copy(s + 1).start()
            return
        mine = self.bufs[4][pl.ds(pl.multiple_of(side(self.order[4]) * rows, 16), rows)]
        total = mine.astype(F32) + self.bufs[5][...].astype(F32)
        for piece, parts in enumerate(self.out):
            for n, (ref, at) in enumerate(parts):
                half = slice(n * rows // 2, (n + 1) * rows // 2)
                ref[:, at : at + 128] = total[half, piece * 128 : piece * 128 + 128]


def bwd_kernel(plan, *refs):
    (
        tok, cot, res, meta, dot_back, rT, f_rows, d_back, q, k, v, pw_far, att, n1, ln1, wqkv, wattn, ln2, wrT, cmT, cvT, cos, sin,
    ) = refs[:23]
    refs = refs[23:]
    if plan:
        stages, order = plan
        p_early, p_late, p_out, out_s, igrad_s, d_qkv, d_attn, d_small, d_ln, g_in_s, g_out_s = refs[:11]
        g_in, g_out = g_in_s.near, g_out_s.near
        refs = refs[11:]
    else:
        out_s, igrad_s, d_qkv, d_attn, d_small = refs[:5]
        refs = refs[5:]
    out, igrad = out_s.near, igrad_s.near
    wcat, rb, fk0, dsn, dots, dcat, n2b, dres, dbr, dproj, datt, dkv, lnacc, f_back, f_send, f_recv, pw, own_sem = refs[:18]
    refs = refs[18:]
    length, width = tok.near.shape
    experts, capacity, _ = f_rows.shape
    slots = experts * capacity
    block = length // 2

    weights = []
    for b in range(2):
        at = (slice(0, pw.shape[0]), slice(b * block, (b + 1) * block), slice(0, (b + 1) * block))
        weights.append(pltpu.make_async_copy(pw_far.at[at], pw.at[at], own_sem.at[b]))
    own_f = pltpu.make_async_copy(f_rows.at[0], f_back.at[0], own_sem.at[2])
    for ref in (d_back, cot, res):
        ref.start()
    greet(order[2:] if plan else (), experts - 1)
    f_copies = exchange(f_rows, f_back, f_send, f_recv)

    acts = {}
    if plan:
        in1, in2, out0, out1, out2, in_send, in_recv, out_send, out_recv = refs[:9]
        slab_refs = [refs[9 + 8 * n : 17 + 8 * n] for n in range(6)]
        late = p_late.near.shape[0]
        slabs_in = late + p_early.near.shape[0]
        ft = p_late.near.shape[2]
        hidden = g_in.shape[1] // 2

        def in_refs(i, s, far=False):
            n = i - (slabs_in - late)
            p = "far" if far else "near"
            first = getattr(p_early, p).at[i] if n < 0 else in1.at[n]
            return (getattr(p_late, p).at[n], first) if s == 0 else (first, in2.at[i])

        def in_copy(i, s):
            src, dst = in_refs(i, s, True)
            return half_copy(src, dst, stages[i % 2][s + 1], dst.shape[0], in_send.at[s, i], in_recv.at[s, i])

        def in_done(i, s):
            in_copy(i, s).wait()
            src, dst = in_refs(i, s)
            if s == 0:
                half_add(src, dst, stages[i % 2][1], dst.shape[0])
                in_copy(i, 1).start()
            else:
                to = (i % 2) * hidden + (i // 2) * ft
                half_add(src, dst, stages[i % 2][2], dst.shape[0], g_in.at[:, to : to + ft])

        def out_refs(i, s, far=False):
            return ((p_out.far if far else p_out.near, out0), (out0, out1), (out1, out2))[s]

        def out_copy(i, s):
            src, dst = out_refs(i, s, True)
            return half_copy(
                src.at[i], dst.at[i], stages[0][s], dst.shape[1], out_send.at[s, i], out_recv.at[s, i]
            )

        def out_done(i, s):
            out_copy(i, s).wait()
            src, dst = out_refs(i, s)
            wide = out2.shape[2]
            into = g_out.at[:, i * wide : (i + 1) * wide] if s == 2 else None
            half_add(src.at[i], dst.at[i], stages[0][s], dst.shape[1], into)
            if s < 2:
                out_copy(i, s + 1).start()

        turned = order[:3] + (order[4], order[3])
        attn_slab, q0, q1, q2a, q2b, ln_slab = (
            Slab(turned if n == 4 else order, r) for n, r in enumerate(slab_refs)
        )

        def columns(ref, at):
            return ((ref, at), (ref, at + 128))

        attn_slab.out = [columns(d_attn, 256 * n) for n in range(3)]
        q0.out = [columns(d_qkv, kind * width) for kind in range(3)]
        q1.out = [columns(d_qkv, kind * width + 256) for kind in range(3)]
        q2a.out = [columns(d_qkv, kind * width + 512) for kind in range(2)]
        q2b.out = [columns(d_qkv, 2 * width + 512)]
        ln_slab.out = [((d_ln, 0), (d_small, 0))]

        for i, n in ((4, 0), (5, 0), (0, 1), (3, 1), (1, 1), (6, 0)):
            in_copy(i, n).start()
        out_copy(1, 0).start()
        acts = {
            "token": [(in_done, 4, 0), (in_done, 5, 0), (in_done, 0, 1)],
            "attn": [(out_start, out_copy, 0, 0), (attn_slab.start,), (in_done, 3, 1)],
            "part0": [
                (out_start, out_copy, 2, 0), (out_start, in_copy, 2, 1), (q0.start,), (in_done, 1, 1),
                (attn_slab.done, 0), (in_done, 6, 0), (out_done, 1, 0),
            ],
            "part1": [(out_start, in_copy, 7, 0), (q1.start,), (in_done, 4, 1), (q0.done, 0), (in_done, 5, 1)],
            "part2": [
                (q2a.start,), (q2b.start,), (attn_slab.done, 1), (q1.done, 0), (in_done, 2, 1), (out_done, 0, 0),
            ],
            "norm": [(out_done, 1, 1), (q2a.done, 0), (in_done, 6, 1), (q2b.done, 0), (q0.done, 1)],
            "input": [(ln_slab.start,)],
            "output": [
                (out_done, 0, 1), (q1.done, 1), (ln_slab.done, 0), (out_done, 2, 0), (out_done, 1, 2), (q2a.done, 1),
                (in_done, 7, 0), (q2b.done, 1), (out_done, 0, 2), (ln_slab.done, 1), (attn_slab.done, 2),
                (out_done, 2, 1), (q0.done, 2), (in_done, 7, 1), (g_in_s.start,), (attn_slab.done, 3), (q1.done, 2),
                (q2a.done, 2), (out_done, 2, 2), (g_out_s.start,), (q0.done, 3), (q2b.done, 2), (attn_slab.done, 4),
                (ln_slab.done, 2), (q1.done, 3), (q2a.done, 3), (q0.done, 4), (q2b.done, 3), (ln_slab.done, 3),
                (q1.done, 4), (q2b.done, 4), (q2a.done, 4), (ln_slab.done, 4),
            ],
        }
    for c in f_copies.values():
        c.start()
    late_refs = (wattn, att, q, k, v, cos, sin, n1, wqkv, tok)
    for ref in ((p_early, p_late, p_out) if plan else ()) + late_refs[:5]:
        ref.start()
    for c in weights:
        c.start()
    own_f.start()
    for ref in late_refs[5:]:
        ref.start()
    d_back = d_back.wait()

    def act(name):
        for f, *a in acts.get(name, ()):
            f(*a)

    wcat[...] = jnp.zeros_like(wcat)
    wcat[0:8] = wrT[...]
    wcat[8:12] = cmT[...]
    for kk in range(2):
        rb[kk] = jnp.transpose(jnp.broadcast_to(rT[kk : kk + 1, :].astype(F32), (128, length)))

    def chosen(rows, wide):
        slot = lax.broadcasted_iota(jnp.int32, (wide, slots), 1)
        r = slot // capacity
        e = jnp.zeros_like(slot)
        for n in range(experts):
            e = jnp.where(r == n, across(n), e)
        s_id = (slot - r * capacity + e * capacity).astype(F32)
        return meta[rows, 0:1] == s_id, meta[rows, 1:2] == s_id

    @pl.loop(0, length // 256)
    def _(i):
        rows = tile(i, 256)
        masks = chosen(rows, 256)
        either = (masks[0] | masks[1]).astype(F32).astype(BF16)
        dsn[rows] = dot(either, d_back[...].reshape(slots, width))
        line = jnp.concatenate([dot_back[r, 0:1] for r in range(experts)], axis=1)
        lane = lax.broadcasted_iota(jnp.int32, (256, 128), 1)
        for n, c in enumerate(masks):
            dots[n, rows] = jnp.where(lane == 0, jnp.sum(jnp.where(c, line, 0.0), axis=-1, keepdims=True), 0.0)

    cot, res = cot.wait(), res.wait()
    w_high = wcat[...].astype(BF16)
    lnacc[...] = jnp.zeros_like(lnacc)

    @pl.loop(0, length // 64)
    def _(i):
        rows = tile(i, 64)
        lane = lax.broadcasted_iota(jnp.int32, (64, 128), 1)
        lane_f = lane.astype(F32)
        m = meta[rows]
        g0, g1, keep = m[:, 2:3], m[:, 3:4], m[:, 4:5]
        cg = (m[:, 5:6], m[:, 6:7])
        shares = ((m[:, 7:8], m[:, 8:9]), (m[:, 9:10], m[:, 10:11]))
        g = cot[rows].astype(F32)
        x = res[rows]
        r2 = lax.rsqrt(row_mean(x * x) + EPS)
        xr = x * r2
        n2 = xr * as_row(ln2)
        n2b[rows] = n2.astype(BF16)
        cv = (cvT[0:1, :], cvT[1:2, :])
        fk0[rows] = x + keep * n2 + (cg[0] * shares[0][1]) * cv[0] + (cg[1] * shares[1][1]) * cv[1]
        gn2 = jnp.sum(g * n2, axis=-1, keepdims=True)
        gcv = [jnp.sum(g * c, axis=-1, keepdims=True) for c in cv]
        hits = [(rb[kk, rows] == lane_f).astype(F32) for kk in range(2)]
        special = jnp.where(lane == 5, gn2, 0.0)
        for j in range(2):
            special = jnp.where(lane == 6 + j, shares[j][0] * gn2 + shares[j][1] * gcv[j], special)
        dg = [
            jnp.sum(h * special + dots[n, rows], axis=-1, keepdims=True)
            for n, h in enumerate(hits)
        ]
        mean_dg = g0 * dg[0] + g1 * dg[1]
        dc0, dc1 = g0 * (dg[0] - mean_dg), g1 * (dg[1] - mean_dg)
        cat = hits[0] * dc0 + hits[1] * dc1
        for j in range(2):
            dm0, dm1 = cg[j] * gn2, cg[j] * gcv[j]
            mean_dm = shares[j][0] * dm0 + shares[j][1] * dm1
            cat = jnp.where(lane == 8 + 2 * j, shares[j][0] * (dm0 - mean_dm), cat)
            cat = jnp.where(lane == 9 + 2 * j, shares[j][1] * (dm1 - mean_dm), cat)
        dcat[rows, 0:128] = cat.astype(BF16)
        vecs = jnp.where(lane == 12, cg[0] * shares[0][1], 0.0)
        vecs = jnp.where(lane == 13, cg[1] * shares[1][1], vecs)
        dcat[rows, 128:256] = vecs.astype(BF16)
        dn2 = keep * g + dsn[rows] + dot(cat.astype(BF16), w_high)
        lnacc[0:8] += jnp.sum((dn2 * xr).reshape(8, 8, width), axis=0)
        dn = dn2 * as_row(ln2)
        dr = g + r2 * dn - xr * (r2 * r2) * row_mean(dn * x)
        dres[rows] = dr
        dbr[rows] = dr.astype(BF16)

    if plan:
        for ref in (p_early, p_late, p_out):
            ref.wait()
    act("token")
    wattn, att = wattn.wait(), att.wait()
    @pl.loop(0, width // 256)
    def _(j):
        cols = tile(j, 256)
        datt[:, cols] = dot_nt(dbr[...], wattn[cols, :]).astype(BF16)

    for j in range(width // 256):
        cols = slice(j * 256, (j + 1) * 256)
        d = dot_tn(att[...], dbr[:, cols])
        if plan:
            attn_slab.store(d, j)
        else:
            d_attn[:, cols] = d
    act("attn")
    q, k, v, cos, sin, n1 = (ref.wait() for ref in (q, k, v, cos, sin, n1))
    for c in weights:
        c.wait()

    for part in range(3):

        @pl.loop(2 * part, 2 * part + 2)
        def _(j):
            cols = tile(j, 128)
            dkv[...] = jnp.zeros_like(dkv)
            for b in range(2):
                rows = slice(b * block, (b + 1) * block)
                nk = (b + 1) * block
                qlane = lax.broadcasted_iota(jnp.int32, (block, 128), 1)
                klane = lax.broadcasted_iota(jnp.int32, (nk, 128), 1)
                do = datt[rows, cols]
                prod = do.astype(F32) * att[rows, cols].astype(F32)
                dq = jnp.zeros((block, 128), F32)
                for h in range(2):
                    delta = jnp.sum(half_mask(prod, qlane, h), axis=-1, keepdims=True)
                    dom = half_mask(do, qlane, h)
                    dp = dot_nt(dom, v[0:nk, cols])
                    w = pw[2 * j + h, rows, 0:nk]
                    ds = (w.astype(F32) * (dp - delta)).astype(BF16)
                    dq = dq + dot(ds, half_mask(k[0:nk, cols], klane, h))
                    dkv[0, 0:nk] += dot_tn(ds, half_mask(q[rows, cols], qlane, h))
                    dkv[1, 0:nk] += dot_tn(w, dom)
                dproj[rows, cols] = rotate(dq * 0.125, cos[rows], -sin[rows]).astype(BF16)
            dproj[:, pl.ds(pl.multiple_of(width + j * 128, 128), 128)] = rotate(dkv[0], cos[...], -sin[...]).astype(BF16)
            dproj[:, pl.ds(pl.multiple_of(2 * width + j * 128, 128), 128)] = dkv[1].astype(BF16)

        for kind in range(3):
            cols = slice(kind * width + part * 256, kind * width + part * 256 + 256)
            d = dot_tn(n1[...], dproj[:, cols])
            if not plan:
                d_qkv[:, cols] = d
            elif part < 2:
                (q0, q1)[part].store(d, kind)
            elif kind < 2:
                q2a.store(d, kind)
            else:
                q2b.store(d, 0)
        act(f"part{part}")

    wqkv = wqkv.wait()

    @pl.loop(0, width // 256)
    def _(j):
        cols = tile(j, 256)
        dsn[:, cols] = dot_nt(dproj[...], wqkv[cols, :])

    act("norm")
    tok = tok.wait()

    @pl.loop(0, length // 64)
    def _(i):
        rows = tile(i, 64)
        x = tok[rows].astype(F32)
        r1 = lax.rsqrt(row_mean(x * x) + EPS)
        xr = x * r1
        d = dsn[rows]
        dn = d * as_row(ln1)
        lnacc[8:16] += jnp.sum((d * xr).reshape(8, 8, width), axis=0)
        igrad[rows] = (dres[rows] + r1 * dn - xr * (r1 * r1) * row_mean(dn * x)).astype(BF16)

    lanes = lax.broadcasted_iota(jnp.int32, (width, 128), 1)
    small = dot_tn(n2b[...], dcat[:, 0:128]) + dot_tn(cot[...], dcat[:, 128:256])
    small = small + jnp.where(lanes == 14, as_columns(lnacc[8:16]), 0.0)
    small = small + jnp.where(lanes == 15, as_columns(lnacc[0:8]), 0.0)
    if plan:
        ln_slab.store(jnp.concatenate([small, small], axis=1), 0)
    else:
        d_small[...] = small
    igrad_s.start()
    act("input")

    own_f.wait()
    for c in f_copies.values():
        c.wait()

    @pl.loop(0, length // 256)
    def _(i):
        rows = tile(i, 256)
        first, second = chosen(rows, 256)
        mix = jnp.where(first, meta[rows, 2:3], jnp.where(second, meta[rows, 3:4], 0.0)).astype(BF16)
        out[rows] = (fk0[rows] + dot(mix, f_back[...].reshape(slots, width))).astype(BF16)

    out_s.start()
    act("output")
    out_s.wait()
    igrad_s.wait()
    if plan:
        g_in_s.wait()
        g_out_s.wait()


def shape(*s, dtype=BF16):
    return jax.ShapeDtypeStruct(s, dtype)


class Staged:
    def __init__(self, far, near, sem, out):
        self.far, self.near = far, near
        src, dst = (near, far) if out else (far, near)
        self.copy = lambda: pltpu.make_async_copy(src, dst, sem)

    def start(self):
        self.copy().start()

    def wait(self):
        self.copy().wait()
        return self.near


def call(kernel, outs, scratch, args, name, collective_id, far, staged):
    shapes = [jax.ShapeDtypeStruct(a.shape, a.dtype) for a in args] + list(outs)
    specs = [
        pl.BlockSpec(memory_space=pl.ANY if n in far or n in staged else pltpu.VMEM) for n in range(len(shapes))
    ]
    own = len(shapes) + len(scratch)
    extra = [pltpu.VMEM(shapes[n].shape, shapes[n].dtype) for n in staged]

    def wrapped(*refs):
        given, rest, near, sems = list(refs[: len(shapes)]), refs[len(shapes) : own], refs[own:-1], refs[-1]
        for i, n in enumerate(staged):
            given[n] = Staged(given[n], near[i], sems.at[i], n >= len(args))
        kernel(*given, *rest)

    return pl.pallas_call(
        wrapped,
        out_shape=outs,
        in_specs=specs[: len(args)],
        out_specs=specs[len(args) :],
        scratch_shapes=list(scratch) + extra + [pltpu.SemaphoreType.DMA((len(staged),))],
        compiler_params=pltpu.CompilerParams(
            vmem_limit_bytes=VMEM_LIMIT, has_side_effects=True, collective_id=collective_id
        ),
        name=name,
    )(*args)


def final_kernel(n, *refs):
    src, small, dst = refs[:n], refs[n], refs[n + 1 : 2 * n + 1]
    router, mix, vec, ln1, ln2 = refs[2 * n + 1 : 2 * n + 6]
    near, sems = refs[2 * n + 6 : 3 * n + 6], refs[-1]
    loads = [pltpu.make_async_copy(a, b, sems.at[0, i]) for i, (a, b) in enumerate(zip(src, near))]
    copies = [pltpu.make_async_copy(a, b, sems.at[1, i]) for i, (a, b) in enumerate(zip(near, dst))]
    for c in loads:
        c.start()
    rows = small.shape[0]
    t = jnp.transpose(jnp.concatenate([small[...], jnp.zeros((128 - rows, 128), F32)], axis=0))[:, 0:rows]
    router[...] = t[0:8]
    mix[...] = t[8:12]
    vec[...] = t[12:14]
    ln1[...] = t[14:15]
    ln2[...] = t[15:16]
    for a, b in zip(loads, copies):
        a.wait()
        b.start()
    for c in copies:
        c.wait()


def final(big, small):
    rows = small.shape[0]
    far, near = pl.BlockSpec(memory_space=pl.ANY), pl.BlockSpec(memory_space=pltpu.VMEM)
    return pl.pallas_call(
        functools.partial(final_kernel, len(big)),
        out_shape=[jax.ShapeDtypeStruct(a.shape, a.dtype) for a in big]
        + [shape(n, rows, dtype=F32) for n in (8, 4, 2, 1, 1)],
        in_specs=[far] * len(big) + [near],
        out_specs=[far] * len(big) + [near] * 5,
        scratch_shapes=[pltpu.VMEM(a.shape, a.dtype) for a in big] + [pltpu.SemaphoreType.DMA((2, len(big)))],
        compiler_params=pltpu.CompilerParams(vmem_limit_bytes=VMEM_LIMIT),
        name="results",
    )(*big, small)


def body(
    tokens, segments, routes, prev_logits, ln1_gain, w_qkv, w_attn, ln2_gain, w_router, const_mix, const_vec,
    expert_in, expert_out, cotangent,
):
    length, width = tokens.shape
    heads = width // HEAD_DIM
    experts = lax.axis_size("expert") * expert_in.shape[0]
    hidden = expert_out.shape[1]
    capacity = length // 2
    slots = experts * capacity
    n_dp = lax.axis_size("dp")
    V = pltpu.VMEM
    DMA = pltpu.SemaphoreType.DMA
    cos, sin = (jnp.asarray(t) for t in rotary_tables(length))
    rT, pT = routes.T, prev_logits.T
    wrT, cmT, cvT = w_router.T, const_mix.T, const_vec.T
    ln1, ln2 = ln1_gain, ln2_gain
    peers = experts - 1

    q, k, v, pw, att, n1, res, target, send, g_rows, high, low = call(
        fwd_kernel,
        [
            shape(length, width), shape(length, width), shape(length, width), shape(heads, length, length),
            shape(length, width), shape(length, width), shape(length, width, dtype=F32),
            shape(length, 128, dtype=F32), shape(experts, capacity, width), shape(experts, capacity, width),
            shape(length, width), shape(length, width),
        ],
        [
            V((length, length), F32), V((3, length, 128), F32), V((128, length), F32), V((slots, length), BF16), V((experts, capacity, width), BF16),
            DMA((peers,)), DMA((peers,)), V((heads, length, length), BF16), V((experts, capacity, width), BF16),
            DMA((width // 128, 2)), DMA((experts + 1,)),
        ],
        (tokens, segments, rT, ln1, w_qkv, w_attn, ln2, cotangent, cos, sin),
        "attention", 0, (13, 18, 19), (0, 4, 5, 7, 8, 9, 10, 11, 12, 14, 15, 16, 20, 21),
    )

    tiles, slabs = 4, 3
    ft = hidden // tiles
    within = n_dp == 8 and experts == 4
    stages = ((("dp", 1), ("dp", 2), ("dp", 4)), (("dp", 2), ("dp", 1), ("dp", 4))) if within else ()
    order = (("expert", 1), ("expert", 2), ("dp", 1), ("dp", 2), ("dp", 4))
    slab_in, slab_out = (2 * tiles, width, ft), (slabs, hidden, width // slabs)

    def part_of(s, n):
        return (s[0], s[1] // n, s[2])

    late = (tiles, width // 2, ft)
    early = (tiles, width // 4, ft)
    f_rows, d_back, g_out, dot_back, meta, *g_in = call(
        functools.partial(expert_kernel, stages),
        [
            shape(experts, capacity, width), shape(experts, capacity, width), shape(*slab_out),
            shape(experts, 8, capacity, dtype=F32), shape(length, 128, dtype=F32),
        ]
        + ([shape(*late), shape(*early)] if within else [shape(*slab_in)]),
        [
            V((experts, capacity, width), BF16), V((slots, width), BF16), V((tiles, slots, ft), BF16),
            V((tiles, slots, 2 * ft), BF16), V((slots, width), F32), V((slots, width), F32),
            V((experts, capacity, width), BF16),
        ]
        + ([V(slab_in, BF16), V(late, BF16)] + [DMA((2 * tiles,))] * 2 + [DMA((tiles,))] * 2 if within else [])
        + [DMA((peers,))] * 4
        + [DMA((2,))]
        + [V((experts, 8, capacity), F32)] * 3
        + [V((128, width), F32), V((3, length, 128), F32)]
        + [DMA((peers,))] * 4,
        (send, g_rows, expert_in, expert_out, high, low, target, rT, pT, wrT, cmT),
        "experts", 1, (0, 12), (1, 2, 3, 4, 5, 11, 13) + ((16, 17) if within else (16,)),
    )

    args = (
        tokens, cotangent, res, meta, dot_back, rT, f_rows, d_back, q, k, v, pw, att, n1, ln1, w_qkv, w_attn, ln2, wrT, cmT, cvT,
        cos, sin,
    )
    n_all = n_dp * experts
    rows = width // n_all if within else width
    outs = [
        shape(length, width), shape(length, width), shape(rows, 3 * width, dtype=F32), shape(rows, width, dtype=F32),
        shape(rows, 128, dtype=F32),
    ]
    scratch = [
        V((128, width), F32), V((2, length, 128), F32), V((length, width), F32), V((length, width), F32),
        V((2, length, 128), F32), V((length, 256), BF16), V((length, width), BF16), V((length, width), F32),
        V((length, width), BF16), V((length, 3 * width), BF16), V((length, width), BF16),
        V((2, length, 128), F32), V((16, width), F32), V((experts, capacity, width), BF16), DMA((peers,)), DMA((peers,)),
        V((heads, length, length), BF16), DMA((3,)),
    ]
    if within:
        args += (g_in[1], g_in[0], g_out)
        outs += [
            shape(rows, 128, dtype=F32),
            shape(width // n_dp, 2 * hidden, dtype=F32), shape(hidden // n_dp, width, dtype=F32)]
        scratch += [
            V(early, BF16), V(part_of(slab_in, 8), BF16), V(part_of(slab_out, 2), BF16),
            V(part_of(slab_out, 4), BF16), V(part_of(slab_out, 8), BF16), DMA((2, 2 * tiles)), DMA((2, 2 * tiles)),
            DMA((3, slabs)), DMA((3, slabs)),
        ]
        for cols in (width, width, width, 512, 256, 256):
            scratch += [V((2 * width >> s, cols // 2), BF16) for s in range(6)] + [DMA((5,)), DMA((5,))]
    plan = (stages, order) if within else ()
    n = len(args)
    staged = (0, 1, 2, 7, 8, 9, 10, 12, 13, 15, 16, 21, 22) + tuple(range(23, n)) + (n, n + 1)
    staged += (n + 6, n + 7) if within else ()
    done = call(functools.partial(bwd_kernel, plan), outs, scratch, args, "backward", 2, (6, 11), staged)
    out, igrad, d_qkv, d_attn, small = done[:5]
    if within:
        out, igrad, d_qkv, d_attn, g_in, g_out, router, mix, vec, ln_one, ln_two = final(
            (out, igrad, d_qkv, d_attn, done[6], done[7]), small
        )
        return (
            out, igrad, ln_one.reshape(rows), d_qkv, d_attn, ln_two.reshape(rows), router.T, mix.T, vec.T,
            g_in[None], g_out[None],
        )
    (g_in,) = g_in
    g_in = jnp.moveaxis(g_in.reshape(tiles, 2, width, ft), 2, 0).transpose(0, 2, 1, 3).reshape(width, 2 * hidden)
    g_out = jnp.moveaxis(g_out, 0, 1).reshape(hidden, width)
    g_in = lax.psum_scatter(g_in, "dp", scatter_dimension=0, tiled=True).astype(F32)
    g_out = lax.psum_scatter(g_out, "dp", scatter_dimension=0, tiled=True).astype(F32)
    d_qkv, d_attn, small = (
        lax.psum_scatter(d, ("dp", "expert"), scatter_dimension=0, tiled=True) for d in (d_qkv, d_attn, small)
    )
    return (
        out, igrad, small[:, 14], d_qkv, d_attn, small[:, 15], small[:, 0:8], small[:, 8:12], small[:, 12:14],
        g_in[None], g_out[None],
    )


def solution(mesh):
    rows = P(("dp", "expert"), None)
    return jax.shard_map(
        body,
        mesh=mesh,
        in_specs=(
            rows, rows, rows, rows, P(), P(), P(), P(), P(), P(), P(),
            P("expert", None, None), P("expert", None, None), rows,
        ),
        out_specs=(
            rows, rows, P(("dp", "expert")), rows, rows, P(("dp", "expert")), rows, rows, rows,
            P("expert", "dp", None), P("expert", "dp", None),
        ),
        check_vma=False,
    )
```

```python
import functools
import math

import jax
import jax.numpy as jnp
import numpy as np
from jax import lax
from jax.experimental import pallas as pl
from jax.experimental.pallas import tpu as pltpu
from jax.sharding import PartitionSpec as P

HEAD_DIM = 64
EPS = 1e-06
MASKED = -1e30
F32 = jnp.float32
BF16 = jnp.bfloat16
VMEM_LIMIT = 62 * 1024 * 1024


def dot(a, b):
    return lax.dot_general(a, b, (((1,), (0,)), ((), ())), preferred_element_type=F32)


def dot_nt(a, b):
    return lax.dot_general(a, b, (((1,), (1,)), ((), ())), preferred_element_type=F32)


def dot_tn(a, b):
    return lax.dot_general(a, b, (((0,), (0,)), ((), ())), preferred_element_type=F32)


def tile(i, size):
    return pl.ds(pl.multiple_of(i * size, size), size)


def rotary_tables(length):
    half = HEAD_DIM // 2
    inverse = np.exp(np.arange(half, dtype=np.float32) * np.float32(-2.0 * math.log(10000.0) / HEAD_DIM))
    angles = np.arange(length, dtype=np.float32)[:, None] * inverse.astype(np.float32)[None, :]
    cos, sin = np.cos(angles), np.sin(angles)
    return (
        np.concatenate([cos] * 4, axis=1).astype(np.float32),
        np.concatenate([-sin, sin] * 2, axis=1).astype(np.float32),
    )


def rotate(x, cos, sin):
    lane = lax.broadcasted_iota(jnp.int32, x.shape, 1)
    front = (lane % HEAD_DIM) < HEAD_DIM // 2
    other = jnp.where(front, pltpu.roll(x, 96, 1), pltpu.roll(x, 32, 1))
    return x * cos + other * sin


def row_mean(x):
    return jnp.mean(x, axis=-1, keepdims=True)


def as_row(gain):
    return gain[...].reshape(1, gain.shape[0])


def pick(x, lane, index):
    return jnp.sum(jnp.where(lane == index, x, 0.0), axis=-1, keepdims=True)


def half_mask(x, lane, which):
    keep = (lane < HEAD_DIM) if which == 0 else (lane >= HEAD_DIM)
    return jnp.where(keep, x, jnp.zeros_like(x))


MESH = pl.DeviceIdType.MESH


def flip(i, m):
    return i + m * (1 - 2 * ((i // m) % 2))


def side(mask):
    axis, m = mask
    return (lax.axis_index(axis) // m) % 2


def partner(mask):
    axis, m = mask
    return {axis: flip(lax.axis_index(axis), m)}


def across(r):
    e = lax.axis_index("expert")
    for m in (1, 2):
        if r & m:
            e = flip(e, m)
    return e


def greet(masks, peers=0, wait=True):
    barrier = pltpu.get_barrier_semaphore()
    for mask in masks:
        pl.semaphore_signal(barrier, inc=1, device_id=partner(mask), device_id_type=MESH)
    for r in range(1, peers + 1):
        pl.semaphore_signal(barrier, inc=1, device_id={"expert": across(r)}, device_id_type=MESH)
    if wait:
        pl.semaphore_wait(barrier, len(masks) + peers)


def exchange(src, dst, send_sem, recv_sem):
    return {
        r: pltpu.make_async_remote_copy(
            src.at[r], dst.at[r], send_sem.at[r - 1], recv_sem.at[r - 1],
            device_id={"expert": across(r)}, device_id_type=MESH,
        )
        for r in range(src.shape[0] - 1, 0, -1)
    }


def half_copy(src, dst, mask, rows, send_sem, recv_sem):
    start = pl.multiple_of((1 - side(mask)) * rows, 16)
    return pltpu.make_async_remote_copy(
        src.at[pl.ds(start, rows)], dst, send_sem, recv_sem, device_id=partner(mask), device_id_type=MESH
    )


def half_add(src, dst, mask, rows, out=None):
    start = side(mask) * rows
    step = 48 if rows % 48 == 0 else 64
    out = dst if out is None else out

    @pl.loop(0, rows // step)
    def _(i):
        here = pl.ds(pl.multiple_of(i * step, 16), step)
        mine = src[pl.ds(pl.multiple_of(start + i * step, 16), step)].astype(F32)
        out[here] = (mine + dst[here].astype(F32)).astype(out.dtype)


def place_of(shard, masks):
    place = 0
    for m in masks:
        place = 2 * place + (shard // m) % 2
    return place


def fwd_kernel(
    tok, seg, rT, ln1, wqkv, wattn, ln2, cot, cos, sin,
    q_out, k_out, v_out, pw_out, att_out, n1_out, res_out, tg, send_out, g_rows, high_out, low_out,
    bias, rb, pb, onehot, g_out, send_sem, recv_sem, pw, send, pw_sem, row_sem,
):
    length, width = tok.near.shape
    capacity = length // 2
    experts = send.shape[0]

    for ref in (cot, tok, wqkv, cos, sin, wattn):
        ref.start()
    q, k, v, att, n1, res = (ref.near for ref in (q_out, k_out, v_out, att_out, n1_out, res_out))
    n2b, n2l = high_out.near, low_out.near
    greet((), experts - 1, wait=False)
    for kk in range(2):
        rb[kk] = jnp.transpose(jnp.broadcast_to(rT[kk : kk + 1, :].astype(F32), (128, length)))
    all_lane = lax.broadcasted_iota(jnp.int32, (length, 128), 1).astype(F32)
    count = ((rb[0] == all_lane).astype(F32) + (rb[1] == all_lane).astype(F32)).astype(BF16)

    t_id = lax.broadcasted_iota(jnp.int32, (length, length), 0)
    before = (t_id > lax.broadcasted_iota(jnp.int32, (length, length), 1)).astype(F32).astype(BF16)
    place = jnp.where(all_lane < experts, dot(before, count) + all_lane * float(capacity) + 1.0, 0.0)
    slot = [jnp.sum(jnp.where(rb[kk] == all_lane, place, 0.0), axis=-1, keepdims=True) - 1.0 for kk in range(2)]
    tg[...] = jnp.where(all_lane == 0, slot[0], jnp.where(all_lane == 1, slot[1], 0.0))

    target = jnp.transpose(tg[...])
    pb[...] = target

    cot = cot.wait()
    pl.semaphore_wait(pltpu.get_barrier_semaphore(), experts - 1)
    copies = exchange(g_out, g_rows, send_sem, recv_sem)
    own_rows = pltpu.make_async_copy(g_out.at[0], g_rows.at[0], row_sem.at[experts])
    for r in range(experts - 1, -1, -1):
        s_id = (lax.broadcasted_iota(jnp.int32, (capacity, length), 0) + across(r) * capacity).astype(F32)
        here = (pb[0:1] == s_id).astype(F32) + (pb[1:2] == s_id).astype(F32)
        onehot[r * capacity : (r + 1) * capacity] = here.astype(BF16)
        g_out[r] = dot(here.astype(BF16), cot[...]).astype(BF16)
        (copies[r] if r else own_rows).start()
    tok = tok.wait()

    @pl.loop(0, length // 256)
    def _(i):
        rows = tile(i, 256)
        x = tok[rows].astype(F32)
        r = lax.rsqrt(row_mean(x * x) + EPS)
        n1[rows] = (x * r * as_row(ln1)).astype(BF16)

    n1_out.start()
    wqkv, cos, sin = wqkv.wait(), cos.wait(), sin.wait()

    @pl.loop(0, width // 256)
    def _(j):
        for kind, dst in enumerate((q, k, v)):
            cols = pl.ds(pl.multiple_of(kind * width + j * 256, 256), 256)
            both = dot(n1[...], wqkv[:, cols])
            for part in range(2):
                x = both[:, part * 128 : part * 128 + 128]
                if kind < 2:
                    x = rotate(x, cos[...], sin[...])
                if kind == 0:
                    x = x * 0.125
                dst[:, pl.ds(pl.multiple_of(j * 256 + part * 128, 128), 128)] = x.astype(BF16)

    for done in (q_out, k_out, v_out):
        done.start()

    seg_f = seg[...].astype(F32)
    rb[2] = jnp.transpose(jnp.broadcast_to(seg_f, (128, length)))

    @pl.loop(0, length // 128)
    def _(i):
        rows = tile(i, 128)
        row_id = lax.broadcasted_iota(jnp.int32, (128, length), 0) + i * 128
        col_id = lax.broadcasted_iota(jnp.int32, (128, length), 1)
        same = rb[2, rows, 0:1] == seg_f
        bias[rows] = jnp.where(same & (row_id >= col_id), 0.0, MASKED)

    block = length // 2

    def weights_copy(j, b):
        at = (pl.ds(2 * j, 2), slice(b * block, (b + 1) * block), slice(0, (b + 1) * block))
        return pltpu.make_async_copy(pw.at[at], pw_out.at[at], pw_sem.at[j, b])

    def heads(j):
        cols = tile(j, 128)
        for b in range(2):
            rows = slice(b * block, (b + 1) * block)
            nk = (b + 1) * block
            qlane = lax.broadcasted_iota(jnp.int32, (block, 128), 1)
            klane = lax.broadcasted_iota(jnp.int32, (nk, 128), 1)
            acc = jnp.zeros((block, 128), F32)
            for h in range(2):
                s = dot_nt(half_mask(q[rows, cols], qlane, h), k[0:nk, cols]) + bias[rows, 0:nk]
                m = jnp.max(s, axis=-1, keepdims=True)
                e = jnp.exp(s - m)
                w = (e * (1.0 / jnp.sum(e, axis=-1, keepdims=True))).astype(BF16)
                pw[2 * j + h, rows, 0:nk] = w
                acc = acc + dot(w, half_mask(v[0:nk, cols], klane, h))
            att[rows, cols] = acc.astype(BF16)
            weights_copy(j, b).start()

    @pl.loop(0, width // 256)
    def _(jj):
        heads(2 * jj)
        heads(2 * jj + 1)

    att_out.start()
    wattn = wattn.wait()

    res[...] = tok[...].astype(F32) + dot(att[...], wattn[...])

    res_out.start()

    @pl.loop(0, length // 256)
    def _(i):
        rows = tile(i, 256)
        x = res[rows]
        n2 = x * lax.rsqrt(row_mean(x * x) + EPS) * as_row(ln2)
        high = n2.astype(BF16)
        n2b[rows] = high
        n2l[rows] = (n2 - high.astype(F32)).astype(BF16)

    high_out.start()
    low_out.start()

    @pl.loop(0, experts)
    def _(e):
        send[e] = dot(onehot[tile(e, capacity)], n2b[...]).astype(BF16)
        pltpu.make_async_copy(send.at[e], send_out.at[e], row_sem.at[e]).start()

    for ref in (q_out, k_out, v_out, att_out, n1_out, res_out, high_out, low_out):
        ref.wait()

    @pl.loop(0, width // 128)
    def _(j):
        for b in range(2):
            weights_copy(j, b).wait()

    @pl.loop(0, experts)
    def _(e):
        pltpu.make_async_copy(send.at[e], send_out.at[e], row_sem.at[e]).wait()

    own_rows.wait()
    for c in copies.values():
        c.wait()


def expert_kernel(stages, xs, g_rows, win, wout, n2b, n2l, tg, rT, pT, wrT, cmT, *refs):
    f_out, d_back, go_out, dot_back, meta = refs[:5]
    refs = refs[:3] + refs[5:]
    f_rows, go = f_out.near, go_out.near
    if stages:
        late_out, early_out = refs[3:5]
        p_late = late_out.near
        refs = refs[5:]
    else:
        gi_out = refs[3]
        gi = gi_out.near
        refs = refs[4:]
    xr, dy, hid, dgu, f_acc, d_acc, d_out = refs[:7]
    refs = refs[7:]
    if stages:
        gi, p_first, p_early, in_send, in_recv, e_send, e_recv, e_out = refs[:8]
        refs = refs[8:]
    x_send, x_recv, d_send, d_recv, own_sem, gates, gate_row, dot_row, wcat, rb, r_send, r_recv, s_send, s_recv = refs
    groups, capacity, _ = xs.shape
    hidden, width = wout.near.shape[1:]
    tiles, rows_all, ft = hid.shape
    slabs = go.shape[0]
    shards = 2 ** len(stages[0]) if stages else 0
    near = rows_all // 2

    greet([s[0] for s in stages], groups - 1)
    copies = exchange(xs, xr, x_send, x_recv)
    n2b.start()
    n2l.start()
    for c in copies.values():
        c.start()
    own_x = pltpu.make_async_copy(xs.at[0], xr.at[0], own_sem.at[0])
    own_x.start()
    for ref in (g_rows, win, wout):
        ref.start()
    n2b, n2l = n2b.wait(), n2l.wait()
    length = n2b.shape[0]
    wcat[...] = jnp.zeros_like(wcat)
    wcat[0:8] = wrT[...]
    wcat[8:12] = cmT[...]
    w_high = wcat[...].astype(BF16)
    w_low = (wcat[...] - w_high.astype(F32)).astype(BF16)

    for kk in range(2):
        rb[kk] = jnp.transpose(jnp.broadcast_to(rT[kk : kk + 1, :].astype(F32), (128, length)))
    rb[2] = jnp.transpose(jnp.concatenate([pT[...], jnp.zeros((120, length), F32)], axis=0))

    @pl.loop(0, length // 256)
    def _(i):
        rows = tile(i, 256)
        lane = lax.broadcasted_iota(jnp.int32, (256, 128), 1)
        lane_f = lane.astype(F32)
        high = n2b[rows]
        mixed = dot_nt(high, w_high) + dot_nt(high, w_low) + dot_nt(n2l[rows], w_high)
        logits = mixed + rb[2, rows]
        hits = [(rb[kk, rows] == lane_f).astype(F32) for kk in range(2)]
        chosen = [jnp.sum(h * logits, axis=-1, keepdims=True) for h in hits]
        top = jnp.maximum(chosen[0], chosen[1])
        e = [jnp.exp(c - top) for c in chosen]
        inv = 1.0 / (e[0] + e[1])
        gates = [v_ * inv for v_ in e]
        shares = []
        for j in range(2):
            a0, a1 = pick(mixed, lane, 8 + 2 * j), pick(mixed, lane, 9 + 2 * j)
            mx = jnp.maximum(a0, a1)
            b0, b1 = jnp.exp(a0 - mx), jnp.exp(a1 - mx)
            binv = 1.0 / (b0 + b1)
            shares.append((b0 * binv, b1 * binv))
        gate_sum = gates[0] * hits[0] + gates[1] * hits[1]
        cg = [pick(gate_sum, lane, 6), pick(gate_sum, lane, 7)]
        keep = pick(gate_sum, lane, 5) + cg[0] * shares[0][0] + cg[1] * shares[1][0]
        values = (
            gates[0], gates[1], keep, cg[0], cg[1], shares[0][0], shares[0][1], shares[1][0], shares[1][1],
        )
        out = tg[rows]
        for n, value in enumerate(values):
            out = jnp.where(lane == n + 2, value, out)
        meta[rows] = out

    row_copies = exchange(gate_row, gates, r_send, r_recv)
    for r in range(groups - 1, -1, -1):
        slot = (lax.broadcasted_iota(jnp.int32, (length, capacity), 1) + across(r) * capacity).astype(F32)
        gate = jnp.where(meta[:, 0:1] == slot, meta[:, 2:3], jnp.where(meta[:, 1:2] == slot, meta[:, 3:4], 0.0))
        line = jnp.broadcast_to(jnp.sum(gate, axis=0, keepdims=True), (8, capacity))
        if r:
            gate_row[r] = line
            row_copies[r].start()
        else:
            gates[0] = line

    def gated(r):
        if r:
            row_copies[r].wait()
        gate = jnp.transpose(jnp.broadcast_to(gates[r, 0:1], (128, capacity)))[:, 0:1]
        dy[r * capacity : (r + 1) * capacity] = (g_rows[r].astype(F32) * gate).astype(BF16)

    def cols_of(f):
        return tile(f, ft), pl.ds(pl.multiple_of(hidden + f * ft, ft), ft)

    def work(f, part):
        gate_cols, up_cols = cols_of(f)
        rows = slice(part * near, (part + 1) * near)
        x = xr[2 * part : 2 * part + 2].reshape(near, width)
        gate = dot(x, win[0, :, gate_cols])
        up = dot(x, win[0, :, up_cols])
        dh = dot_nt(dy[rows], wout[0, gate_cols, :])
        sig = 1.0 / (1.0 + jnp.exp(-gate))
        silu = gate * sig
        h = (silu * up).astype(BF16)
        da = (dh * up * (sig + silu * (1.0 - sig))).astype(BF16)
        db = (dh * silu).astype(BF16)
        hid[f, rows] = h
        dgu[f, rows, 0:ft] = da
        dgu[f, rows, ft : 2 * ft] = db

    def gather(f, part):
        gate_cols, up_cols = cols_of(f)
        rows = slice(part * near, (part + 1) * near)
        y = dot(hid[f, rows], wout[0, gate_cols, :])
        d = dot_nt(dgu[f, rows, 0:ft], win[0, :, gate_cols]) + dot_nt(dgu[f, rows, ft : 2 * ft], win[0, :, up_cols])

        @pl.when(f == 0)
        def _():
            f_acc[rows] = y
            d_acc[rows] = d

        @pl.when(f > 0)
        def _():
            f_acc[rows] += y
            d_acc[rows] += d

    def in_copy(part, f, p):
        dst = (p_first if part == 0 else p_late).at[2 * (f - part * tiles // 2) + p]
        slab = 2 * f + p
        return half_copy(gi.at[slab], dst, stages[p][0], width // 2, in_send.at[slab], in_recv.at[slab]), dst

    def early_store(slab):
        return pltpu.make_async_copy(p_early.at[slab], early_out.at[slab], e_out.at[slab])

    def early_copy(slab):
        return half_copy(
            p_first.at[slab], p_early.at[slab], stages[slab % 2][1], width // 4, e_send.at[slab], e_recv.at[slab]
        )

    own_x.wait()
    g_rows = g_rows.wait()
    gated(0)
    gated(1)
    copies[1].wait()

    win, wout = win.wait(), wout.wait()

    @pl.loop(0, tiles)
    def _(f):
        work(f, 0)
        gather(f, 0)

    gated(3)
    gated(2)
    copies[3].wait()
    copies[2].wait()

    for part in range(2):

        @pl.loop(part * (tiles // 2), (part + 1) * (tiles // 2))
        def _(f):
            work(f, 1)
            for p in range(2):
                d = dot_tn(xr[...].reshape(rows_all, width), dgu[f, :, p * ft : (p + 1) * ft])
                if not stages:
                    gi[2 * f + p] = d.astype(BF16)
                    continue
                size = width // shards
                for j in range(shards):
                    at = place_of(j, [m for _, m in stages[p]]) * size
                    gi[2 * f + p, at : at + size] = d[j * size : (j + 1) * size].astype(BF16)
                in_copy(part, f, p)[0].start()
            gather(f, 1)

    d_copies = exchange(d_out, d_back, d_send, d_recv)
    dot_copies = exchange(dot_row, dot_back, s_send, s_recv)
    own_d = pltpu.make_async_copy(d_out.at[0], d_back.at[0], own_sem.at[1])
    for r in range(groups - 1, -1, -1):
        rows = slice(r * capacity, (r + 1) * capacity)
        y = f_acc[rows]
        f_rows[r] = y.astype(BF16)
        dots = jnp.sum(y * g_rows[r].astype(F32), axis=-1, keepdims=True)
        as_rows = jnp.transpose(jnp.broadcast_to(dots, (capacity, 128)))[0:8]
        d_out[r] = d_acc[rows].astype(BF16)
        if r:
            dot_row[r] = as_rows
            dot_copies[r].start()
            d_copies[r].start()
        else:
            dot_back[0] = as_rows
            own_d.start()
    f_out.start()

    for c in range(slabs):
        cols = slice(c * (width // slabs), (c + 1) * (width // slabs))

        @pl.loop(0, tiles)
        def _(t):
            d = dot_tn(hid[t], dy[:, cols]).astype(BF16)
            if not stages:
                go[c, tile(t, ft)] = d
                return
            size = hidden // shards
            for i in range(ft // size):
                at = place_of(t * (ft // size) + i, [m for _, m in stages[0]])
                go[c, tile(at, size)] = d[i * size : (i + 1) * size]

    go_out.start()
    if stages:
        for part in range(2):
            for f in range(part * (tiles // 2), (part + 1) * (tiles // 2)):
                for p in range(2):
                    copy, dst = in_copy(part, f, p)
                    copy.wait()
                    half_add(gi.at[2 * f + p], dst, stages[p][0], width // 2)
                    if part == 0:
                        early_copy(2 * f + p).start()
        late_out.start()
        for slab in range(tiles):
            early_copy(slab).wait()
            half_add(p_first.at[slab], p_early.at[slab], stages[slab % 2][1], width // 4)
            early_store(slab).start()
        late_out.wait()
        for slab in range(tiles):
            early_store(slab).wait()
    else:
        gi_out.start()
        gi_out.wait()
    f_out.wait()
    go_out.wait()
    own_d.wait()
    for r, c in d_copies.items():
        dot_copies[r].wait()
        c.wait()


def out_start(copy, i, s):
    copy(i, s).start()


def as_columns(x):
    row = jnp.sum(x, axis=0, keepdims=True)
    return jnp.transpose(jnp.broadcast_to(row, (128, row.shape[1])))


class Slab:
    def __init__(self, order, refs):
        self.order = order
        self.bufs, (self.send, self.recv) = refs[:6], refs[6:]
        self.bits = [m * (1 if a == "expert" else lax.axis_size("expert")) for a, m in order]
        self.out = ()

    def store(self, value, piece):
        total = 2 ** len(self.order)
        size = value.shape[0] // total
        for j in range(total):
            row = place_of(j, self.bits) * 2 * size
            mine = value[j * size : (j + 1) * size]
            both = jnp.concatenate([mine[:, 0:128], mine[:, 128:256]], axis=0)
            self.bufs[0][row : row + 2 * size, piece * 128 : piece * 128 + 128] = both.astype(BF16)

    def copy(self, s):
        dst = self.bufs[s + 1]
        return half_copy(self.bufs[s], dst, self.order[s], dst.shape[0], self.send.at[s], self.recv.at[s])

    def start(self):
        self.copy(0).start()

    def done(self, s):
        self.copy(s).wait()
        rows = self.bufs[s + 1].shape[0]
        if s < 4:
            half_add(self.bufs[s], self.bufs[s + 1], self.order[s], rows)
            self.copy(s + 1).start()
            return
        mine = self.bufs[4][pl.ds(pl.multiple_of(side(self.order[4]) * rows, 16), rows)]
        total = mine.astype(F32) + self.bufs[5][...].astype(F32)
        for piece, parts in enumerate(self.out):
            for n, (ref, at) in enumerate(parts):
                half = slice(n * rows // 2, (n + 1) * rows // 2)
                ref[:, at : at + 128] = total[half, piece * 128 : piece * 128 + 128]


def bwd_kernel(plan, *refs):
    (
        tok, cot, res, meta, dot_back, rT, f_rows, d_back, q, k, v, pw_far, att, n1, ln1, wqkv, wattn, ln2, wrT, cmT, cvT, cos, sin,
    ) = refs[:23]
    refs = refs[23:]
    if plan:
        stages, order = plan
        p_early, p_late, p_out, out_s, igrad_s, d_qkv, d_attn, d_small, d_ln, g_in_s, g_out_s = refs[:11]
        g_in, g_out = g_in_s.near, g_out_s.near
        refs = refs[11:]
    else:
        out_s, igrad_s, d_qkv, d_attn, d_small = refs[:5]
        refs = refs[5:]
    out, igrad = out_s.near, igrad_s.near
    wcat, rb, fk0, dsn, dots, dcat, n2b, dres, dbr, dproj, datt, dkv, lnacc, f_back, f_send, f_recv, pw, own_sem = refs[:18]
    refs = refs[18:]
    length, width = tok.near.shape
    experts, capacity, _ = f_rows.shape
    slots = experts * capacity
    block = length // 2

    weights = []
    for b in range(2):
        at = (slice(0, pw.shape[0]), slice(b * block, (b + 1) * block), slice(0, (b + 1) * block))
        weights.append(pltpu.make_async_copy(pw_far.at[at], pw.at[at], own_sem.at[b]))
    own_f = pltpu.make_async_copy(f_rows.at[0], f_back.at[0], own_sem.at[2])
    for ref in (d_back, cot, res):
        ref.start()
    greet(order[2:] if plan else (), experts - 1)
    f_copies = exchange(f_rows, f_back, f_send, f_recv)

    acts = {}
    if plan:
        in1, in2, out0, out1, out2, in_send, in_recv, out_send, out_recv = refs[:9]
        slab_refs = [refs[9 + 8 * n : 17 + 8 * n] for n in range(6)]
        late = p_late.near.shape[0]
        slabs_in = late + p_early.near.shape[0]
        ft = p_late.near.shape[2]
        hidden = g_in.shape[1] // 2

        def in_refs(i, s, far=False):
            n = i - (slabs_in - late)
            p = "far" if far else "near"
            first = getattr(p_early, p).at[i] if n < 0 else in1.at[n]
            return (getattr(p_late, p).at[n], first) if s == 0 else (first, in2.at[i])

        def in_copy(i, s):
            src, dst = in_refs(i, s, True)
            return half_copy(src, dst, stages[i % 2][s + 1], dst.shape[0], in_send.at[s, i], in_recv.at[s, i])

        def in_done(i, s):
            in_copy(i, s).wait()
            src, dst = in_refs(i, s)
            if s == 0:
                half_add(src, dst, stages[i % 2][1], dst.shape[0])
                in_copy(i, 1).start()
            else:
                to = (i % 2) * hidden + (i // 2) * ft
                half_add(src, dst, stages[i % 2][2], dst.shape[0], g_in.at[:, to : to + ft])

        def out_refs(i, s, far=False):
            return ((p_out.far if far else p_out.near, out0), (out0, out1), (out1, out2))[s]

        def out_copy(i, s):
            src, dst = out_refs(i, s, True)
            return half_copy(
                src.at[i], dst.at[i], stages[0][s], dst.shape[1], out_send.at[s, i], out_recv.at[s, i]
            )

        def out_done(i, s):
            out_copy(i, s).wait()
            src, dst = out_refs(i, s)
            wide = out2.shape[2]
            into = g_out.at[:, i * wide : (i + 1) * wide] if s == 2 else None
            half_add(src.at[i], dst.at[i], stages[0][s], dst.shape[1], into)
            if s < 2:
                out_copy(i, s + 1).start()

        turned = order[:3] + (order[4], order[3])
        attn_slab, q0, q1, q2a, q2b, ln_slab = (
            Slab(turned if n == 4 else order, r) for n, r in enumerate(slab_refs)
        )

        def columns(ref, at):
            return ((ref, at), (ref, at + 128))

        attn_slab.out = [columns(d_attn, 256 * n) for n in range(3)]
        q0.out = [columns(d_qkv, kind * width) for kind in range(3)]
        q1.out = [columns(d_qkv, kind * width + 256) for kind in range(3)]
        q2a.out = [columns(d_qkv, kind * width + 512) for kind in range(2)]
        q2b.out = [columns(d_qkv, 2 * width + 512)]
        ln_slab.out = [((d_ln, 0), (d_small, 0))]

        for i, n in ((4, 0), (5, 0), (0, 1), (3, 1), (1, 1), (6, 0)):
            in_copy(i, n).start()
        out_copy(1, 0).start()
        acts = {
            "token": [(out_start, out_copy, 0, 0), (in_done, 4, 0), (in_done, 5, 0), (in_done, 0, 1)],
            "attn": [(attn_slab.start,), (in_done, 3, 1)],
            "part0": [
                (out_start, in_copy, 2, 1), (q0.start,), (in_done, 1, 1), (out_start, out_copy, 2, 0),
                (attn_slab.done, 0), (in_done, 6, 0), (out_done, 1, 0),
            ],
            "part1": [(out_start, in_copy, 7, 0), (q1.start,), (in_done, 4, 1), (q0.done, 0), (in_done, 5, 1)],
            "part2": [
                (q2a.start,), (q2b.start,), (attn_slab.done, 1), (q1.done, 0), (in_done, 2, 1), (out_done, 0, 0),
            ],
            "norm": [(out_done, 1, 1), (q2a.done, 0), (in_done, 6, 1), (q2b.done, 0), (q0.done, 1)],
            "input": [(ln_slab.start,)],
            "output": [
                (out_done, 0, 1), (q1.done, 1), (ln_slab.done, 0), (out_done, 2, 0), (out_done, 1, 2), (q2a.done, 1),
                (in_done, 7, 0), (q2b.done, 1), (out_done, 0, 2), (ln_slab.done, 1), (attn_slab.done, 2),
                (out_done, 2, 1), (q0.done, 2), (in_done, 7, 1), (g_in_s.start,), (attn_slab.done, 3), (q1.done, 2),
                (q2a.done, 2), (out_done, 2, 2), (g_out_s.start,), (q0.done, 3), (q2b.done, 2), (attn_slab.done, 4),
                (ln_slab.done, 2), (q1.done, 3), (q2a.done, 3), (q0.done, 4), (q2b.done, 3), (ln_slab.done, 3),
                (q1.done, 4), (q2b.done, 4), (q2a.done, 4), (ln_slab.done, 4),
            ],
        }
    for c in f_copies.values():
        c.start()
    late_refs = (wattn, att, q, k, v, cos, sin, n1, wqkv, tok)
    for ref in ((p_early, p_late, p_out) if plan else ()) + late_refs[:5]:
        ref.start()
    for c in weights:
        c.start()
    own_f.start()
    for ref in late_refs[5:]:
        ref.start()
    d_back = d_back.wait()

    def act(name):
        for f, *a in acts.get(name, ()):
            f(*a)

    wcat[...] = jnp.zeros_like(wcat)
    wcat[0:8] = wrT[...]
    wcat[8:12] = cmT[...]
    for kk in range(2):
        rb[kk] = jnp.transpose(jnp.broadcast_to(rT[kk : kk + 1, :].astype(F32), (128, length)))

    def chosen(rows, wide):
        slot = lax.broadcasted_iota(jnp.int32, (wide, slots), 1)
        r = slot // capacity
        e = jnp.zeros_like(slot)
        for n in range(experts):
            e = jnp.where(r == n, across(n), e)
        s_id = (slot - r * capacity + e * capacity).astype(F32)
        return meta[rows, 0:1] == s_id, meta[rows, 1:2] == s_id

    @pl.loop(0, length // 256)
    def _(i):
        rows = tile(i, 256)
        masks = chosen(rows, 256)
        either = (masks[0] | masks[1]).astype(F32).astype(BF16)
        dsn[rows] = dot(either, d_back[...].reshape(slots, width))
        line = jnp.concatenate([dot_back[r, 0:1] for r in range(experts)], axis=1)
        lane = lax.broadcasted_iota(jnp.int32, (256, 128), 1)
        for n, c in enumerate(masks):
            dots[n, rows] = jnp.where(lane == 0, jnp.sum(jnp.where(c, line, 0.0), axis=-1, keepdims=True), 0.0)

    cot, res = cot.wait(), res.wait()
    w_high = wcat[...].astype(BF16)
    lnacc[...] = jnp.zeros_like(lnacc)

    @pl.loop(0, length // 64)
    def _(i):
        rows = tile(i, 64)
        lane = lax.broadcasted_iota(jnp.int32, (64, 128), 1)
        lane_f = lane.astype(F32)
        m = meta[rows]
        g0, g1, keep = m[:, 2:3], m[:, 3:4], m[:, 4:5]
        cg = (m[:, 5:6], m[:, 6:7])
        shares = ((m[:, 7:8], m[:, 8:9]), (m[:, 9:10], m[:, 10:11]))
        g = cot[rows].astype(F32)
        x = res[rows]
        r2 = lax.rsqrt(row_mean(x * x) + EPS)
        xr = x * r2
        n2 = xr * as_row(ln2)
        n2b[rows] = n2.astype(BF16)
        cv = (cvT[0:1, :], cvT[1:2, :])
        fk0[rows] = x + keep * n2 + (cg[0] * shares[0][1]) * cv[0] + (cg[1] * shares[1][1]) * cv[1]
        gn2 = jnp.sum(g * n2, axis=-1, keepdims=True)
        gcv = [jnp.sum(g * c, axis=-1, keepdims=True) for c in cv]
        hits = [(rb[kk, rows] == lane_f).astype(F32) for kk in range(2)]
        special = jnp.where(lane == 5, gn2, 0.0)
        for j in range(2):
            special = jnp.where(lane == 6 + j, shares[j][0] * gn2 + shares[j][1] * gcv[j], special)
        dg = [
            jnp.sum(h * special + dots[n, rows], axis=-1, keepdims=True)
            for n, h in enumerate(hits)
        ]
        mean_dg = g0 * dg[0] + g1 * dg[1]
        dc0, dc1 = g0 * (dg[0] - mean_dg), g1 * (dg[1] - mean_dg)
        cat = hits[0] * dc0 + hits[1] * dc1
        for j in range(2):
            dm0, dm1 = cg[j] * gn2, cg[j] * gcv[j]
            mean_dm = shares[j][0] * dm0 + shares[j][1] * dm1
            cat = jnp.where(lane == 8 + 2 * j, shares[j][0] * (dm0 - mean_dm), cat)
            cat = jnp.where(lane == 9 + 2 * j, shares[j][1] * (dm1 - mean_dm), cat)
        dcat[rows, 0:128] = cat.astype(BF16)
        vecs = jnp.where(lane == 12, cg[0] * shares[0][1], 0.0)
        vecs = jnp.where(lane == 13, cg[1] * shares[1][1], vecs)
        dcat[rows, 128:256] = vecs.astype(BF16)
        dn2 = keep * g + dsn[rows] + dot(cat.astype(BF16), w_high)
        lnacc[0:8] += jnp.sum((dn2 * xr).reshape(8, 8, width), axis=0)
        dn = dn2 * as_row(ln2)
        dr = g + r2 * dn - xr * (r2 * r2) * row_mean(dn * x)
        dres[rows] = dr
        dbr[rows] = dr.astype(BF16)

    if plan:
        for ref in (p_early, p_late, p_out):
            ref.wait()
    act("token")
    wattn, att = wattn.wait(), att.wait()
    @pl.loop(0, width // 256)
    def _(j):
        cols = tile(j, 256)
        datt[:, cols] = dot_nt(dbr[...], wattn[cols, :]).astype(BF16)

    for j in range(width // 256):
        cols = slice(j * 256, (j + 1) * 256)
        d = dot_tn(att[...], dbr[:, cols])
        if plan:
            attn_slab.store(d, j)
        else:
            d_attn[:, cols] = d
    act("attn")
    q, k, v, cos, sin, n1 = (ref.wait() for ref in (q, k, v, cos, sin, n1))
    for c in weights:
        c.wait()

    for part in range(3):

        @pl.loop(2 * part, 2 * part + 2)
        def _(j):
            cols = tile(j, 128)
            dkv[...] = jnp.zeros_like(dkv)
            for b in range(2):
                rows = slice(b * block, (b + 1) * block)
                nk = (b + 1) * block
                qlane = lax.broadcasted_iota(jnp.int32, (block, 128), 1)
                klane = lax.broadcasted_iota(jnp.int32, (nk, 128), 1)
                do = datt[rows, cols]
                prod = do.astype(F32) * att[rows, cols].astype(F32)
                dq = jnp.zeros((block, 128), F32)
                for h in range(2):
                    delta = jnp.sum(half_mask(prod, qlane, h), axis=-1, keepdims=True)
                    dom = half_mask(do, qlane, h)
                    dp = dot_nt(dom, v[0:nk, cols])
                    w = pw[2 * j + h, rows, 0:nk]
                    ds = (w.astype(F32) * (dp - delta)).astype(BF16)
                    dq = dq + dot(ds, half_mask(k[0:nk, cols], klane, h))
                    dkv[0, 0:nk] += dot_tn(ds, half_mask(q[rows, cols], qlane, h))
                    dkv[1, 0:nk] += dot_tn(w, dom)
                dproj[rows, cols] = rotate(dq * 0.125, cos[rows], -sin[rows]).astype(BF16)
            dproj[:, pl.ds(pl.multiple_of(width + j * 128, 128), 128)] = rotate(dkv[0], cos[...], -sin[...]).astype(BF16)
            dproj[:, pl.ds(pl.multiple_of(2 * width + j * 128, 128), 128)] = dkv[1].astype(BF16)

        for kind in range(3):
            cols = slice(kind * width + part * 256, kind * width + part * 256 + 256)
            d = dot_tn(n1[...], dproj[:, cols])
            if not plan:
                d_qkv[:, cols] = d
            elif part < 2:
                (q0, q1)[part].store(d, kind)
            elif kind < 2:
                q2a.store(d, kind)
            else:
                q2b.store(d, 0)
        act(f"part{part}")

    wqkv = wqkv.wait()

    @pl.loop(0, width // 256)
    def _(j):
        cols = tile(j, 256)
        dsn[:, cols] = dot_nt(dproj[...], wqkv[cols, :])

    act("norm")
    tok = tok.wait()

    @pl.loop(0, length // 64)
    def _(i):
        rows = tile(i, 64)
        x = tok[rows].astype(F32)
        r1 = lax.rsqrt(row_mean(x * x) + EPS)
        xr = x * r1
        d = dsn[rows]
        dn = d * as_row(ln1)
        lnacc[8:16] += jnp.sum((d * xr).reshape(8, 8, width), axis=0)
        igrad[rows] = (dres[rows] + r1 * dn - xr * (r1 * r1) * row_mean(dn * x)).astype(BF16)

    lanes = lax.broadcasted_iota(jnp.int32, (width, 128), 1)
    small = dot_tn(n2b[...], dcat[:, 0:128]) + dot_tn(cot[...], dcat[:, 128:256])
    small = small + jnp.where(lanes == 14, as_columns(lnacc[8:16]), 0.0)
    small = small + jnp.where(lanes == 15, as_columns(lnacc[0:8]), 0.0)
    if plan:
        ln_slab.store(jnp.concatenate([small, small], axis=1), 0)
    else:
        d_small[...] = small
    igrad_s.start()
    act("input")

    own_f.wait()
    for c in f_copies.values():
        c.wait()

    @pl.loop(0, length // 256)
    def _(i):
        rows = tile(i, 256)
        first, second = chosen(rows, 256)
        mix = jnp.where(first, meta[rows, 2:3], jnp.where(second, meta[rows, 3:4], 0.0)).astype(BF16)
        out[rows] = (fk0[rows] + dot(mix, f_back[...].reshape(slots, width))).astype(BF16)

    out_s.start()
    act("output")
    out_s.wait()
    igrad_s.wait()
    if plan:
        g_in_s.wait()
        g_out_s.wait()


def shape(*s, dtype=BF16):
    return jax.ShapeDtypeStruct(s, dtype)


class Staged:
    def __init__(self, far, near, sem, out):
        self.far, self.near = far, near
        src, dst = (near, far) if out else (far, near)
        self.copy = lambda: pltpu.make_async_copy(src, dst, sem)

    def start(self):
        self.copy().start()

    def wait(self):
        self.copy().wait()
        return self.near


def call(kernel, outs, scratch, args, name, collective_id, far, staged):
    shapes = [jax.ShapeDtypeStruct(a.shape, a.dtype) for a in args] + list(outs)
    specs = [
        pl.BlockSpec(memory_space=pl.ANY if n in far or n in staged else pltpu.VMEM) for n in range(len(shapes))
    ]
    own = len(shapes) + len(scratch)
    extra = [pltpu.VMEM(shapes[n].shape, shapes[n].dtype) for n in staged]

    def wrapped(*refs):
        given, rest, near, sems = list(refs[: len(shapes)]), refs[len(shapes) : own], refs[own:-1], refs[-1]
        for i, n in enumerate(staged):
            given[n] = Staged(given[n], near[i], sems.at[i], n >= len(args))
        kernel(*given, *rest)

    return pl.pallas_call(
        wrapped,
        out_shape=outs,
        in_specs=specs[: len(args)],
        out_specs=specs[len(args) :],
        scratch_shapes=list(scratch) + extra + [pltpu.SemaphoreType.DMA((len(staged),))],
        compiler_params=pltpu.CompilerParams(
            vmem_limit_bytes=VMEM_LIMIT, has_side_effects=True, collective_id=collective_id
        ),
        name=name,
    )(*args)


def final_kernel(n, *refs):
    src, small, dst = refs[:n], refs[n], refs[n + 1 : 2 * n + 1]
    router, mix, vec, ln1, ln2 = refs[2 * n + 1 : 2 * n + 6]
    near, sems = refs[2 * n + 6 : 3 * n + 6], refs[-1]
    loads = [pltpu.make_async_copy(a, b, sems.at[0, i]) for i, (a, b) in enumerate(zip(src, near))]
    copies = [pltpu.make_async_copy(a, b, sems.at[1, i]) for i, (a, b) in enumerate(zip(near, dst))]
    for c in loads:
        c.start()
    rows = small.shape[0]
    t = jnp.transpose(jnp.concatenate([small[...], jnp.zeros((128 - rows, 128), F32)], axis=0))[:, 0:rows]
    router[...] = t[0:8]
    mix[...] = t[8:12]
    vec[...] = t[12:14]
    ln1[...] = t[14:15]
    ln2[...] = t[15:16]
    for a, b in zip(loads, copies):
        a.wait()
        b.start()
    for c in copies:
        c.wait()


def final(big, small):
    rows = small.shape[0]
    far, near = pl.BlockSpec(memory_space=pl.ANY), pl.BlockSpec(memory_space=pltpu.VMEM)
    return pl.pallas_call(
        functools.partial(final_kernel, len(big)),
        out_shape=[jax.ShapeDtypeStruct(a.shape, a.dtype) for a in big]
        + [shape(n, rows, dtype=F32) for n in (8, 4, 2, 1, 1)],
        in_specs=[far] * len(big) + [near],
        out_specs=[far] * len(big) + [near] * 5,
        scratch_shapes=[pltpu.VMEM(a.shape, a.dtype) for a in big] + [pltpu.SemaphoreType.DMA((2, len(big)))],
        compiler_params=pltpu.CompilerParams(vmem_limit_bytes=VMEM_LIMIT),
        name="results",
    )(*big, small)


def body(
    tokens, segments, routes, prev_logits, ln1_gain, w_qkv, w_attn, ln2_gain, w_router, const_mix, const_vec,
    expert_in, expert_out, cotangent,
):
    length, width = tokens.shape
    heads = width // HEAD_DIM
    experts = lax.axis_size("expert") * expert_in.shape[0]
    hidden = expert_out.shape[1]
    capacity = length // 2
    slots = experts * capacity
    n_dp = lax.axis_size("dp")
    V = pltpu.VMEM
    DMA = pltpu.SemaphoreType.DMA
    cos, sin = (jnp.asarray(t) for t in rotary_tables(length))
    rT, pT = routes.T, prev_logits.T
    wrT, cmT, cvT = w_router.T, const_mix.T, const_vec.T
    ln1, ln2 = ln1_gain, ln2_gain
    peers = experts - 1

    q, k, v, pw, att, n1, res, target, send, g_rows, high, low = call(
        fwd_kernel,
        [
            shape(length, width), shape(length, width), shape(length, width), shape(heads, length, length),
            shape(length, width), shape(length, width), shape(length, width, dtype=F32),
            shape(length, 128, dtype=F32), shape(experts, capacity, width), shape(experts, capacity, width),
            shape(length, width), shape(length, width),
        ],
        [
            V((length, length), F32), V((3, length, 128), F32), V((128, length), F32), V((slots, length), BF16), V((experts, capacity, width), BF16),
            DMA((peers,)), DMA((peers,)), V((heads, length, length), BF16), V((experts, capacity, width), BF16),
            DMA((width // 128, 2)), DMA((experts + 1,)),
        ],
        (tokens, segments, rT, ln1, w_qkv, w_attn, ln2, cotangent, cos, sin),
        "attention", 0, (13, 18, 19), (0, 4, 5, 7, 8, 9, 10, 11, 12, 14, 15, 16, 20, 21),
    )

    tiles, slabs = 4, 3
    ft = hidden // tiles
    within = n_dp == 8 and experts == 4
    stages = ((("dp", 1), ("dp", 2), ("dp", 4)), (("dp", 2), ("dp", 1), ("dp", 4))) if within else ()
    order = (("expert", 1), ("expert", 2), ("dp", 1), ("dp", 2), ("dp", 4))
    slab_in, slab_out = (2 * tiles, width, ft), (slabs, hidden, width // slabs)

    def part_of(s, n):
        return (s[0], s[1] // n, s[2])

    late = (tiles, width // 2, ft)
    early = (tiles, width // 4, ft)
    f_rows, d_back, g_out, dot_back, meta, *g_in = call(
        functools.partial(expert_kernel, stages),
        [
            shape(experts, capacity, width), shape(experts, capacity, width), shape(*slab_out),
            shape(experts, 8, capacity, dtype=F32), shape(length, 128, dtype=F32),
        ]
        + ([shape(*late), shape(*early)] if within else [shape(*slab_in)]),
        [
            V((experts, capacity, width), BF16), V((slots, width), BF16), V((tiles, slots, ft), BF16),
            V((tiles, slots, 2 * ft), BF16), V((slots, width), F32), V((slots, width), F32),
            V((experts, capacity, width), BF16),
        ]
        + ([V(slab_in, BF16), V(late, BF16), V(early, BF16)] + [DMA((2 * tiles,))] * 2 + [DMA((tiles,))] * 3 if within else [])
        + [DMA((peers,))] * 4
        + [DMA((2,))]
        + [V((experts, 8, capacity), F32)] * 3
        + [V((128, width), F32), V((3, length, 128), F32)]
        + [DMA((peers,))] * 4,
        (send, g_rows, expert_in, expert_out, high, low, target, rT, pT, wrT, cmT),
        "experts", 1, (0, 12) + ((17,) if within else ()), (1, 2, 3, 4, 5, 11, 13, 16),
    )

    args = (
        tokens, cotangent, res, meta, dot_back, rT, f_rows, d_back, q, k, v, pw, att, n1, ln1, w_qkv, w_attn, ln2, wrT, cmT, cvT,
        cos, sin,
    )
    n_all = n_dp * experts
    rows = width // n_all if within else width
    outs = [
        shape(length, width), shape(length, width), shape(rows, 3 * width, dtype=F32), shape(rows, width, dtype=F32),
        shape(rows, 128, dtype=F32),
    ]
    scratch = [
        V((128, width), F32), V((2, length, 128), F32), V((length, width), F32), V((length, width), F32),
        V((2, length, 128), F32), V((length, 256), BF16), V((length, width), BF16), V((length, width), F32),
        V((length, width), BF16), V((length, 3 * width), BF16), V((length, width), BF16),
        V((2, length, 128), F32), V((16, width), F32), V((experts, capacity, width), BF16), DMA((peers,)), DMA((peers,)),
        V((heads, length, length), BF16), DMA((3,)),
    ]
    if within:
        args += (g_in[1], g_in[0], g_out)
        outs += [
            shape(rows, 128, dtype=F32),
            shape(width // n_dp, 2 * hidden, dtype=F32), shape(hidden // n_dp, width, dtype=F32)]
        scratch += [
            V(early, BF16), V(part_of(slab_in, 8), BF16), V(part_of(slab_out, 2), BF16),
            V(part_of(slab_out, 4), BF16), V(part_of(slab_out, 8), BF16), DMA((2, 2 * tiles)), DMA((2, 2 * tiles)),
            DMA((3, slabs)), DMA((3, slabs)),
        ]
        for cols in (width, width, width, 512, 256, 256):
            scratch += [V((2 * width >> s, cols // 2), BF16) for s in range(6)] + [DMA((5,)), DMA((5,))]
    plan = (stages, order) if within else ()
    n = len(args)
    staged = (0, 1, 2, 7, 8, 9, 10, 12, 13, 15, 16, 21, 22) + tuple(range(23, n)) + (n, n + 1)
    staged += (n + 6, n + 7) if within else ()
    done = call(functools.partial(bwd_kernel, plan), outs, scratch, args, "backward", 2, (6, 11), staged)
    out, igrad, d_qkv, d_attn, small = done[:5]
    if within:
        out, igrad, d_qkv, d_attn, g_in, g_out, router, mix, vec, ln_one, ln_two = final(
            (out, igrad, d_qkv, d_attn, done[6], done[7]), small
        )
        return (
            out, igrad, ln_one.reshape(rows), d_qkv, d_attn, ln_two.reshape(rows), router.T, mix.T, vec.T,
            g_in[None], g_out[None],
        )
    (g_in,) = g_in
    g_in = jnp.moveaxis(g_in.reshape(tiles, 2, width, ft), 2, 0).transpose(0, 2, 1, 3).reshape(width, 2 * hidden)
    g_out = jnp.moveaxis(g_out, 0, 1).reshape(hidden, width)
    g_in = lax.psum_scatter(g_in, "dp", scatter_dimension=0, tiled=True).astype(F32)
    g_out = lax.psum_scatter(g_out, "dp", scatter_dimension=0, tiled=True).astype(F32)
    d_qkv, d_attn, small = (
        lax.psum_scatter(d, ("dp", "expert"), scatter_dimension=0, tiled=True) for d in (d_qkv, d_attn, small)
    )
    return (
        out, igrad, small[:, 14], d_qkv, d_attn, small[:, 15], small[:, 0:8], small[:, 8:12], small[:, 12:14],
        g_in[None], g_out[None],
    )


def solution(mesh):
    rows = P(("dp", "expert"), None)
    return jax.shard_map(
        body,
        mesh=mesh,
        in_specs=(
            rows, rows, rows, rows, P(), P(), P(), P(), P(), P(), P(),
            P("expert", None, None), P("expert", None, None), rows,
        ),
        out_specs=(
            rows, rows, P(("dp", "expert")), rows, rows, P(("dp", "expert")), rows, rows, rows,
            P("expert", "dp", None), P("expert", "dp", None),
        ),
        check_vma=False,
    )
```
